32 devices in a mesh: ens: 2 (over x), tile: 16 (over z, y, core).
Axes of the slice: x: 2, y: 2, z: 4, core: 2. Of those that a mesh axis runs over, the one named last changes fastest.
Arguments:
- observations: float32 [1024, 64], P(('ens', 'tile')), parts along dimension 0, may hold values from -24 to 24
- jacobian: float32 [256, 64, 256], P('tile'), may hold values from -0.375 to 0.375
- block_row: int32 [256], P('tile'), may hold values from 0 to 31
- block_col: int32 [256], P('tile'), may hold values from 0 to 127, as said below
- block_count: int32 [16], P('tile'), may hold values from 1 to 16, as said below
- block_band: int32 [512], P('tile'), may hold values from 0 to 127
- carry_decay: float32 [128], replicated, may hold values from 0.3 to 0.99
- sparsity_weight: float32 [1024], replicated, may hold values from 0.1 to 2
Outputs:
- coefficients: float32 [128, 8, 1024], P(('ens', 'tile')), parts along dimension 0
- misfit: float32 [1024, 64], P(('ens', 'tile')), parts along dimension 0
The draws below stay inside these ranges and needn't reach their ends.
There are 2 independent parts, one for each index of `ens`. The reference program is written for one: setup_inputs(seed, part) draws one part's arguments, and reference() takes and returns one part's arrays. A program takes and returns all parts, laid end to end along the dimension named above; an argument that names none is the same for every part. Nothing has to cross between parts.
Inputs may be any that keep to these rules, and one draw needn't show every extreme that they name: block_count[d] slots, 0 to block_count[d] - 1, of index d hold blocks; the other slots hold no blocks; some index uses all 16 slots. `block_col`: owner of a strip j is j // 8; among the 16 slots of one index d at most 2 name strips of one owner, and in every index some owner is named by exactly 2 slots.
All inputs are finite; a program needn't handle non-finite values.
Results may differ from the reference program's by a relative error of at most 0.0003.
Values sent between devices are 32-bit elements; how exact they have to be, the bound alone decides.
No kernel may reach another device: no remote copies, remote signals or barrier semaphores. Data moves between devices by JAX's collectives and lax.ppermute only.
A program may use at most 128 MiB of HBM per device.

```python
import math
import jax
import jax.numpy as jnp
from jax import lax

WIN = 8
NLAT = 64
SEC_STRIPS = 2
STRIP = 256
SOUNDS = 64
K_DEV = 16
SB_DEV = 32
NBANDS = 128
ITERS = 3
NLON = 1024
NBLOCKS = 256
SOUND_B = 512
CAP = 2
N_TILE = 16


def draw_block_count(key, part):
    base = jax.random.randint(key, (N_TILE,), max(1, K_DEV // 8), K_DEV // 2 + 1)
    chosen = jax.random.randint(jax.random.fold_in(key, 7), (), 0, N_TILE)
    return jnp.where(jnp.arange(N_TILE) == chosen, K_DEV, base).astype(jnp.int32)


def draw_block_col(key, part):
    span = NLAT // N_TILE * SEC_STRIPS
    slots = N_TILE * CAP

    def one_pair(pair_key):
        owners = jnp.arange(slots, dtype=jnp.int32) // CAP
        chosen = jax.random.randint(jax.random.fold_in(pair_key, 1), (), 0, N_TILE)
        order_score = jax.random.permutation(jax.random.fold_in(pair_key, 2), slots).astype(jnp.int32)
        score = jnp.where(owners == chosen, -1 - jnp.arange(slots, dtype=jnp.int32), order_score)
        picked = owners[jnp.argsort(score)[:K_DEV]]
        offset = jax.random.randint(jax.random.fold_in(pair_key, 3), (K_DEV,), 0, span)
        return picked * span + offset
    pair_keys = jax.random.split(jax.random.fold_in(key, 11), N_TILE)
    return jax.vmap(one_pair)(pair_keys).reshape(-1).astype(jnp.int32)


def plant(drawn, own_key, low, high):
    shape = drawn.shape
    index_at = [jax.random.randint(jax.random.fold_in(own_key, axis), (), 0, shape[axis]) for axis in range(len(shape))]
    drawn = drawn.at[tuple(index_at)].set(low)
    longest = shape.index(max(shape))
    index_at[longest] = (index_at[longest] + 1) % shape[longest]
    return drawn.at[tuple(index_at)].set(high)


def steps_of(stream_key, dims, shards, least, top_value):
    gain = 1.0
    for dim, blocks in shards:
        heights = jax.random.uniform(jax.random.fold_in(jax.random.fold_in(stream_key, 6), dim), (blocks,), jnp.float32, least / len(shards), top_value / len(shards))
        gain = gain * jnp.repeat(jnp.exp(heights), dims[dim] // blocks).reshape((-1,) + (1,) * (len(dims) - 1 - dim))
    return gain


def centred(key, shape, width, bound, shards=(), held_as=jnp.bfloat16):
    level = steps_of(key, shape, shards, -0.22, 0.18) if shards else 1.0
    values = jax.random.normal(key, shape, jnp.float32) * width * level
    return jnp.minimum(jnp.maximum(values, -bound), bound).astype(held_as)


def setup_inputs(seed: int = 0, part: int = 0) -> dict:
    arg_keys = jax.random.split(jax.random.key(seed), 9)
    own_keys = jax.random.split(jax.random.fold_in(arg_keys[8], part), 9)
    observations = centred(own_keys[0], (SOUND_B, SOUNDS), 4.0, 24.0, ((0, 16),), jnp.float32)
    jacobian = centred(arg_keys[1], (NBLOCKS, SOUNDS, STRIP), STRIP ** -0.5, 0.375, ((0, 16),), jnp.float32)
    block_row = plant(jax.random.randint(arg_keys[2], (NBLOCKS,), 0, SB_DEV), jax.random.fold_in(arg_keys[2], 1), 0, SB_DEV - 1).astype(jnp.int32)
    block_col = draw_block_col(jax.random.fold_in(arg_keys[8], 71), part)
    block_count = draw_block_count(jax.random.fold_in(arg_keys[8], 71), part)
    block_band = plant(jax.random.randint(arg_keys[5], (SOUND_B,), 0, NBANDS), jax.random.fold_in(arg_keys[5], 1), 0, NBANDS - 1).astype(jnp.int32)
    carry_decay = jnp.clip(jax.random.uniform(arg_keys[6], (NBANDS,), jnp.float32, 0.3, 0.99), 0.3, 0.99)
    sparsity_weight = jnp.clip(jnp.exp(jax.random.uniform(arg_keys[7], (NLON,), jnp.float32, math.log(0.1), math.log(2.0))), 0.1, 2.0)
    return {"observations": observations, "jacobian": jacobian, "block_row": block_row, "block_col": block_col, "block_count": block_count, "block_band": block_band, "carry_decay": carry_decay, "sparsity_weight": sparsity_weight}


root_half = math.sqrt(0.5)
step_size = 0.2
highest = lax.Precision.HIGHEST

def haar_forward(values):
    details = []
    approx = values
    while approx.shape[-1] % 2 == 0 and approx.shape[-1] > 1:
        paired = approx.reshape(approx.shape[:-1] + (approx.shape[-1] // 2, 2))
        even_part = paired[..., 0]
        odd_part = paired[..., 1]
        details.insert(0, (even_part - odd_part) * root_half)
        approx = (even_part + odd_part) * root_half
    return jnp.concatenate([approx] + details, axis=-1)

def haar_inverse(coeffs):
    length = coeffs.shape[-1]
    widths = []
    while length % 2 == 0 and length > 1:
        length = length // 2
        widths.append(length)
    approx = coeffs[..., :length]
    offset = length
    for detail_len in reversed(widths):
        detail = coeffs[..., offset:offset + detail_len]
        offset = offset + detail_len
        even_part = (approx + detail) * root_half
        odd_part = (approx - detail) * root_half
        approx = jnp.stack([even_part, odd_part], axis=-1).reshape(approx.shape[:-1] + (2 * detail_len,))
    return approx

def momentum_weights(total_steps):
    weights = []
    current = 1.0
    for iteration in range(total_steps):
        following = (1.0 + math.sqrt(1.0 + 4.0 * current * current)) / 2.0
        weights.append((current - 1.0) / following)
        current = following
    return weights

def shrink(values, limit):
    return jnp.sign(values) * jnp.maximum(jnp.abs(values) - limit, 0.0)

def reference(observations, jacobian, block_row, block_col, block_count, block_band, carry_decay, sparsity_weight):
    sectors = N_TILE // WIN
    sector_width = SEC_STRIPS * STRIP
    strips_dev = NLAT * SEC_STRIPS
    obs_rows = observations.reshape(N_TILE, SB_DEV, SOUNDS)
    blocks = jacobian.reshape(N_TILE, K_DEV, SOUNDS, STRIP)
    cols = block_col.reshape(N_TILE, K_DEV).astype(jnp.int32)
    row_hot = jax.nn.one_hot(block_row.reshape(N_TILE, K_DEV), SB_DEV, dtype=jnp.float32)
    col_hot = jax.nn.one_hot(cols, strips_dev, dtype=jnp.float32)
    band_hot = jax.nn.one_hot(block_band.reshape(N_TILE, SB_DEV), NBANDS, dtype=jnp.float32)
    valid = (jnp.arange(K_DEV, dtype=jnp.int32)[None, :] < block_count[:, None]).astype(jnp.float32)
    coeffs = jnp.zeros((NLAT, WIN, sectors * sector_width), jnp.float32)
    point = coeffs
    misfit = jnp.zeros((N_TILE, SB_DEV, SOUNDS), jnp.float32)
    for beta in momentum_weights(ITERS):
        flux = haar_inverse(point)
        fields = flux.reshape(NLAT, N_TILE, sector_width).transpose(1, 0, 2).reshape(N_TILE, strips_dev, STRIP)
        strips = jnp.take_along_axis(fields, cols[:, :, None], axis=1)
        direct_blocks = jnp.einsum('dkis,dks->dki', blocks, strips, precision=highest) * valid[:, :, None]
        direct = jnp.einsum('dkb,dki->dbi', row_hot, direct_blocks, precision=highest)
        partial_value = jnp.einsum('dbg,db->dg', band_hot, lax.optimization_barrier(jnp.sum(direct, axis=2)), precision=highest) / SOUNDS
        window_total = lax.optimization_barrier(jnp.sum(partial_value.reshape(WIN, sectors, NBANDS), axis=1))
        running = window_total[0]
        carried_list = [running]
        for window in range(1, WIN):
            running = running * carry_decay + window_total[window]
            carried_list.append(running)
        carried = jnp.repeat(jnp.stack(carried_list, axis=0), sectors, axis=0)
        predicted = direct + jnp.einsum('dbg,dg->db', band_hot, carried, precision=highest)[:, :, None]
        misfit = predicted - obs_rows
        back_total = jnp.einsum('dbg,db->dg', band_hot, lax.optimization_barrier(jnp.sum(misfit, axis=2)), precision=highest)
        window_back = lax.optimization_barrier(jnp.sum(back_total.reshape(WIN, sectors, NBANDS), axis=1))
        running = window_back[WIN - 1]
        returned_list = [running]
        for window in range(WIN - 2, -1, -1):
            running = running * carry_decay + window_back[window]
            returned_list.insert(0, running)
        returned = jnp.repeat(jnp.stack(returned_list, axis=0), sectors, axis=0)
        adjoint = misfit + jnp.einsum('dbg,dg->db', band_hot, returned, precision=highest)[:, :, None] / SOUNDS
        picked = jnp.einsum('dkb,dbi->dki', row_hot, adjoint, precision=highest)
        grad_blocks = jnp.einsum('dkis,dki->dks', blocks, picked, precision=highest) * valid[:, :, None]
        grad_fields = jnp.einsum('dkp,dks->dps', col_hot, grad_blocks, precision=highest)
        grad_flux = grad_fields.reshape(N_TILE, NLAT, sector_width).transpose(1, 0, 2).reshape(NLAT, WIN, sectors * sector_width)
        gradient = haar_forward(grad_flux)
        updated = shrink(point - step_size * gradient, step_size * sparsity_weight)
        point = updated + beta * (updated - coeffs)
        coeffs = updated
    return (coeffs, misfit.reshape(N_TILE * SB_DEV, SOUNDS))
```

```python
import functools
import math

import jax
import jax.numpy as jnp
from jax import lax
from jax.experimental import pallas as pl
from jax.experimental.pallas import tpu as pltpu
from jax.sharding import PartitionSpec as P

WIN = 8
NLAT = 64
SEC_STRIPS = 2
STRIP = 256
SOUNDS = 64
SB_DEV = 32
NBANDS = 128
ITERS = 3
SLOTS = 16
LANES = 128
ROWS = 8
STEP = 0.2

F32 = jnp.float32
BF16 = jnp.bfloat16
HIGHEST = lax.Precision.HIGHEST

LINE, SPOT, BAND, TOTAL, APPROX, ROW, COL, VALID, FIRST, RANK = range(10)


def momentum_weights(total_steps):
    weights = []
    current = 1.0
    for _ in range(total_steps):
        following = (1.0 + math.sqrt(1.0 + 4.0 * current * current)) / 2.0
        weights.append((current - 1.0) / following)
        current = following
    return weights


def iota(shape, axis):
    return lax.broadcasted_iota(jnp.int32, shape, axis)


def shrink(values, limit):
    return values - jnp.minimum(jnp.maximum(values, -limit), limit)


def to_col(row):
    n = row.shape[1]
    eye = iota((n, n), 0) == iota((n, n), 1)
    return jnp.sum(jnp.where(eye, row, 0.0), axis=1, keepdims=True)


def to_row(col):
    n = col.shape[0]
    eye = iota((n, n), 0) == iota((n, n), 1)
    return jnp.sum(jnp.where(eye, col, 0.0), axis=0, keepdims=True)


def exact_dot(left, right):
    return jnp.dot(left, right, precision=HIGHEST, preferred_element_type=F32)


def dot(left, right):
    return jnp.dot(left, right, preferred_element_type=F32)


def dot_nt(left, right):
    return lax.dot_general(left, right, (((1,), (1,)), ((), ())), preferred_element_type=F32)


def split(values):
    high = values.astype(BF16)
    return high, (values - high.astype(F32)).astype(BF16)


def haar_signs():
    cell = iota((STRIP, STRIP), 0)
    coef = iota((STRIP, STRIP), 1)
    out = jnp.where(coef == 0, 1.0, 0.0)
    m = 1
    while m < STRIP:
        span = STRIP // m
        level = (coef >= m) & (coef < 2 * m)
        within = cell - (coef - m) * span
        sign = jnp.where(within < span // 2, 1.0, -1.0)
        out = jnp.where(level & (within >= 0) & (within < span), sign, out)
        m *= 2
    return out.astype(BF16)


def haar_scales():
    coef = iota((1, STRIP), 1)
    out = jnp.full((1, STRIP), math.sqrt(1.0 / STRIP), F32)
    m = 1
    while m < STRIP:
        out = jnp.where((coef >= m) & (coef < 2 * m), math.sqrt(m / STRIP), out)
        m *= 2
    return out


def top_entry(spot, index, strips):
    if index == 0:
        return jnp.full(spot.shape, math.sqrt(1.0 / strips), F32)
    m = 1 << (index.bit_length() - 1)
    span = strips // m
    start = float((index - m) * span)
    half = start + span / 2
    end = start + span
    scale = math.sqrt(m / strips)
    positive = (spot >= start) & (spot < half)
    negative = (spot >= half) & (spot < end)
    return jnp.where(positive, scale, jnp.where(negative, -scale, 0.0))


def weekly(rows, sectors):
    return [sum(rows[w * sectors + 1 : (w + 1) * sectors], rows[w * sectors]) for w in range(WIN)]


def scan_back(totals, decay):
    running = totals[WIN - 1]
    out = [running]
    for w in range(WIN - 2, -1, -1):
        running = running * decay + totals[w]
        out.insert(0, running)
    return out


def scan_ahead(totals, decay):
    running = totals[0]
    out = [running]
    for w in range(1, WIN):
        running = running * decay + totals[w]
        out.append(running)
    return out


def pick(rows, index):
    out = rows[0]
    for w in range(1, len(rows)):
        out = jnp.where(index == w, rows[w], out)
    return out


def background(first, partial_rows, decay, sectors):
    counts = weekly([first[t, 0:1, :] for t in range(WIN * sectors)], sectors)
    sums = weekly([first[t, 1:2, :] for t in range(WIN * sectors)], sectors)
    partials = weekly(partial_rows, sectors)
    carried = scan_ahead(partials, decay)
    back = [
        SOUNDS * partials[w] + (SOUNDS * counts[w]) * carried[w] - sums[w] for w in range(WIN)
    ]
    returned = scan_back(back, decay)
    return [carried[w] + returned[w] / SOUNDS for w in range(WIN)], carried


def one_hot_bands(band_col):
    return jnp.where(band_col == iota((band_col.shape[0], NBANDS), 1).astype(F32), 1.0, 0.0)


def own_block_mask(rows):
    return iota((rows, SLOTS * SOUNDS), 0) == iota((rows, SLOTS * SOUNDS), 1) // SOUNDS


def back_project(chosen, high_ref, low_ref):
    wide = jnp.concatenate([chosen] * (SLOTS * SOUNDS // LANES), axis=1)
    spread = jnp.where(own_block_mask(SLOTS), wide, 0.0)
    high, low = split(spread)
    both = dot(jnp.concatenate([high, low], axis=0), high_ref[...])
    return both[:SLOTS] + both[SLOTS:] + dot(high, low_ref[...])


def forward(point, high_ref, low_ref):
    high, low = split(point)
    both = dot_nt(jnp.concatenate([high, low], axis=0), high_ref[...])
    full = both[:SLOTS] + both[SLOTS:] + dot_nt(high, low_ref[...])
    return jnp.sum(jnp.where(own_block_mask(SLOTS), full, 0.0), axis=0, keepdims=True)


def fold(weights, values):
    product = weights * values
    total = product[:, :LANES]
    for start in range(LANES, SLOTS * SOUNDS, LANES):
        total = total + product[:, start : start + LANES]
    return total + pltpu.roll(total, SOUNDS, 1)


def start_kernel(band_ref, obs_ref, out_ref):
    band = to_col(band_ref[...].astype(F32))
    hot = one_hot_bands(band)
    sums = jnp.sum(obs_ref[...], axis=1, keepdims=True)
    counted = jnp.sum(hot, axis=0, keepdims=True)
    summed = jnp.sum(hot * sums, axis=0, keepdims=True)
    for t in range(out_ref.shape[0]):
        out_ref[t, 0:1, :] = counted
        out_ref[t, 1:2, :] = summed


def prepare_kernel(
    strips,
    owners,
    jac_ref,
    obs_ref,
    row_ref,
    col_ref,
    count_ref,
    band_ref,
    weight_ref,
    high_ref,
    low_ref,
    column_ref,
    obs_grad_ref,
    obs_slot_ref,
    row_match_ref,
    info_ref,
    limit_ref,
    send_ref,
    strip_match_ref,
):
    sectors = strips // SEC_STRIPS
    strips_owner = NLAT * SEC_STRIPS // owners
    sector = lax.rem(lax.axis_index("tile"), sectors).astype(F32)
    signs = haar_signs()
    scales = haar_scales()
    chunk = STRIP
    for start in range(0, SLOTS * SOUNDS, chunk):
        high, low = split(jac_ref[start : start + chunk, :])
        changed = (dot(high, signs) + dot(low, signs)) * scales
        high, low = split(changed)
        high_ref[start : start + chunk, :] = high
        low_ref[start : start + chunk, :] = low
        per = chunk // SOUNDS
        column_ref[start // SOUNDS : start // SOUNDS + per, :] = jnp.sum(
            changed.reshape(per, SOUNDS, STRIP), axis=1
        )

    row_of = to_col(row_ref[...].astype(F32))
    col_row = col_ref[...].astype(F32)
    col_of = to_col(col_row)
    valid_row = jnp.where(iota((1, SLOTS), 1) < count_ref[...], 1.0, 0.0)
    valid = to_col(valid_row)
    line = jnp.floor(col_of / SEC_STRIPS)
    spot = sector * SEC_STRIPS + (col_of - line * SEC_STRIPS)
    row_hot = jnp.where(row_of == iota((SLOTS, SB_DEV), 1).astype(F32), 1.0, 0.0)
    band_row = band_ref[...].astype(F32)
    band = jnp.sum(row_hot * band_row, axis=1, keepdims=True)
    band = jnp.where(valid > 0.0, band, -1.0)
    observed = obs_ref[...]
    obs_slot = exact_dot(row_hot, jnp.concatenate([observed, observed], axis=1))
    obs_slot_ref[...] = obs_slot
    obs_grad = back_project(obs_slot, high_ref, low_ref)
    obs_grad_ref[...] = obs_grad
    column = column_ref[...]

    lane = iota((SLOTS, SLOTS * SOUNDS), 1) // SOUNDS
    slot = iota((SLOTS, SLOTS * SOUNDS), 0)
    row_lane = jnp.sum(jnp.where(lane == slot, row_of, 0.0), axis=0, keepdims=True)
    row_lane = jnp.where(
        jnp.sum(jnp.where(lane == slot, valid, 0.0), axis=0, keepdims=True) > 0.0, row_lane, -1.0
    )
    row_match_ref[...] = jnp.where(row_of == row_lane, 1.0, 0.0)

    same = jnp.where(col_of == col_row, 1.0, 0.0)
    before = jnp.where(iota((SLOTS, SLOTS), 1) < iota((SLOTS, SLOTS), 0), 1.0, 0.0)
    strip_match_ref[...] = same * valid_row
    first = jnp.where(jnp.sum(same * before, axis=1, keepdims=True) > 0.0, 0.0, 1.0)
    owner = jnp.floor(col_of / strips_owner)
    owner_row = jnp.floor(col_row / strips_owner)
    rank = jnp.sum(jnp.where(owner == owner_row, before, 0.0), axis=1, keepdims=True)

    at = iota((SLOTS, LANES), 1)
    info = jnp.zeros((SLOTS, LANES), F32)
    for place, values in (
        (LINE, line),
        (SPOT, spot),
        (BAND, band),
        (TOTAL, column[:, 0:1] * valid),
        (APPROX, -obs_grad[:, 0:1] * valid),
        (ROW, row_of),
        (COL, col_of),
        (VALID, valid),
        (FIRST, first),
        (RANK, rank),
    ):
        info = jnp.where(at == place, values, info)
    info_ref[...] = info

    local = iota((1, LANES), 1)
    limits_low = jnp.zeros((SLOTS, LANES), F32)
    limits_high = jnp.zeros((SLOTS, LANES), F32)
    for j in range(strips):
        low_row = jnp.zeros((1, LANES), F32)
        m = 1
        while m < LANES:
            start = strips * m + j * m
            block = weight_ref[0:1, start // LANES * LANES : start // LANES * LANES + LANES]
            shift = (m - start % LANES) % LANES
            moved = pltpu.roll(jnp.broadcast_to(block, (ROWS, LANES)), shift, 1)[0:1] if shift else block
            low_row = jnp.where((local >= m) & (local < 2 * m), moved, low_row)
            m *= 2
        high_row = weight_ref[0:1, (strips + j) * LANES : (strips + j + 1) * LANES]
        limits_low = jnp.where(spot == float(j), low_row, limits_low)
        limits_high = jnp.where(spot == float(j), high_row, limits_high)
    limit_ref[:, :LANES] = STEP * limits_low
    limit_ref[:, LANES:] = STEP * limits_high

    shape = (owners * ROWS, 4 * SLOTS)
    target = (iota(shape, 0) // ROWS).astype(F32)
    kind = iota(shape, 0) % ROWS
    group = iota(shape, 1) // SLOTS
    slim = iota((SLOTS, 4 * SLOTS), 1) % SLOTS == iota((SLOTS, 4 * SLOTS), 0)
    owner_wide = jnp.sum(jnp.where(slim, owner, 0.0), axis=0, keepdims=True)
    rank_wide = jnp.sum(jnp.where(slim, rank, 0.0), axis=0, keepdims=True)
    kind_f = kind.astype(F32)
    mine = owner_wide == target
    hit = (group == 0) & (kind_f == 2.0 * rank_wide)
    hit = hit | ((group == 1) & (kind_f == 2.0 * rank_wide + 1.0))
    hit = hit | ((group == 2) & (kind == 5))
    hit = (hit & mine) | ((iota(shape, 1) == 3 * SLOTS) & (kind == 4))
    send_ref[...] = jnp.where(hit, 1.0, 0.0)


def fill_message(out_ref, send, strips_part, meta, partial):
    bottom = jnp.where(iota((SLOTS, LANES), 0) == 0, partial, 0.0)
    stacked = jnp.concatenate([strips_part[:, :LANES], strips_part[:, LANES:], meta, bottom], axis=0)
    rows = exact_dot(send, stacked)
    out_ref[...] = rows.reshape(out_ref.shape)


def advance(strips, scalar, local_grad, column, info, info_all, approx_all, strip_match, limit, top_limit, point, top):
    c_all = jnp.sum(one_hot_bands(info_all[:, BAND : BAND + 1]) * scalar, axis=1, keepdims=True)
    grads = exact_dot(strip_match, local_grad + c_all[:SLOTS] * column)
    approx_row = to_row(approx_all + c_all * info_all[:, TOTAL : TOTAL + 1])
    line_row = to_row(info_all[:, LINE : LINE + 1])
    spot_row = to_row(info_all[:, SPOT : SPOT + 1])
    on_line = jnp.where(info[:, LINE : LINE + 1] == line_row, approx_row, 0.0)
    at = iota((SLOTS, LANES), 1)
    top_grad = jnp.zeros((SLOTS, LANES), F32)
    for t in range(strips):
        value = jnp.sum(on_line * top_entry(spot_row, t, strips), axis=1, keepdims=True)
        top_grad = jnp.where(at == t, value, top_grad)
    if point is None:
        return shrink(-STEP * grads, limit), shrink(-STEP * top_grad, top_limit)
    return shrink(point - STEP * grads, limit), shrink(top - STEP * top_grad, top_limit)


def with_approx(point, top, info, strips):
    at = iota((SLOTS, LANES), 1)
    matrix = jnp.zeros((SLOTS, LANES), F32)
    for t in range(strips):
        matrix = jnp.where(at == t, top_entry(info[:, SPOT : SPOT + 1], t, strips), matrix)
    approx = jnp.sum(matrix * top, axis=1, keepdims=True)
    return jnp.where(iota((SLOTS, STRIP), 1) == 0, approx, point)


def band_partial(point, column, info):
    dots = jnp.sum(point * column, axis=1, keepdims=True)
    hot = one_hot_bands(info[:, BAND : BAND + 1])
    return jnp.sum(hot * dots, axis=0, keepdims=True) / SOUNDS


def gather_info(info_ref, others_refs):
    return jnp.concatenate([info_ref[...]] + [r[...] for r in others_refs], axis=0)


def first_step_kernel(
    strips,
    owners,
    first_ref,
    info_ref,
    column_ref,
    obs_grad_ref,
    limit_ref,
    strip_match_ref,
    send_ref,
    decay_ref,
    weight_ref,
    *rest,
):
    sectors = strips // SEC_STRIPS
    others_refs = rest[: sectors - 1]
    point_ref, top_ref, message_ref = rest[sectors - 1 :]
    window = lax.axis_index("tile") // sectors
    decay = decay_ref[...]
    sums = weekly([first_ref[t, 1:2, :] for t in range(owners)], sectors)
    returned = scan_back([-s for s in sums], decay)
    scalar = pick(returned, window) / SOUNDS
    info = info_ref[...]
    info_all = gather_info(info_ref, others_refs)
    column = column_ref[...]
    top_limit = STEP * weight_ref[0:1, :LANES]
    updated, top = advance(
        strips,
        scalar,
        -obs_grad_ref[...],
        column,
        info,
        info_all,
        info_all[:, APPROX : APPROX + 1],
        strip_match_ref[...],
        limit_ref[...],
        top_limit,
        None,
        None,
    )
    point = with_approx(updated, top, info, strips)
    point_ref[...] = point
    top_ref[...] = top
    partial = band_partial(point, column, info)
    at = iota((SLOTS, LANES), 1).astype(F32)
    strips_owner = NLAT * SEC_STRIPS // owners
    col = info[:, COL : COL + 1]
    local = col - jnp.floor(col / strips_owner) * strips_owner
    base = info[:, RANK : RANK + 1] * (LANES // 2)
    meta = jnp.where(at == base, local + 1.0, 0.0)
    meta = jnp.where(at == base + 1.0, info[:, BAND : BAND + 1] + 1.0, meta)
    fill_message(message_ref, send_ref[...], column * info[:, VALID : VALID + 1], meta, partial)


def local_grad_kernel(point_ref, high_ref, low_ref, row_match_ref, obs_slot_ref, info_ref, grad_ref, approx_ref):
    values = forward(point_ref[...], high_ref, low_ref)
    chosen = fold(row_match_ref[...], values) - obs_slot_ref[...]
    grad = back_project(chosen, high_ref, low_ref)
    grad_ref[...] = grad
    approx_ref[...] = jnp.broadcast_to(
        grad[:, 0:1] * info_ref[:, VALID : VALID + 1], approx_ref.shape
    )


def second_step_kernel(
    strips,
    owners,
    beta,
    first_ref,
    second_ref,
    info_ref,
    column_ref,
    grad_ref,
    limit_ref,
    strip_match_ref,
    send_ref,
    decay_ref,
    weight_ref,
    point_ref,
    top_ref,
    high_ref,
    low_ref,
    row_match_ref,
    obs_slot_ref,
    obs_ref,
    approx_ref,
    *rest,
):
    sectors = strips // SEC_STRIPS
    others_refs = rest[: sectors - 1]
    approx_refs = rest[sectors - 1 : 2 * (sectors - 1)]
    message_ref, differ_ref = rest[2 * (sectors - 1) :]
    my_index = lax.axis_index("tile")
    window = my_index // sectors
    sector = lax.rem(my_index, sectors).astype(F32)
    decay = decay_ref[...]
    combined, _ = background(first_ref, [second_ref[t, 4:5, :] for t in range(owners)], decay, sectors)
    info = info_ref[...]
    info_all = gather_info(info_ref, others_refs)
    approx_all = gather_info(approx_ref, approx_refs)[:, 0:1]
    column = column_ref[...]
    top_limit = STEP * weight_ref[0:1, :LANES]
    old = point_ref[...]
    old_top = top_ref[...]
    updated, top = advance(
        strips,
        pick(combined, window),
        grad_ref[...],
        column,
        info,
        info_all,
        approx_all,
        strip_match_ref[...],
        limit_ref[...],
        top_limit,
        old,
        old_top,
    )
    point = updated + beta * (updated - old)
    top = top + beta * (top - old_top)
    point = with_approx(point, top, info, strips)
    partial = band_partial(point, column, info)
    values = forward(point, high_ref, low_ref)
    chosen = fold(row_match_ref[...], values) - obs_slot_ref[...]
    grad = back_project(chosen, high_ref, low_ref)

    valid = info[:, VALID : VALID + 1]
    lane = iota((SLOTS, SLOTS * SOUNDS), 1) // SOUNDS
    slot = iota((SLOTS, SLOTS * SOUNDS), 0)
    row_lane = jnp.sum(
        jnp.where(lane == slot, (info[:, ROW : ROW + 1] + 1.0) * valid, 0.0), axis=0, keepdims=True
    )
    per_row = jnp.where(
        iota((SB_DEV, SLOTS * SOUNDS), 0).astype(F32) + 1.0 == row_lane, 1.0, 0.0
    )
    differ_ref[...] = fold(per_row, values)[:, :SOUNDS] - obs_ref[...]

    count = info_all.shape[0]
    line_row = to_row(info_all[:, LINE : LINE + 1])
    sector_row = to_row(jnp.floor(info_all[:, SPOT : SPOT + 1] / SEC_STRIPS))
    lane = iota((SLOTS, count), 1)
    earlier = jnp.where(lane < SLOTS, jnp.where(lane < iota((SLOTS, count), 0), 1.0, 0.0), jnp.where(sector_row < sector, 1.0, 0.0))
    taken = jnp.sum(jnp.where(info[:, LINE : LINE + 1] == line_row, earlier, 0.0), axis=1, keepdims=True)
    top = jnp.where(taken > 0.0, 0.0, top)
    rank = info[:, RANK : RANK + 1]
    meta = jnp.where(rank == 0.0, pltpu.roll(top, ROWS, 1), pltpu.roll(top, LANES // 2 + ROWS, 1))
    kept = jnp.where(iota((SLOTS, STRIP), 1) == 0, 0.0, point * info[:, FIRST : FIRST + 1])
    fill_message(message_ref, send_ref[...], kept - STEP * (valid * grad), meta, partial)


def place_kernel(strips, owners, second_ref, place_ref, band_hot_ref):
    sectors = strips // SEC_STRIPS
    lines = NLAT // owners
    count = owners * ROWS
    meta = second_ref[:, 5, :]
    wide = (owners, count)
    pair_of = iota(wide, 1) // ROWS == iota(wide, 0)
    kind = iota((1, count), 1) % ROWS
    tall = (count, owners)
    tall_pair = iota(tall, 0) // ROWS == iota(tall, 1)
    tall_kind = iota((count, 1), 0) % ROWS
    strip_rows = []
    band_col = jnp.zeros((count, 1), F32)
    for q in range(2):
        strip = meta[:, q * (LANES // 2) : q * (LANES // 2) + 1]
        band = meta[:, q * (LANES // 2) + 1 : q * (LANES // 2) + 2]
        strip_rows.append(jnp.sum(jnp.where(pair_of, strip, 0.0), axis=0, keepdims=True) - 1.0)
        band_tall = jnp.sum(jnp.where(tall_pair, to_row(band), 0.0), axis=1, keepdims=True)
        band_col = jnp.where(tall_kind // 2 == q, band_tall, band_col)
    band_hot_ref[...] = one_hot_bands(band_col - 1.0)

    def line_of(strip):
        return jnp.floor(strip / SEC_STRIPS)

    blocks = lines * WIN
    pair = iota((1, count), 1) // ROWS
    window = pair // sectors
    sector = (pair - window * sectors).astype(F32)
    line_col = (iota((blocks, 1), 0) // WIN).astype(F32)
    window_col = iota((blocks, 1), 0) % WIN
    strip_row = jnp.where(kind < 2, strip_rows[0], strip_rows[1])
    slot_line = line_of(strip_row)
    slot_spot = sector * SEC_STRIPS + strip_row - slot_line * SEC_STRIPS
    base = (window == window_col) & (slot_line == line_col) & (strip_row >= 0.0)
    base = jnp.where(base & (kind < 4), 1.0, 0.0)
    for half in range(2):
        part = jnp.where(kind % 2 == half, base, 0.0)
        for j in range(strips):
            start = (half * strips + j) * blocks
            place_ref[start : start + blocks, :] = jnp.where(slot_spot == float(j), part, 0.0)
    for q in range(2):
        start = (2 * strips + q) * blocks
        hit = (window == window_col) & (line_of(strip_rows[q]) == line_col) & (strip_rows[q] >= 0.0) & (kind == 5)
        place_ref[start : start + blocks, :] = jnp.where(hit, 1.0, 0.0)


def finish_kernel(
    strips,
    owners,
    first_ref,
    second_ref,
    third_ref,
    place_ref,
    band_hot_ref,
    decay_ref,
    weight_ref,
    differ_ref,
    band_ref,
    out_ref,
    misfit_ref,
):
    sectors = strips // SEC_STRIPS
    blocks = NLAT // owners * WIN
    count = owners * ROWS
    window = lax.axis_index("tile") // sectors
    combined, carried = background(
        first_ref, [third_ref[t, 4:5, :] for t in range(owners)], decay_ref[...], sectors
    )
    hot = one_hot_bands(to_col(band_ref[...].astype(F32)))
    offset = jnp.sum(hot * pick(carried, window), axis=1, keepdims=True)
    misfit_ref[...] = differ_ref[...] + offset

    spread = jnp.concatenate(
        [jnp.broadcast_to(row, (sectors * ROWS, NBANDS)) for row in combined], axis=0
    )
    scalars = jnp.sum(band_hot_ref[...] * spread, axis=1, keepdims=True)
    third = third_ref[...].reshape(count, LANES)
    second = second_ref[...].reshape(count, LANES)
    kind = iota((count, 1), 0) % ROWS
    rows = third - (STEP * scalars) * jnp.where(kind < 4, second, 0.0)
    placed = exact_dot(place_ref[...], rows)

    lane = iota((1, LANES), 1)
    for j in range(strips):
        start = (strips + j) * LANES
        values = placed[(strips + j) * blocks : (strips + j + 1) * blocks]
        out_ref[:, start : start + LANES] = shrink(values, STEP * weight_ref[0:1, start : start + LANES])

    low = [placed[j * blocks : (j + 1) * blocks] for j in range(strips)]
    tops = [placed[(2 * strips + q) * blocks : (2 * strips + q + 1) * blocks] for q in range(2)]
    top = pltpu.roll(tops[0], LANES - ROWS, 1) + pltpu.roll(tops[1], LANES // 2 - ROWS, 1)
    made = [jnp.zeros((blocks, LANES), F32) for _ in range(strips)]
    for t in range(strips):
        value = jnp.zeros((blocks, 1), F32)
        for j in range(strips):
            entry = top_value(j, t, strips)
            if entry:
                value = value + entry * low[j][:, 0:1]
        made[0] = jnp.where(lane == t, value + top, made[0])
    m = 1
    while m < LANES:
        for j in range(strips):
            start = strips * m + j * m
            block = start // LANES
            shift = (start % LANES - m) % LANES
            moved = pltpu.roll(low[j], shift, 1) if shift else low[j]
            inside = (lane >= start % LANES) & (lane < start % LANES + m)
            made[block] = jnp.where(inside, moved, made[block])
        m *= 2
    for block in range(strips):
        start = block * LANES
        out_ref[:, start : start + LANES] = shrink(made[block], STEP * weight_ref[0:1, start : start + LANES])


def top_value(spot, index, strips):
    if index == 0:
        return math.sqrt(1.0 / strips)
    m = 1 << (index.bit_length() - 1)
    span = strips // m
    within = spot - (index - m) * span
    if within < 0 or within >= span:
        return 0.0
    return math.sqrt(m / strips) * (1.0 if within < span // 2 else -1.0)


def call(kernel, outs, *operands):
    return pl.pallas_call(
        kernel,
        out_shape=[jax.ShapeDtypeStruct(shape, dtype) for shape, dtype in outs],
        compiler_params=pltpu.CompilerParams(vmem_limit_bytes=48 * 1024 * 1024),
    )(*operands)


def body(
    observations,
    jacobian,
    block_row,
    block_col,
    block_count,
    block_band,
    carry_decay,
    sparsity_weight,
):
    owners = lax.axis_size("tile")
    sectors = owners // WIN
    strips = sectors * SEC_STRIPS
    lines = NLAT // owners
    betas = momentum_weights(ITERS)
    rows = block_row.reshape(1, SLOTS)
    cols = block_col.reshape(1, SLOTS)
    count = block_count.reshape(1, 1)
    bands = block_band.reshape(1, SB_DEV)
    decay = carry_decay.reshape(1, NBANDS)
    weight = sparsity_weight.reshape(1, -1)
    flat = jacobian.reshape(SLOTS * SOUNDS, STRIP)
    message = ((owners, ROWS, LANES), F32)
    table = ((SLOTS, LANES), F32)
    strip_rows = ((SLOTS, STRIP), F32)

    def trade(values):
        return lax.all_to_all(values, "tile", 0, 0, tiled=True)

    def from_sectors(values):
        found = []
        for shift in range(1, sectors):
            pairs = [
                (d, d // sectors * sectors + (d + shift) % sectors) for d in range(owners)
            ]
            found.append(lax.ppermute(values, "tile", pairs))
        return found

    (first,) = call(start_kernel, [((owners, 2, LANES), F32)], bands, observations)
    first = trade(first)
    high, low, column, obs_grad, obs_slot, row_match, info, limit, send, strip_match = call(
        functools.partial(prepare_kernel, strips, owners),
        [
            ((SLOTS * SOUNDS, STRIP), BF16),
            ((SLOTS * SOUNDS, STRIP), BF16),
            strip_rows,
            strip_rows,
            table,
            ((SLOTS, SLOTS * SOUNDS), F32),
            table,
            strip_rows,
            ((owners * ROWS, 4 * SLOTS), F32),
            ((SLOTS, SLOTS), F32),
        ],
        flat,
        observations,
        rows,
        cols,
        count,
        bands,
        weight,
    )
    others = from_sectors(info)
    point, top, second = call(
        functools.partial(first_step_kernel, strips, owners),
        [strip_rows, table, message],
        first,
        info,
        column,
        obs_grad,
        limit,
        strip_match,
        send,
        decay,
        weight,
        *others,
    )
    second = trade(second)
    grad, approx = call(
        local_grad_kernel, [strip_rows, table], point, high, low, row_match, obs_slot, info
    )
    others_approx = from_sectors(approx)
    third, differ = call(
        functools.partial(second_step_kernel, strips, owners, betas[1]),
        [message, ((SB_DEV, SOUNDS), F32)],
        first,
        second,
        info,
        column,
        grad,
        limit,
        strip_match,
        send,
        decay,
        weight,
        point,
        top,
        high,
        low,
        row_match,
        obs_slot,
        observations,
        approx,
        *others,
        *others_approx,
    )
    third = trade(third)
    place, band_hot = call(
        functools.partial(place_kernel, strips, owners),
        [
            (((2 * strips + 2) * lines * WIN, owners * ROWS), F32),
            ((owners * ROWS, NBANDS), F32),
        ],
        second,
    )
    coeffs, misfit = call(
        functools.partial(finish_kernel, strips, owners),
        [((lines * WIN, strips * STRIP), F32), ((SB_DEV, SOUNDS), F32)],
        first,
        second,
        third,
        place,
        band_hot,
        decay,
        weight,
        differ,
        bands,
    )
    return (coeffs.reshape(lines, WIN, strips * STRIP), misfit)


def solution(mesh):
    return jax.shard_map(
        body,
        mesh=mesh,
        in_specs=(
            P(("ens", "tile"), None),
            P("tile", None, None),
            P("tile"),
            P("tile"),
            P("tile"),
            P("tile"),
            P(),
            P(),
        ),
        out_specs=(P(("ens", "tile"), None, None), P(("ens", "tile"), None)),
        check_vma=False,
    )
```

```python
import functools
import math

import jax
import jax.numpy as jnp
from jax import lax
from jax.experimental import pallas as pl
from jax.experimental.pallas import tpu as pltpu
from jax.sharding import PartitionSpec as P

WIN = 8
NLAT = 64
SEC_STRIPS = 2
STRIP = 256
SOUNDS = 64
SB_DEV = 32
NBANDS = 128
ITERS = 3
SLOTS = 16
LANES = 128
ROWS = 8
STEP = 0.2

F32 = jnp.float32
BF16 = jnp.bfloat16
HIGHEST = lax.Precision.HIGHEST

LINE, SPOT, BAND, TOTAL, ROW, COL, VALID, FIRST, RANK = range(9)
LINE_ROW, SPOT_ROW, TOTAL_ROW, APPROX_ROW = range(SLOTS, SLOTS + 4)
TABLE_ROWS = SLOTS + ROWS


def momentum_weights(total_steps):
    weights = []
    current = 1.0
    for _ in range(total_steps):
        following = (1.0 + math.sqrt(1.0 + 4.0 * current * current)) / 2.0
        weights.append((current - 1.0) / following)
        current = following
    return weights


def iota(shape, axis):
    return lax.broadcasted_iota(jnp.int32, shape, axis)


def shrink(values, limit):
    return values - jnp.minimum(jnp.maximum(values, -limit), limit)


def to_col(row):
    n = row.shape[1]
    eye = iota((n, n), 0) == iota((n, n), 1)
    return jnp.sum(jnp.where(eye, row, 0.0), axis=1, keepdims=True)


def to_row(col):
    n = col.shape[0]
    eye = iota((n, n), 0) == iota((n, n), 1)
    return jnp.sum(jnp.where(eye, col, 0.0), axis=0, keepdims=True)


def exact_dot(left, right):
    return jnp.dot(left, right, precision=HIGHEST, preferred_element_type=F32)


def dot(left, right):
    return jnp.dot(left, right, preferred_element_type=F32)


def dot_nt(left, right):
    return lax.dot_general(left, right, (((1,), (1,)), ((), ())), preferred_element_type=F32)


def split(values):
    high = values.astype(BF16)
    return high, (values - high.astype(F32)).astype(BF16)


def split_rows(values):
    high = values.astype(BF16)
    rest = values - high.astype(F32)
    middle = rest.astype(BF16)
    return jnp.concatenate([high, middle, (rest - middle.astype(F32)).astype(BF16)], axis=0)


def haar_signs():
    cell = iota((STRIP, STRIP), 0)
    coef = iota((STRIP, STRIP), 1)
    out = jnp.where(coef == 0, 1.0, 0.0)
    m = 1
    while m < STRIP:
        span = STRIP // m
        level = (coef >= m) & (coef < 2 * m)
        within = cell - (coef - m) * span
        sign = jnp.where(within < span // 2, 1.0, -1.0)
        out = jnp.where(level & (within >= 0) & (within < span), sign, out)
        m *= 2
    return out.astype(BF16)


def haar_scales():
    coef = iota((1, STRIP), 1)
    out = jnp.full((1, STRIP), math.sqrt(1.0 / STRIP), F32)
    m = 1
    while m < STRIP:
        out = jnp.where((coef >= m) & (coef < 2 * m), math.sqrt(m / STRIP), out)
        m *= 2
    return out


def top_entry(spot, index, strips):
    if index == 0:
        return jnp.full(spot.shape, math.sqrt(1.0 / strips), F32)
    m = 1 << (index.bit_length() - 1)
    span = strips // m
    start = float((index - m) * span)
    half = start + span / 2
    end = start + span
    scale = math.sqrt(m / strips)
    positive = (spot >= start) & (spot < half)
    negative = (spot >= half) & (spot < end)
    return jnp.where(positive, scale, jnp.where(negative, -scale, 0.0))


def weekly(rows, sectors):
    return [sum(rows[w * sectors + 1 : (w + 1) * sectors], rows[w * sectors]) for w in range(WIN)]


def scan_back(totals, decay):
    running = totals[WIN - 1]
    out = [running]
    for w in range(WIN - 2, -1, -1):
        running = running * decay + totals[w]
        out.insert(0, running)
    return out


def scan_ahead(totals, decay):
    running = totals[0]
    out = [running]
    for w in range(1, WIN):
        running = running * decay + totals[w]
        out.append(running)
    return out


def pick(rows, index):
    out = rows[0]
    for w in range(1, len(rows)):
        out = jnp.where(index == w, rows[w], out)
    return out


def background(first, partial_rows, decay, sectors):
    counts = weekly([first[t, 0:1, :] for t in range(WIN * sectors)], sectors)
    sums = weekly([first[t, 1:2, :] for t in range(WIN * sectors)], sectors)
    partials = weekly(partial_rows, sectors)
    carried = scan_ahead(partials, decay)
    back = [
        SOUNDS * partials[w] + (SOUNDS * counts[w]) * carried[w] - sums[w] for w in range(WIN)
    ]
    returned = scan_back(back, decay)
    return [carried[w] + returned[w] / SOUNDS for w in range(WIN)], carried


def one_hot_bands(band_col):
    return jnp.where(band_col == iota((band_col.shape[0], NBANDS), 1).astype(F32), 1.0, 0.0)


def own_block_mask(rows):
    return iota((rows, SLOTS * SOUNDS), 0) == iota((rows, SLOTS * SOUNDS), 1) // SOUNDS


def back_project(chosen, high_ref, low_ref):
    wide = jnp.concatenate([chosen] * (SLOTS * SOUNDS // LANES), axis=1)
    spread = jnp.where(own_block_mask(SLOTS), wide, 0.0)
    high, low = split(spread)
    both = dot(jnp.concatenate([high, low], axis=0), high_ref[...])
    return both[:SLOTS] + both[SLOTS:] + dot(high, low_ref[...])


def forward(point, high_ref, low_ref):
    high, low = split(point)
    both = dot_nt(jnp.concatenate([high, low], axis=0), high_ref[...])
    full = both[:SLOTS] + both[SLOTS:] + dot_nt(high, low_ref[...])
    return jnp.sum(jnp.where(own_block_mask(SLOTS), full, 0.0), axis=0, keepdims=True)


def fold(weights, values):
    product = weights * values
    total = product[:, :LANES]
    for start in range(LANES, SLOTS * SOUNDS, LANES):
        total = total + product[:, start : start + LANES]
    return total + pltpu.roll(total, SOUNDS, 1)


def start_kernel(*refs):
    fetched = (len(refs) - 2) // 2
    sources, targets = refs[:fetched], refs[fetched : 2 * fetched]
    out_ref, sems = refs[2 * fetched :]
    copies = [
        pltpu.make_async_copy(source, target, sems.at[i])
        for i, (source, target) in enumerate(zip(sources, targets))
    ]
    for copy in copies:
        copy.start()
    copies[0].wait()
    copies[1].wait()
    band_ref, obs_ref = targets[:2]
    hot = one_hot_bands(to_col(band_ref[...].astype(F32)))
    sums = jnp.sum(obs_ref[...], axis=1, keepdims=True)
    counted = jnp.sum(hot, axis=0, keepdims=True)
    summed = jnp.sum(hot * sums, axis=0, keepdims=True)
    for t in range(out_ref.shape[0]):
        out_ref[t, 0:1, :] = counted
        out_ref[t, 1:2, :] = summed
    for copy in copies[2:]:
        copy.wait()


def along_lanes(col):
    n = col.shape[0]
    here = iota((n, LANES), 0) == iota((n, LANES), 1)
    return jnp.sum(jnp.where(here, col, 0.0), axis=0, keepdims=True)


def prepare_kernel(
    strips,
    owners,
    jac_ref,
    obs_ref,
    row_ref,
    col_ref,
    count_ref,
    band_ref,
    weight_ref,
    high_ref,
    low_ref,
    column_ref,
    twin_ref,
    start_grad_ref,
    obs_slot_ref,
    row_match_ref,
    table_ref,
    limit_ref,
    send_ref,
    strip_match_ref,
    top_matrix_ref,
    message_ref,
):
    sectors = strips // SEC_STRIPS
    strips_owner = NLAT * SEC_STRIPS // owners
    sector = lax.rem(lax.axis_index("tile"), sectors).astype(F32)
    signs = haar_signs()
    scales = haar_scales()
    chunk = STRIP
    per = chunk // SOUNDS
    columns = []
    for start in range(0, SLOTS * SOUNDS, chunk):
        high, low = split(jac_ref[start : start + chunk, :])
        changed = (dot(high, signs) + dot(low, signs)) * scales
        high, low = split(changed)
        high_ref[start : start + chunk, :] = high
        low_ref[start : start + chunk, :] = low
        columns.append(jnp.sum(changed.reshape(per, SOUNDS, STRIP), axis=1))
    column = jnp.concatenate(columns, axis=0)

    row_of = to_col(row_ref[...].astype(F32))
    col_row = col_ref[...].astype(F32)
    col_of = to_col(col_row)
    valid_row = jnp.where(iota((1, SLOTS), 1) < count_ref[0], 1.0, 0.0)
    valid = to_col(valid_row)
    line = jnp.floor(col_of / SEC_STRIPS)
    spot = sector * SEC_STRIPS + (col_of - line * SEC_STRIPS)
    row_hot = jnp.where(row_of == iota((SLOTS, SB_DEV), 1).astype(F32), 1.0, 0.0)
    band_row = band_ref[...].astype(F32)
    band = jnp.sum(row_hot * band_row, axis=1, keepdims=True)
    band = jnp.where(valid > 0.0, band, -1.0)
    observed = obs_ref[...]
    obs_slot = exact_dot(row_hot, jnp.concatenate([observed, observed], axis=1))
    obs_slot_ref[...] = obs_slot
    obs_grad = back_project(obs_slot, high_ref, low_ref)
    column = column * valid
    column_ref[...] = column

    lane = iota((SLOTS, SLOTS * SOUNDS), 1) // SOUNDS
    slot = iota((SLOTS, SLOTS * SOUNDS), 0)
    row_lane = jnp.sum(
        jnp.where(lane == slot, (row_of + 1.0) * valid - 1.0, 0.0), axis=0, keepdims=True
    )
    row_match_ref[...] = jnp.where(row_of == row_lane, 1.0, 0.0)

    same = jnp.where(col_of == col_row, 1.0, 0.0)
    before = jnp.where(iota((SLOTS, SLOTS), 1) < iota((SLOTS, SLOTS), 0), 1.0, 0.0)
    other = jnp.where(iota((SLOTS, SLOTS), 1) != iota((SLOTS, SLOTS), 0), same, 0.0)
    strip_match_ref[...] = same * valid_row
    start_grad_ref[...] = -exact_dot(same * valid_row, obs_grad)
    twin_ref[...] = exact_dot(other, column)
    first = jnp.where(jnp.sum(same * before, axis=1, keepdims=True) > 0.0, 0.0, 1.0)
    owner = jnp.floor(col_of / strips_owner)
    owner_row = jnp.floor(col_row / strips_owner)
    rank = jnp.sum(jnp.where(owner == owner_row, before, 0.0), axis=1, keepdims=True)

    at = iota((SLOTS, LANES), 1)
    info = jnp.zeros((SLOTS, LANES), F32)
    for place, values in (
        (LINE, line),
        (SPOT, spot),
        (BAND, band),
        (TOTAL, column[:, 0:1]),
        (ROW, row_of),
        (COL, col_of),
        (VALID, valid),
        (FIRST, first),
        (RANK, rank),
    ):
        info = jnp.where(at == place, values, info)
    table_ref[0:SLOTS, :] = info
    table_ref[SLOTS:TABLE_ROWS, :] = jnp.zeros((TABLE_ROWS - SLOTS, LANES), F32)
    table_ref[LINE_ROW : LINE_ROW + 1, :] = along_lanes(line + 1.0)
    table_ref[SPOT_ROW : SPOT_ROW + 1, :] = along_lanes(spot + 1.0)
    table_ref[TOTAL_ROW : TOTAL_ROW + 1, :] = along_lanes(column[:, 0:1])
    table_ref[APPROX_ROW : APPROX_ROW + 1, :] = along_lanes(-obs_grad[:, 0:1] * valid)
    matrix = jnp.zeros((SLOTS, LANES), F32)
    for t in range(strips):
        matrix = jnp.where(at == t, top_entry(spot, t, strips), matrix)
    top_matrix_ref[...] = matrix

    local = iota((1, LANES), 1)
    limits_low = jnp.zeros((SLOTS, LANES), F32)
    limits_high = jnp.zeros((SLOTS, LANES), F32)
    for j in range(strips):
        low_row = jnp.zeros((1, LANES), F32)
        m = 1
        while m < LANES:
            start = strips * m + j * m
            block = weight_ref[0:1, start // LANES * LANES : start // LANES * LANES + LANES]
            shift = (m - start % LANES) % LANES
            moved = pltpu.roll(jnp.broadcast_to(block, (ROWS, LANES)), shift, 1)[0:1] if shift else block
            low_row = jnp.where((local >= m) & (local < 2 * m), moved, low_row)
            m *= 2
        high_row = weight_ref[0:1, (strips + j) * LANES : (strips + j + 1) * LANES]
        limits_low = jnp.where(spot == float(j), low_row, limits_low)
        limits_high = jnp.where(spot == float(j), high_row, limits_high)
    limit_ref[:, :LANES] = STEP * limits_low
    limit_ref[:, LANES:] = STEP * limits_high

    shape = (owners * ROWS, 3 * 4 * SLOTS)
    target = (iota(shape, 0) // ROWS).astype(F32)
    kind = iota(shape, 0) % ROWS
    place = iota(shape, 1) % (4 * SLOTS)
    group = place // SLOTS
    slim_shape = (SLOTS, shape[1])
    slim = iota(slim_shape, 1) % SLOTS == iota(slim_shape, 0)
    owner_wide = jnp.sum(jnp.where(slim, owner, 0.0), axis=0, keepdims=True)
    rank_wide = jnp.sum(jnp.where(slim, rank, 0.0), axis=0, keepdims=True)
    kind_f = kind.astype(F32)
    hit = (group == 0) & (kind_f == 2.0 * rank_wide)
    hit = hit | ((group == 1) & (kind_f == 2.0 * rank_wide + 1.0))
    hit = hit | ((group == 2) & (kind == 5))
    hit = (hit & (owner_wide == target)) | ((place == 3 * SLOTS) & (kind == 4))
    send = jnp.where(hit, 1.0, 0.0).astype(BF16)
    send_ref[...] = send

    at_f = at.astype(F32)
    base = rank * (LANES // 2)
    meta = jnp.where(at_f == base, col_of - owner * strips_owner + 1.0, 0.0)
    meta = jnp.where(at_f == base + 1.0, band + 1.0, meta)
    message_ref[...] = message_rows(send, column, meta, None).reshape(message_ref.shape)


def message_rows(send, strips_part, meta, partial):
    if partial is None:
        bottom = jnp.zeros((SLOTS, LANES), F32)
    else:
        bottom = jnp.where(iota((SLOTS, LANES), 0) == 0, partial, 0.0)
    stacked = jnp.concatenate([strips_part[:, :LANES], strips_part[:, LANES:], meta, bottom], axis=0)
    return dot(send, split_rows(stacked))


def side_by_side(rows):
    out = rows[0]
    for i, row in enumerate(rows[1:], 1):
        wide = jnp.broadcast_to(row, (ROWS, LANES))
        out = out + pltpu.roll(wide, i * SLOTS, 1)[0:1]
    return out


def slot_scalars(hot, scalar):
    col = jnp.sum(hot * scalar, axis=1, keepdims=True)
    return col, along_lanes(col)


def advance(strips, col, row, grads, column, twin, same, approx_row, total_row, line_tops):
    other = jnp.sum(jnp.where(same > 0.0, row[:, :SLOTS], 0.0), axis=1, keepdims=True)
    full = grads + col[:SLOTS] * column + other * twin
    sources = approx_row + row * total_row
    at = iota((SLOTS, LANES), 1)
    top_grad = jnp.zeros((SLOTS, LANES), F32)
    for t in range(strips):
        value = jnp.sum(line_tops[t * SLOTS : (t + 1) * SLOTS] * sources, axis=1, keepdims=True)
        top_grad = jnp.where(at == t, value, top_grad)
    return full, top_grad


def with_approx(point, top, matrix):
    approx = jnp.sum(matrix * top, axis=1, keepdims=True)
    return jnp.where(iota((SLOTS, STRIP), 1) == 0, approx, point)


def band_partial(point, column, hot):
    dots = jnp.sum(point * column, axis=1, keepdims=True)
    return jnp.sum(hot * dots, axis=0, keepdims=True) / SOUNDS


def twins(strip_match):
    return jnp.where(iota((SLOTS, SLOTS), 0) == iota((SLOTS, SLOTS), 1), 0.0, strip_match)


def first_step_kernel(
    strips,
    owners,
    first_ref,
    column_ref,
    twin_ref,
    grad_ref,
    limit_ref,
    strip_match_ref,
    top_matrix_ref,
    decay_ref,
    weight_ref,
    prepared_ref,
    *rest,
):
    sectors = strips // SEC_STRIPS
    tables = rest[:sectors]
    point_ref, top_ref, message_ref, hot_ref, line_tops_ref = rest[sectors:]
    window = lax.axis_index("tile") // sectors
    sums = weekly([first_ref[t, 1:2, :] for t in range(owners)], sectors)
    returned = scan_back([-s for s in sums], decay_ref[...])
    scalar = pick(returned, window) / SOUNDS
    hot = jnp.concatenate([one_hot_bands(t[0:SLOTS, BAND : BAND + 1]) for t in tables], axis=0)
    hot_ref[...] = hot

    def row(index):
        return side_by_side([t[index : index + 1, :] for t in tables])

    spot_row = row(SPOT_ROW) - 1.0
    on_line = tables[0][0:SLOTS, LINE : LINE + 1] + 1.0 == row(LINE_ROW)
    line_tops = jnp.concatenate(
        [jnp.where(on_line, top_entry(spot_row, t, strips), 0.0) for t in range(strips)], axis=0
    )
    line_tops_ref[...] = line_tops
    column = column_ref[...]
    col, along = slot_scalars(hot, scalar)
    grads, top_grad = advance(
        strips,
        col,
        along,
        grad_ref[...],
        column,
        twin_ref[...],
        twins(strip_match_ref[...]),
        row(APPROX_ROW),
        row(TOTAL_ROW),
        line_tops,
    )
    updated = shrink(-STEP * grads, limit_ref[...])
    top = shrink(-STEP * top_grad, STEP * weight_ref[0:1, :LANES])
    point = with_approx(updated, top, top_matrix_ref[...])
    point_ref[...] = point
    top_ref[...] = top
    partial = band_partial(point, column, hot[:SLOTS])
    is_partial = iota(message_ref.shape, 1) == 4
    message_ref[...] = jnp.where(is_partial, partial.reshape(1, 1, LANES), prepared_ref[...])


def local_grad_kernel(
    strips,
    point_ref,
    high_ref,
    low_ref,
    row_match_ref,
    obs_slot_ref,
    strip_match_ref,
    *rest,
):
    sectors = strips // SEC_STRIPS
    tables = rest[:sectors]
    grad_ref, approx_ref, lead_ref = rest[sectors:]
    values = forward(point_ref[...], high_ref, low_ref)
    chosen = fold(row_match_ref[...], values) - obs_slot_ref[...]
    grad = back_project(chosen, high_ref, low_ref)
    grad_ref[...] = exact_dot(strip_match_ref[...], grad)
    info = tables[0][0:SLOTS, :]
    approx = grad[:, 0:1] * info[:, VALID : VALID + 1]
    approx_ref[...] = jnp.broadcast_to(along_lanes(approx), approx_ref.shape)

    sector = lax.rem(lax.axis_index("tile"), sectors).astype(F32)
    line_row = side_by_side([t[LINE_ROW : LINE_ROW + 1, :] for t in tables])
    spot_row = side_by_side([t[SPOT_ROW : SPOT_ROW + 1, :] for t in tables])
    sector_row = jnp.floor((spot_row - 1.0) / SEC_STRIPS)
    lane = iota((SLOTS, LANES), 1)
    before = jnp.where(lane < iota((SLOTS, LANES), 0), 1.0, 0.0)
    earlier = jnp.where(lane < SLOTS, before, jnp.where(sector_row < sector, 1.0, 0.0))
    on_line = info[:, LINE : LINE + 1] + 1.0 == line_row
    taken = jnp.sum(jnp.where(on_line, earlier, 0.0), axis=1, keepdims=True)
    lead_ref[...] = jnp.broadcast_to(jnp.where(taken > 0.0, 0.0, 1.0), lead_ref.shape)


def second_step_kernel(
    strips,
    owners,
    beta,
    first_ref,
    second_ref,
    column_ref,
    twin_ref,
    grad_ref,
    limit_ref,
    strip_match_ref,
    top_matrix_ref,
    decay_ref,
    weight_ref,
    hot_ref,
    line_tops_ref,
    lead_ref,
    send_ref,
    point_ref,
    top_ref,
    high_ref,
    low_ref,
    row_match_ref,
    obs_slot_ref,
    *rest,
):
    sectors = strips // SEC_STRIPS
    tables, rest = rest[:sectors], rest[sectors:]
    approx_refs, rest = rest[:sectors], rest[sectors:]
    message_ref, values_ref = rest
    window = lax.axis_index("tile") // sectors
    combined, _ = background(
        first_ref, [second_ref[t, 4:5, :] for t in range(owners)], decay_ref[...], sectors
    )
    hot = hot_ref[...]
    column = column_ref[...]
    col, along = slot_scalars(hot, pick(combined, window))
    grads, top_grad = advance(
        strips,
        col,
        along,
        grad_ref[...],
        column,
        twin_ref[...],
        twins(strip_match_ref[...]),
        side_by_side([r[0:1, :] for r in approx_refs]),
        side_by_side([t[TOTAL_ROW : TOTAL_ROW + 1, :] for t in tables]),
        line_tops_ref[...],
    )
    old = point_ref[...]
    old_top = top_ref[...]
    updated = shrink(old - STEP * grads, limit_ref[...])
    top = shrink(old_top - STEP * top_grad, STEP * weight_ref[0:1, :LANES])
    point = updated + beta * (updated - old)
    top = top + beta * (top - old_top)
    point = with_approx(point, top, top_matrix_ref[...])
    values = forward(point, high_ref, low_ref)
    values_ref[...] = values
    chosen = fold(row_match_ref[...], values) - obs_slot_ref[...]
    grad = back_project(chosen, high_ref, low_ref)

    partial = band_partial(point, column, hot[:SLOTS])
    info = tables[0][0:SLOTS, :]
    valid = info[:, VALID : VALID + 1]
    top = top * lead_ref[:, 0:1]
    rank = info[:, RANK : RANK + 1]
    meta = jnp.where(rank == 0.0, pltpu.roll(top, ROWS, 1), pltpu.roll(top, LANES // 2 + ROWS, 1))
    kept = jnp.where(iota((SLOTS, STRIP), 1) == 0, 0.0, point * info[:, FIRST : FIRST + 1])
    rows = message_rows(send_ref[...], kept - STEP * (valid * grad), meta, partial)
    message_ref[...] = rows.reshape(message_ref.shape)


def place_kernel(
    strips,
    owners,
    second_ref,
    table_ref,
    values_ref,
    obs_ref,
    band_ref,
    place_ref,
    band_hot_ref,
    scaled_ref,
    differ_ref,
    block_hot_ref,
):
    sectors = strips // SEC_STRIPS
    lines = NLAT // owners
    count = owners * ROWS
    meta = second_ref[:, 5, :]
    wide = (owners, count)
    pair_of = iota(wide, 1) // ROWS == iota(wide, 0)
    kind = iota((1, count), 1) % ROWS
    tall = (count, owners)
    tall_pair = iota(tall, 0) // ROWS == iota(tall, 1)
    tall_kind = iota((count, 1), 0) % ROWS
    strip_rows = []
    band_col = jnp.zeros((count, 1), F32)
    for q in range(2):
        strip = meta[:, q * (LANES // 2) : q * (LANES // 2) + 1]
        band = meta[:, q * (LANES // 2) + 1 : q * (LANES // 2) + 2]
        strip_rows.append(jnp.sum(jnp.where(pair_of, strip, 0.0), axis=0, keepdims=True) - 1.0)
        band_tall = jnp.sum(jnp.where(tall_pair, to_row(band), 0.0), axis=1, keepdims=True)
        band_col = jnp.where(tall_kind // 2 == q, band_tall, band_col)
    band_hot_ref[...] = one_hot_bands(band_col - 1.0)
    scaled_ref[...] = jnp.where(tall_kind < 4, STEP * second_ref[...].reshape(count, LANES), 0.0)

    def line_of(strip):
        return jnp.floor(strip / SEC_STRIPS)

    blocks = lines * WIN
    pair = iota((1, count), 1) // ROWS
    window = pair // sectors
    sector = (pair - window * sectors).astype(F32)
    line_col = (iota((blocks, 1), 0) // WIN).astype(F32)
    window_col = iota((blocks, 1), 0) % WIN
    strip_row = jnp.where(kind < 2, strip_rows[0], strip_rows[1])
    slot_line = line_of(strip_row)
    slot_spot = sector * SEC_STRIPS + strip_row - slot_line * SEC_STRIPS
    base = (window == window_col) & (slot_line == line_col) & (strip_row >= 0.0)
    base = jnp.where(base & (kind < 4), 1.0, 0.0)
    parts = []
    for half in range(2):
        part = jnp.where(kind % 2 == half, base, 0.0)
        for j in range(strips):
            parts.append(jnp.where(slot_spot == float(j), part, 0.0))
    for q in range(2):
        hit = (window == window_col) & (line_of(strip_rows[q]) == line_col) & (strip_rows[q] >= 0.0) & (kind == 5)
        parts.append(jnp.where(hit, 1.0, 0.0))
    place = jnp.concatenate(parts, axis=0).astype(BF16)
    place_ref[...] = jnp.concatenate([place, place, place], axis=1)

    info = table_ref[0:SLOTS, :]
    lane = iota((SLOTS, SLOTS * SOUNDS), 1) // SOUNDS
    slot = iota((SLOTS, SLOTS * SOUNDS), 0)
    row_lane = jnp.sum(
        jnp.where(lane == slot, (info[:, ROW : ROW + 1] + 1.0) * info[:, VALID : VALID + 1], 0.0),
        axis=0,
        keepdims=True,
    )
    per_row = jnp.where(iota((SB_DEV, SLOTS * SOUNDS), 0).astype(F32) + 1.0 == row_lane, 1.0, 0.0)
    differ_ref[...] = fold(per_row, values_ref[...])[:, :SOUNDS] - obs_ref[...]
    block_hot_ref[...] = one_hot_bands(to_col(band_ref[...].astype(F32)))


def finish_kernel(
    strips,
    owners,
    first_ref,
    third_ref,
    place_ref,
    band_hot_ref,
    scaled_ref,
    decay_ref,
    weight_ref,
    differ_ref,
    block_hot_ref,
    out_ref,
    misfit_ref,
):
    sectors = strips // SEC_STRIPS
    blocks = NLAT // owners * WIN
    count = owners * ROWS
    window = lax.axis_index("tile") // sectors
    combined, carried = background(
        first_ref, [third_ref[t, 4:5, :] for t in range(owners)], decay_ref[...], sectors
    )
    spread = jnp.concatenate(
        [jnp.broadcast_to(row, (sectors * ROWS, NBANDS)) for row in combined], axis=0
    )
    scalars = jnp.sum(band_hot_ref[...] * spread, axis=1, keepdims=True)
    rows = third_ref[...].reshape(count, LANES) - scalars * scaled_ref[...]
    placed = dot(place_ref[...], split_rows(rows))
    offset = jnp.sum(block_hot_ref[...] * pick(carried, window), axis=1, keepdims=True)
    misfit_ref[...] = differ_ref[...] + offset

    lane = iota((1, LANES), 1)
    for j in range(strips):
        start = (strips + j) * LANES
        values = placed[(strips + j) * blocks : (strips + j + 1) * blocks]
        out_ref[:, start : start + LANES] = shrink(values, STEP * weight_ref[0:1, start : start + LANES])

    low = [placed[j * blocks : (j + 1) * blocks] for j in range(strips)]
    tops = [placed[(2 * strips + q) * blocks : (2 * strips + q + 1) * blocks] for q in range(2)]
    top = pltpu.roll(tops[0], LANES - ROWS, 1) + pltpu.roll(tops[1], LANES // 2 - ROWS, 1)
    made = [jnp.zeros((blocks, LANES), F32) for _ in range(strips)]
    for t in range(strips):
        value = jnp.zeros((blocks, 1), F32)
        for j in range(strips):
            entry = top_value(j, t, strips)
            if entry:
                value = value + entry * low[j][:, 0:1]
        made[0] = jnp.where(lane == t, value + top, made[0])
    m = 1
    while m < LANES:
        for j in range(strips):
            start = strips * m + j * m
            block = start // LANES
            shift = (start % LANES - m) % LANES
            moved = pltpu.roll(low[j], shift, 1) if shift else low[j]
            inside = (lane >= start % LANES) & (lane < start % LANES + m)
            made[block] = jnp.where(inside, moved, made[block])
        m *= 2
    for block in range(strips):
        start = block * LANES
        out_ref[:, start : start + LANES] = shrink(made[block], STEP * weight_ref[0:1, start : start + LANES])


def top_value(spot, index, strips):
    if index == 0:
        return math.sqrt(1.0 / strips)
    m = 1 << (index.bit_length() - 1)
    span = strips // m
    within = spot - (index - m) * span
    if within < 0 or within >= span:
        return 0.0
    return math.sqrt(m / strips) * (1.0 if within < span // 2 else -1.0)


def call(kernel, outs, *operands, **kwargs):
    return pl.pallas_call(
        kernel,
        out_shape=[jax.ShapeDtypeStruct(shape, dtype) for shape, dtype in outs],
        compiler_params=pltpu.CompilerParams(vmem_limit_bytes=40 * 1024 * 1024),
        **kwargs,
    )(*operands)


def body(
    observations,
    jacobian,
    block_row,
    block_col,
    block_count,
    block_band,
    carry_decay,
    sparsity_weight,
):
    owners = lax.axis_size("tile")
    sectors = owners // WIN
    strips = sectors * SEC_STRIPS
    lines = NLAT // owners
    betas = momentum_weights(ITERS)
    arguments = [
        block_band.reshape(1, SB_DEV),
        observations,
        jacobian.reshape(SLOTS * SOUNDS, STRIP),
        block_row.reshape(1, SLOTS),
        block_col.reshape(1, SLOTS),
        carry_decay.reshape(1, NBANDS),
        sparsity_weight.reshape(1, -1),
    ]
    message = ((owners, ROWS, LANES), F32)
    narrow = ((SLOTS, LANES), F32)
    strip_rows = ((SLOTS, STRIP), F32)
    table_rows = ((TABLE_ROWS, LANES), F32)

    def trade(values):
        return lax.all_to_all(values, "tile", 0, 0, tiled=True)

    def with_sectors(values):
        found = [values]
        for shift in range(1, sectors):
            pairs = [
                (d, d // sectors * sectors + (d + shift) % sectors) for d in range(owners)
            ]
            found.append(lax.ppermute(values, "tile", pairs))
        return found

    arguments = [pltpu.with_memory_space_constraint(a, pltpu.HBM) for a in arguments]
    bands, observed, flat, rows, cols, decay, weight, first = call(
        start_kernel,
        [(a.shape, a.dtype) for a in arguments] + [((owners, 2, LANES), F32)],
        *arguments,
        in_specs=[pl.BlockSpec(memory_space=pltpu.HBM)] * len(arguments),
        out_specs=[pl.BlockSpec(memory_space=pltpu.VMEM)] * (len(arguments) + 1),
        scratch_shapes=[pltpu.SemaphoreType.DMA((len(arguments),))],
    )
    first = trade(first)
    (
        high,
        low,
        column,
        twin,
        start_grad,
        obs_slot,
        row_match,
        table,
        limit,
        send,
        strip_match,
        top_matrix,
        prepared,
    ) = call(
        functools.partial(prepare_kernel, strips, owners),
        [
            ((SLOTS * SOUNDS, STRIP), BF16),
            ((SLOTS * SOUNDS, STRIP), BF16),
            strip_rows,
            strip_rows,
            strip_rows,
            narrow,
            ((SLOTS, SLOTS * SOUNDS), F32),
            table_rows,
            strip_rows,
            ((owners * ROWS, 3 * 4 * SLOTS), BF16),
            ((SLOTS, SLOTS), F32),
            narrow,
            message,
        ],
        flat,
        observed,
        rows,
        cols,
        block_count,
        bands,
        weight,
        in_specs=[
            pl.BlockSpec(memory_space=pltpu.SMEM if i == 4 else pltpu.VMEM) for i in range(7)
        ],
    )
    tables = with_sectors(table)
    point, top, second, hot, line_tops = call(
        functools.partial(first_step_kernel, strips, owners),
        [
            strip_rows,
            narrow,
            message,
            ((sectors * SLOTS, NBANDS), F32),
            ((strips * SLOTS, LANES), F32),
        ],
        first,
        column,
        twin,
        start_grad,
        limit,
        strip_match,
        top_matrix,
        decay,
        weight,
        prepared,
        *tables,
    )
    second = trade(second)
    grad, approx, lead = call(
        functools.partial(local_grad_kernel, strips),
        [strip_rows, ((ROWS, LANES), F32), narrow],
        point,
        high,
        low,
        row_match,
        obs_slot,
        strip_match,
        *tables,
    )
    third, values = call(
        functools.partial(second_step_kernel, strips, owners, betas[1]),
        [message, ((1, SLOTS * SOUNDS), F32)],
        first,
        second,
        column,
        twin,
        grad,
        limit,
        strip_match,
        top_matrix,
        decay,
        weight,
        hot,
        line_tops,
        lead,
        send,
        point,
        top,
        high,
        low,
        row_match,
        obs_slot,
        *tables,
        *with_sectors(approx),
    )
    third = trade(third)
    placed_rows = (2 * strips + 2) * lines * WIN
    place, band_hot, scaled, differ, block_hot = call(
        functools.partial(place_kernel, strips, owners),
        [
            ((placed_rows, 3 * owners * ROWS), BF16),
            ((owners * ROWS, NBANDS), F32),
            ((owners * ROWS, LANES), F32),
            ((SB_DEV, SOUNDS), F32),
            ((SB_DEV, NBANDS), F32),
        ],
        second,
        table,
        values,
        observed,
        bands,
    )
    coeffs, misfit = call(
        functools.partial(finish_kernel, strips, owners),
        [((lines * WIN, strips * STRIP), F32), ((SB_DEV, SOUNDS), F32)],
        first,
        third,
        place,
        band_hot,
        scaled,
        decay,
        weight,
        differ,
        block_hot,
    )
    return (coeffs.reshape(lines, WIN, strips * STRIP), misfit)


def solution(mesh):
    return jax.shard_map(
        body,
        mesh=mesh,
        in_specs=(
            P(("ens", "tile"), None),
            P("tile", None, None),
            P("tile"),
            P("tile"),
            P("tile"),
            P("tile"),
            P(),
            P(),
        ),
        out_specs=(P(("ens", "tile"), None, None), P(("ens", "tile"), None)),
        check_vma=False,
    )
```

```python
import functools
import math

import jax
import jax.numpy as jnp
from jax import lax
from jax.experimental import pallas as pl
from jax.experimental.pallas import tpu as pltpu
from jax.sharding import PartitionSpec as P

WIN = 8
NLAT = 64
SEC_STRIPS = 2
STRIP = 256
SOUNDS = 64
SB_DEV = 32
NBANDS = 128
ITERS = 3
SLOTS = 16
LANES = 128
ROWS = 8
STEP = 0.2
PIECES = 8

F32 = jnp.float32
BF16 = jnp.bfloat16
HIGHEST = lax.Precision.HIGHEST

LINE, SPOT, BAND, TOTAL, ROW, COL, VALID = range(7)
LINE_ROW, SPOT_ROW, TOTAL_ROW, APPROX_ROW = range(SLOTS, SLOTS + 4)
TABLE_ROWS = SLOTS + ROWS


def momentum_weights(total_steps):
    weights = []
    current = 1.0
    for _ in range(total_steps):
        following = (1.0 + math.sqrt(1.0 + 4.0 * current * current)) / 2.0
        weights.append((current - 1.0) / following)
        current = following
    return weights


def iota(shape, axis):
    return lax.broadcasted_iota(jnp.int32, shape, axis)


def shrink(values, limit):
    return values - jnp.minimum(jnp.maximum(values, -limit), limit)


def to_col(row):
    n = row.shape[1]
    eye = iota((n, n), 0) == iota((n, n), 1)
    return jnp.sum(jnp.where(eye, row, 0.0), axis=1, keepdims=True)


def to_row(col):
    n = col.shape[0]
    eye = iota((n, n), 0) == iota((n, n), 1)
    return jnp.sum(jnp.where(eye, col, 0.0), axis=0, keepdims=True)


def exact_dot(left, right):
    return jnp.dot(left, right, precision=HIGHEST, preferred_element_type=F32)


def dot(left, right):
    return jnp.dot(left, right, preferred_element_type=F32)


def dot_nt(left, right):
    return lax.dot_general(left, right, (((1,), (1,)), ((), ())), preferred_element_type=F32)


def split(values):
    high = values.astype(BF16)
    return high, (values - high.astype(F32)).astype(BF16)


def split_rows(values):
    high = values.astype(BF16)
    rest = values - high.astype(F32)
    middle = rest.astype(BF16)
    return jnp.concatenate([high, middle, (rest - middle.astype(F32)).astype(BF16)], axis=0)


def haar_signs():
    cell = iota((STRIP, STRIP), 0)
    coef = iota((STRIP, STRIP), 1)
    out = jnp.where(coef == 0, 1.0, 0.0)
    m = 1
    while m < STRIP:
        span = STRIP // m
        level = (coef >= m) & (coef < 2 * m)
        within = cell - (coef - m) * span
        sign = jnp.where(within < span // 2, 1.0, -1.0)
        out = jnp.where(level & (within >= 0) & (within < span), sign, out)
        m *= 2
    return out.astype(BF16)


def haar_scales():
    coef = iota((1, STRIP), 1)
    out = jnp.full((1, STRIP), math.sqrt(1.0 / STRIP), F32)
    m = 1
    while m < STRIP:
        out = jnp.where((coef >= m) & (coef < 2 * m), math.sqrt(m / STRIP), out)
        m *= 2
    return out


def top_entry(spot, index, strips):
    if index == 0:
        return jnp.full(spot.shape, math.sqrt(1.0 / strips), F32)
    m = 1 << (index.bit_length() - 1)
    span = strips // m
    start = float((index - m) * span)
    half = start + span / 2
    end = start + span
    scale = math.sqrt(m / strips)
    positive = (spot >= start) & (spot < half)
    negative = (spot >= half) & (spot < end)
    return jnp.where(positive, scale, jnp.where(negative, -scale, 0.0))


def weekly(rows, sectors):
    return [sum(rows[w * sectors + 1 : (w + 1) * sectors], rows[w * sectors]) for w in range(WIN)]


def scan_back(totals, decay):
    running = totals[WIN - 1]
    out = [running]
    for w in range(WIN - 2, -1, -1):
        running = running * decay + totals[w]
        out.insert(0, running)
    return out


def scan_ahead(totals, decay):
    running = totals[0]
    out = [running]
    for w in range(1, WIN):
        running = running * decay + totals[w]
        out.append(running)
    return out


def pick(rows, index):
    out = rows[0]
    for w in range(1, len(rows)):
        out = jnp.where(index == w, rows[w], out)
    return out


def background(first, partial_rows, decay, sectors):
    counts = weekly([first[t, 0:1, :] for t in range(WIN * sectors)], sectors)
    sums = weekly([first[t, 1:2, :] for t in range(WIN * sectors)], sectors)
    partials = weekly(partial_rows, sectors)
    carried = scan_ahead(partials, decay)
    back = [
        SOUNDS * partials[w] + (SOUNDS * counts[w]) * carried[w] - sums[w] for w in range(WIN)
    ]
    returned = scan_back(back, decay)
    return [carried[w] + returned[w] / SOUNDS for w in range(WIN)], carried


def one_hot_bands(band_col):
    return jnp.where(band_col == iota((band_col.shape[0], NBANDS), 1).astype(F32), 1.0, 0.0)


def own_block_mask(rows):
    return iota((rows, SLOTS * SOUNDS), 0) == iota((rows, SLOTS * SOUNDS), 1) // SOUNDS


def back_project(chosen, high_ref, low_ref):
    wide = jnp.concatenate([chosen] * (SLOTS * SOUNDS // LANES), axis=1)
    spread = jnp.where(own_block_mask(SLOTS), wide, 0.0)
    high, low = split(spread)
    both = dot(jnp.concatenate([high, low], axis=0), high_ref[...])
    return both[:SLOTS] + both[SLOTS:] + dot(high, low_ref[...])


def forward(point, high_ref, low_ref):
    high, low = split(point)
    both = dot_nt(jnp.concatenate([high, low], axis=0), high_ref[...])
    full = both[:SLOTS] + both[SLOTS:] + dot_nt(high, low_ref[...])
    return jnp.sum(jnp.where(own_block_mask(SLOTS), full, 0.0), axis=0, keepdims=True)


def fold(weights, values):
    product = weights * values
    total = product[:, :LANES]
    for start in range(LANES, SLOTS * SOUNDS, LANES):
        total = total + product[:, start : start + LANES]
    return total + pltpu.roll(total, SOUNDS, 1)


def start_kernel(*refs):
    fetched = (len(refs) - 2) // 2
    sources, targets = refs[:fetched], refs[fetched : 2 * fetched]
    out_ref, sems = refs[2 * fetched :]
    pairs = list(zip(sources, targets))
    wide_source, wide_target = pairs.pop()
    part = wide_source.shape[0] // PIECES
    for start in range(0, wide_source.shape[0], part):
        pairs.append((wide_source.at[start : start + part], wide_target.at[start : start + part]))
    copies = [
        pltpu.make_async_copy(source, target, sems.at[i])
        for i, (source, target) in enumerate(pairs)
    ]
    for copy in copies:
        copy.start()
    copies[0].wait()
    copies[1].wait()
    band_ref, obs_ref = targets[:2]
    hot = one_hot_bands(to_col(band_ref[...].astype(F32)))
    sums = jnp.sum(obs_ref[...], axis=1, keepdims=True)
    counted = jnp.sum(hot, axis=0, keepdims=True)
    summed = jnp.sum(hot * sums, axis=0, keepdims=True)
    for t in range(out_ref.shape[0]):
        out_ref[t, 0:1, :] = counted
        out_ref[t, 1:2, :] = summed
    for copy in copies[2:]:
        copy.wait()


def along_lanes(col):
    n = col.shape[0]
    here = iota((n, LANES), 0) == iota((n, LANES), 1)
    return jnp.sum(jnp.where(here, col, 0.0), axis=0, keepdims=True)


def transform_kernel(
    strips,
    jac_ref,
    obs_ref,
    row_ref,
    col_ref,
    count_ref,
    band_ref,
    high_ref,
    low_ref,
    column_ref,
    obs_grad_ref,
    obs_slot_ref,
    table_ref,
):
    sectors = strips // SEC_STRIPS
    sector = lax.rem(lax.axis_index("tile"), sectors).astype(F32)
    signs = haar_signs()
    scales = haar_scales()
    chunk = STRIP
    per = chunk // SOUNDS
    columns = []
    for start in range(0, SLOTS * SOUNDS, chunk):
        high, low = split(jac_ref[start : start + chunk, :])
        changed = (dot(high, signs) + dot(low, signs)) * scales
        high, low = split(changed)
        high_ref[start : start + chunk, :] = high
        low_ref[start : start + chunk, :] = low
        columns.append(jnp.sum(changed.reshape(per, SOUNDS, STRIP), axis=1))
    column = jnp.concatenate(columns, axis=0)

    row_of = to_col(row_ref[...].astype(F32))
    col_of = to_col(col_ref[...].astype(F32))
    valid = jnp.where(iota((SLOTS, 1), 0) < count_ref[0], 1.0, 0.0)
    line = jnp.floor(col_of / SEC_STRIPS)
    spot = sector * SEC_STRIPS + (col_of - line * SEC_STRIPS)
    row_hot = jnp.where(row_of == iota((SLOTS, SB_DEV), 1).astype(F32), 1.0, 0.0)
    band_row = band_ref[...].astype(F32)
    band = jnp.sum(row_hot * band_row, axis=1, keepdims=True)
    band = jnp.where(valid > 0.0, band, -1.0)
    observed = obs_ref[...]
    obs_slot = exact_dot(row_hot, jnp.concatenate([observed, observed], axis=1))
    obs_slot_ref[...] = obs_slot
    obs_grad = back_project(obs_slot, high_ref, low_ref)
    obs_grad_ref[...] = obs_grad
    column = column * valid
    column_ref[...] = column

    at = iota((SLOTS, LANES), 1)
    info = jnp.zeros((SLOTS, LANES), F32)
    for place, values in (
        (LINE, line),
        (SPOT, spot),
        (BAND, band),
        (TOTAL, column[:, 0:1]),
        (ROW, row_of),
        (COL, col_of),
        (VALID, valid),
    ):
        info = jnp.where(at == place, values, info)
    table_ref[0:SLOTS, :] = info
    table_ref[SLOTS:TABLE_ROWS, :] = jnp.zeros((TABLE_ROWS - SLOTS, LANES), F32)
    table_ref[LINE_ROW : LINE_ROW + 1, :] = along_lanes(line + 1.0)
    table_ref[SPOT_ROW : SPOT_ROW + 1, :] = along_lanes(spot + 1.0)
    table_ref[TOTAL_ROW : TOTAL_ROW + 1, :] = along_lanes(column[:, 0:1])
    table_ref[APPROX_ROW : APPROX_ROW + 1, :] = along_lanes(-obs_grad[:, 0:1] * valid)


def prepare_kernel(
    strips,
    owners,
    column_ref,
    obs_grad_ref,
    table_ref,
    weight_ref,
    twin_ref,
    start_grad_ref,
    row_match_ref,
    limit_ref,
    send_ref,
    strip_match_ref,
    top_matrix_ref,
    message_ref,
    rank_ref,
):
    strips_owner = NLAT * SEC_STRIPS // owners
    column = column_ref[...]
    info = table_ref[0:SLOTS, :]
    spot = info[:, SPOT : SPOT + 1]
    band = info[:, BAND : BAND + 1]
    row_of = info[:, ROW : ROW + 1]
    col_of = info[:, COL : COL + 1]
    valid = info[:, VALID : VALID + 1]
    col_row = to_row(col_of)
    valid_row = to_row(valid)

    lane = iota((SLOTS, SLOTS * SOUNDS), 1) // SOUNDS
    slot = iota((SLOTS, SLOTS * SOUNDS), 0)
    row_lane = jnp.sum(
        jnp.where(lane == slot, (row_of + 1.0) * valid - 1.0, 0.0), axis=0, keepdims=True
    )
    row_match_ref[...] = jnp.where(row_of == row_lane, 1.0, 0.0)

    same = jnp.where(col_of == col_row, 1.0, 0.0)
    before = jnp.where(iota((SLOTS, SLOTS), 1) < iota((SLOTS, SLOTS), 0), 1.0, 0.0)
    other = jnp.where(iota((SLOTS, SLOTS), 1) != iota((SLOTS, SLOTS), 0), same, 0.0)
    strip_match_ref[...] = same * valid_row
    start_grad_ref[...] = -exact_dot(same * valid_row, obs_grad_ref[...])
    twin_ref[...] = exact_dot(other, column)
    first = jnp.where(jnp.sum(same * before, axis=1, keepdims=True) > 0.0, 0.0, 1.0)
    owner = jnp.floor(col_of / strips_owner)
    owner_row = jnp.floor(col_row / strips_owner)
    rank = jnp.sum(jnp.where(owner == owner_row, before, 0.0), axis=1, keepdims=True)

    at = iota((SLOTS, LANES), 1)
    rank_ref[...] = jnp.where(at == 0, rank, jnp.where(at == 1, first, 0.0))
    matrix = jnp.zeros((SLOTS, LANES), F32)
    for t in range(strips):
        matrix = jnp.where(at == t, top_entry(spot, t, strips), matrix)
    top_matrix_ref[...] = matrix

    local = iota((1, LANES), 1)
    limits_low = jnp.zeros((SLOTS, LANES), F32)
    limits_high = jnp.zeros((SLOTS, LANES), F32)
    for j in range(strips):
        low_row = jnp.zeros((1, LANES), F32)
        m = 1
        while m < LANES:
            start = strips * m + j * m
            block = weight_ref[0:1, start // LANES * LANES : start // LANES * LANES + LANES]
            shift = (m - start % LANES) % LANES
            moved = pltpu.roll(jnp.broadcast_to(block, (ROWS, LANES)), shift, 1)[0:1] if shift else block
            low_row = jnp.where((local >= m) & (local < 2 * m), moved, low_row)
            m *= 2
        high_row = weight_ref[0:1, (strips + j) * LANES : (strips + j + 1) * LANES]
        limits_low = jnp.where(spot == float(j), low_row, limits_low)
        limits_high = jnp.where(spot == float(j), high_row, limits_high)
    limit_ref[:, :LANES] = STEP * limits_low
    limit_ref[:, LANES:] = STEP * limits_high

    shape = (owners * ROWS, 3 * 4 * SLOTS)
    target = (iota(shape, 0) // ROWS).astype(F32)
    kind = iota(shape, 0) % ROWS
    place = iota(shape, 1) % (4 * SLOTS)
    group = place // SLOTS
    slim_shape = (SLOTS, shape[1])
    slim = iota(slim_shape, 1) % SLOTS == iota(slim_shape, 0)
    owner_wide = jnp.sum(jnp.where(slim, owner, 0.0), axis=0, keepdims=True)
    rank_wide = jnp.sum(jnp.where(slim, rank, 0.0), axis=0, keepdims=True)
    kind_f = kind.astype(F32)
    hit = (group == 0) & (kind_f == 2.0 * rank_wide)
    hit = hit | ((group == 1) & (kind_f == 2.0 * rank_wide + 1.0))
    hit = hit | ((group == 2) & (kind == 5))
    hit = (hit & (owner_wide == target)) | ((place == 3 * SLOTS) & (kind == 4))
    send = jnp.where(hit, 1.0, 0.0).astype(BF16)
    send_ref[...] = send

    at_f = at.astype(F32)
    base = rank * (LANES // 2)
    meta = jnp.where(at_f == base, col_of - owner * strips_owner + 1.0, 0.0)
    meta = jnp.where(at_f == base + 1.0, band + 1.0, meta)
    message_ref[...] = message_rows(send, column, meta, None).reshape(message_ref.shape)


def message_rows(send, strips_part, meta, partial):
    if partial is None:
        bottom = jnp.zeros((SLOTS, LANES), F32)
    else:
        bottom = jnp.where(iota((SLOTS, LANES), 0) == 0, partial, 0.0)
    stacked = jnp.concatenate([strips_part[:, :LANES], strips_part[:, LANES:], meta, bottom], axis=0)
    return dot(send, split_rows(stacked))


def side_by_side(rows):
    out = rows[0]
    for i, row in enumerate(rows[1:], 1):
        wide = jnp.broadcast_to(row, (ROWS, LANES))
        out = out + pltpu.roll(wide, i * SLOTS, 1)[0:1]
    return out


def slot_scalars(hot, scalar):
    col = jnp.sum(hot * scalar, axis=1, keepdims=True)
    return col, along_lanes(col)


def advance(strips, col, row, grads, column, twin, same, approx_row, total_row, line_tops):
    other = jnp.sum(jnp.where(same > 0.0, row[:, :SLOTS], 0.0), axis=1, keepdims=True)
    full = grads + col[:SLOTS] * column + other * twin
    sources = approx_row + row * total_row
    at = iota((SLOTS, LANES), 1)
    top_grad = jnp.zeros((SLOTS, LANES), F32)
    for t in range(strips):
        value = jnp.sum(line_tops[t * SLOTS : (t + 1) * SLOTS] * sources, axis=1, keepdims=True)
        top_grad = jnp.where(at == t, value, top_grad)
    return full, top_grad


def with_approx(point, top, matrix):
    approx = jnp.sum(matrix * top, axis=1, keepdims=True)
    return jnp.where(iota((SLOTS, STRIP), 1) == 0, approx, point)


def band_partial(point, column, hot):
    dots = jnp.sum(point * column, axis=1, keepdims=True)
    return jnp.sum(hot * dots, axis=0, keepdims=True) / SOUNDS


def twins(strip_match):
    return jnp.where(iota((SLOTS, SLOTS), 0) == iota((SLOTS, SLOTS), 1), 0.0, strip_match)


def first_step_kernel(
    strips,
    owners,
    first_ref,
    column_ref,
    twin_ref,
    grad_ref,
    limit_ref,
    strip_match_ref,
    top_matrix_ref,
    decay_ref,
    weight_ref,
    prepared_ref,
    *rest,
):
    sectors = strips // SEC_STRIPS
    tables = rest[:sectors]
    point_ref, top_ref, message_ref, hot_ref, line_tops_ref = rest[sectors:]
    window = lax.axis_index("tile") // sectors
    sums = weekly([first_ref[t, 1:2, :] for t in range(owners)], sectors)
    returned = scan_back([-s for s in sums], decay_ref[...])
    scalar = pick(returned, window) / SOUNDS
    hot = jnp.concatenate([one_hot_bands(t[0:SLOTS, BAND : BAND + 1]) for t in tables], axis=0)
    hot_ref[...] = hot

    def row(index):
        return side_by_side([t[index : index + 1, :] for t in tables])

    spot_row = row(SPOT_ROW) - 1.0
    on_line = tables[0][0:SLOTS, LINE : LINE + 1] + 1.0 == row(LINE_ROW)
    line_tops = jnp.concatenate(
        [jnp.where(on_line, top_entry(spot_row, t, strips), 0.0) for t in range(strips)], axis=0
    )
    line_tops_ref[...] = line_tops
    column = column_ref[...]
    col, along = slot_scalars(hot, scalar)
    grads, top_grad = advance(
        strips,
        col,
        along,
        grad_ref[...],
        column,
        twin_ref[...],
        twins(strip_match_ref[...]),
        row(APPROX_ROW),
        row(TOTAL_ROW),
        line_tops,
    )
    updated = shrink(-STEP * grads, limit_ref[...])
    top = shrink(-STEP * top_grad, STEP * weight_ref[0:1, :LANES])
    point = with_approx(updated, top, top_matrix_ref[...])
    point_ref[...] = point
    top_ref[...] = top
    partial = band_partial(point, column, hot[:SLOTS])
    is_partial = iota(message_ref.shape, 1) == 4
    message_ref[...] = jnp.where(is_partial, partial.reshape(1, 1, LANES), prepared_ref[...])


def local_grad_kernel(
    strips,
    point_ref,
    high_ref,
    low_ref,
    row_match_ref,
    obs_slot_ref,
    strip_match_ref,
    *rest,
):
    sectors = strips // SEC_STRIPS
    tables = rest[:sectors]
    grad_ref, approx_ref, lead_ref = rest[sectors:]
    values = forward(point_ref[...], high_ref, low_ref)
    chosen = fold(row_match_ref[...], values) - obs_slot_ref[...]
    grad = back_project(chosen, high_ref, low_ref)
    grad_ref[...] = exact_dot(strip_match_ref[...], grad)
    info = tables[0][0:SLOTS, :]
    approx = grad[:, 0:1] * info[:, VALID : VALID + 1]
    approx_ref[...] = jnp.broadcast_to(along_lanes(approx), approx_ref.shape)

    sector = lax.rem(lax.axis_index("tile"), sectors).astype(F32)
    line_row = side_by_side([t[LINE_ROW : LINE_ROW + 1, :] for t in tables])
    spot_row = side_by_side([t[SPOT_ROW : SPOT_ROW + 1, :] for t in tables])
    sector_row = jnp.floor((spot_row - 1.0) / SEC_STRIPS)
    lane = iota((SLOTS, LANES), 1)
    before = jnp.where(lane < iota((SLOTS, LANES), 0), 1.0, 0.0)
    earlier = jnp.where(lane < SLOTS, before, jnp.where(sector_row < sector, 1.0, 0.0))
    on_line = info[:, LINE : LINE + 1] + 1.0 == line_row
    taken = jnp.sum(jnp.where(on_line, earlier, 0.0), axis=1, keepdims=True)
    lead_ref[...] = jnp.broadcast_to(jnp.where(taken > 0.0, 0.0, 1.0), lead_ref.shape)


def second_step_kernel(
    strips,
    owners,
    beta,
    first_ref,
    second_ref,
    column_ref,
    twin_ref,
    grad_ref,
    limit_ref,
    strip_match_ref,
    top_matrix_ref,
    decay_ref,
    weight_ref,
    hot_ref,
    line_tops_ref,
    lead_ref,
    rank_ref,
    send_ref,
    point_ref,
    top_ref,
    high_ref,
    low_ref,
    row_match_ref,
    obs_slot_ref,
    *rest,
):
    sectors = strips // SEC_STRIPS
    tables, rest = rest[:sectors], rest[sectors:]
    approx_refs, rest = rest[:sectors], rest[sectors:]
    message_ref, values_ref = rest
    window = lax.axis_index("tile") // sectors
    combined, _ = background(
        first_ref, [second_ref[t, 4:5, :] for t in range(owners)], decay_ref[...], sectors
    )
    hot = hot_ref[...]
    column = column_ref[...]
    col, along = slot_scalars(hot, pick(combined, window))
    grads, top_grad = advance(
        strips,
        col,
        along,
        grad_ref[...],
        column,
        twin_ref[...],
        twins(strip_match_ref[...]),
        side_by_side([r[0:1, :] for r in approx_refs]),
        side_by_side([t[TOTAL_ROW : TOTAL_ROW + 1, :] for t in tables]),
        line_tops_ref[...],
    )
    old = point_ref[...]
    old_top = top_ref[...]
    updated = shrink(old - STEP * grads, limit_ref[...])
    top = shrink(old_top - STEP * top_grad, STEP * weight_ref[0:1, :LANES])
    point = updated + beta * (updated - old)
    top = top + beta * (top - old_top)
    point = with_approx(point, top, top_matrix_ref[...])
    values = forward(point, high_ref, low_ref)
    values_ref[...] = values
    chosen = fold(row_match_ref[...], values) - obs_slot_ref[...]
    grad = back_project(chosen, high_ref, low_ref)

    partial = band_partial(point, column, hot[:SLOTS])
    info = tables[0][0:SLOTS, :]
    valid = info[:, VALID : VALID + 1]
    top = top * lead_ref[:, 0:1]
    rank = rank_ref[:, 0:1]
    meta = jnp.where(rank == 0.0, pltpu.roll(top, ROWS, 1), pltpu.roll(top, LANES // 2 + ROWS, 1))
    kept = jnp.where(iota((SLOTS, STRIP), 1) == 0, 0.0, point * rank_ref[:, 1:2])
    rows = message_rows(send_ref[...], kept - STEP * (valid * grad), meta, partial)
    message_ref[...] = rows.reshape(message_ref.shape)


def place_kernel(
    strips,
    owners,
    second_ref,
    table_ref,
    values_ref,
    obs_ref,
    band_ref,
    place_ref,
    band_hot_ref,
    scaled_ref,
    differ_ref,
    block_hot_ref,
):
    sectors = strips // SEC_STRIPS
    lines = NLAT // owners
    count = owners * ROWS
    meta = second_ref[:, 5, :]
    wide = (owners, count)
    pair_of = iota(wide, 1) // ROWS == iota(wide, 0)
    kind = iota((1, count), 1) % ROWS
    tall = (count, owners)
    tall_pair = iota(tall, 0) // ROWS == iota(tall, 1)
    tall_kind = iota((count, 1), 0) % ROWS
    strip_rows = []
    band_col = jnp.zeros((count, 1), F32)
    for q in range(2):
        strip = meta[:, q * (LANES // 2) : q * (LANES // 2) + 1]
        band = meta[:, q * (LANES // 2) + 1 : q * (LANES // 2) + 2]
        strip_rows.append(jnp.sum(jnp.where(pair_of, strip, 0.0), axis=0, keepdims=True) - 1.0)
        band_tall = jnp.sum(jnp.where(tall_pair, to_row(band), 0.0), axis=1, keepdims=True)
        band_col = jnp.where(tall_kind // 2 == q, band_tall, band_col)
    band_hot_ref[...] = one_hot_bands(band_col - 1.0)
    scaled_ref[...] = jnp.where(tall_kind < 4, STEP * second_ref[...].reshape(count, LANES), 0.0)

    def line_of(strip):
        return jnp.floor(strip / SEC_STRIPS)

    blocks = lines * WIN
    pair = iota((1, count), 1) // ROWS
    window = pair // sectors
    sector = (pair - window * sectors).astype(F32)
    line_col = (iota((blocks, 1), 0) // WIN).astype(F32)
    window_col = iota((blocks, 1), 0) % WIN
    strip_row = jnp.where(kind < 2, strip_rows[0], strip_rows[1])
    slot_line = line_of(strip_row)
    slot_spot = sector * SEC_STRIPS + strip_row - slot_line * SEC_STRIPS
    base = (window == window_col) & (slot_line == line_col) & (strip_row >= 0.0)
    base = jnp.where(base & (kind < 4), 1.0, 0.0)
    parts = []
    for half in range(2):
        part = jnp.where(kind % 2 == half, base, 0.0)
        for j in range(strips):
            parts.append(jnp.where(slot_spot == float(j), part, 0.0))
    for q in range(2):
        hit = (window == window_col) & (line_of(strip_rows[q]) == line_col) & (strip_rows[q] >= 0.0) & (kind == 5)
        parts.append(jnp.where(hit, 1.0, 0.0))
    place = jnp.concatenate(parts, axis=0).astype(BF16)
    place_ref[...] = jnp.concatenate([place, place, place], axis=1)

    info = table_ref[0:SLOTS, :]
    lane = iota((SLOTS, SLOTS * SOUNDS), 1) // SOUNDS
    slot = iota((SLOTS, SLOTS * SOUNDS), 0)
    row_lane = jnp.sum(
        jnp.where(lane == slot, (info[:, ROW : ROW + 1] + 1.0) * info[:, VALID : VALID + 1], 0.0),
        axis=0,
        keepdims=True,
    )
    per_row = jnp.where(iota((SB_DEV, SLOTS * SOUNDS), 0).astype(F32) + 1.0 == row_lane, 1.0, 0.0)
    differ_ref[...] = fold(per_row, values_ref[...])[:, :SOUNDS] - obs_ref[...]
    block_hot_ref[...] = one_hot_bands(to_col(band_ref[...].astype(F32)))


def finish_kernel(
    strips,
    owners,
    first_ref,
    third_ref,
    place_ref,
    band_hot_ref,
    scaled_ref,
    decay_ref,
    weight_ref,
    differ_ref,
    block_hot_ref,
    out_ref,
    misfit_ref,
):
    sectors = strips // SEC_STRIPS
    blocks = NLAT // owners * WIN
    count = owners * ROWS
    window = lax.axis_index("tile") // sectors
    combined, carried = background(
        first_ref, [third_ref[t, 4:5, :] for t in range(owners)], decay_ref[...], sectors
    )
    spread = jnp.concatenate(
        [jnp.broadcast_to(row, (sectors * ROWS, NBANDS)) for row in combined], axis=0
    )
    scalars = jnp.sum(band_hot_ref[...] * spread, axis=1, keepdims=True)
    rows = third_ref[...].reshape(count, LANES) - scalars * scaled_ref[...]
    placed = dot(place_ref[...], split_rows(rows))
    offset = jnp.sum(block_hot_ref[...] * pick(carried, window), axis=1, keepdims=True)
    misfit_ref[...] = differ_ref[...] + offset

    lane = iota((1, LANES), 1)
    for j in range(strips):
        start = (strips + j) * LANES
        values = placed[(strips + j) * blocks : (strips + j + 1) * blocks]
        out_ref[:, start : start + LANES] = shrink(values, STEP * weight_ref[0:1, start : start + LANES])

    low = [placed[j * blocks : (j + 1) * blocks] for j in range(strips)]
    tops = [placed[(2 * strips + q) * blocks : (2 * strips + q + 1) * blocks] for q in range(2)]
    top = pltpu.roll(tops[0], LANES - ROWS, 1) + pltpu.roll(tops[1], LANES // 2 - ROWS, 1)
    made = [jnp.zeros((blocks, LANES), F32) for _ in range(strips)]
    for t in range(strips):
        value = jnp.zeros((blocks, 1), F32)
        for j in range(strips):
            entry = top_value(j, t, strips)
            if entry:
                value = value + entry * low[j][:, 0:1]
        made[0] = jnp.where(lane == t, value + top, made[0])
    m = 1
    while m < LANES:
        for j in range(strips):
            start = strips * m + j * m
            block = start // LANES
            shift = (start % LANES - m) % LANES
            moved = pltpu.roll(low[j], shift, 1) if shift else low[j]
            inside = (lane >= start % LANES) & (lane < start % LANES + m)
            made[block] = jnp.where(inside, moved, made[block])
        m *= 2
    for block in range(strips):
        start = block * LANES
        out_ref[:, start : start + LANES] = shrink(made[block], STEP * weight_ref[0:1, start : start + LANES])


def top_value(spot, index, strips):
    if index == 0:
        return math.sqrt(1.0 / strips)
    m = 1 << (index.bit_length() - 1)
    span = strips // m
    within = spot - (index - m) * span
    if within < 0 or within >= span:
        return 0.0
    return math.sqrt(m / strips) * (1.0 if within < span // 2 else -1.0)


def call(kernel, outs, *operands, **kwargs):
    return pl.pallas_call(
        kernel,
        out_shape=[jax.ShapeDtypeStruct(shape, dtype) for shape, dtype in outs],
        compiler_params=pltpu.CompilerParams(vmem_limit_bytes=40 * 1024 * 1024),
        **kwargs,
    )(*operands)


def body(
    observations,
    jacobian,
    block_row,
    block_col,
    block_count,
    block_band,
    carry_decay,
    sparsity_weight,
):
    owners = lax.axis_size("tile")
    sectors = owners // WIN
    strips = sectors * SEC_STRIPS
    lines = NLAT // owners
    betas = momentum_weights(ITERS)
    arguments = [
        block_band.reshape(1, SB_DEV),
        observations,
        block_row.reshape(1, SLOTS),
        block_col.reshape(1, SLOTS),
        carry_decay.reshape(1, NBANDS),
        sparsity_weight.reshape(1, -1),
        jacobian.reshape(SLOTS * SOUNDS, STRIP),
    ]
    message = ((owners, ROWS, LANES), F32)
    narrow = ((SLOTS, LANES), F32)
    strip_rows = ((SLOTS, STRIP), F32)
    table_rows = ((TABLE_ROWS, LANES), F32)

    def trade(values):
        return lax.all_to_all(values, "tile", 0, 0, tiled=True)

    def with_sectors(values):
        found = [values]
        for shift in range(1, sectors):
            pairs = [
                (d, d // sectors * sectors + (d + shift) % sectors) for d in range(owners)
            ]
            found.append(lax.ppermute(values, "tile", pairs))
        return found

    arguments = [pltpu.with_memory_space_constraint(a, pltpu.HBM) for a in arguments]
    bands, observed, rows, cols, decay, weight, flat, first = call(
        start_kernel,
        [(a.shape, a.dtype) for a in arguments] + [((owners, 2, LANES), F32)],
        *arguments,
        in_specs=[pl.BlockSpec(memory_space=pltpu.HBM)] * len(arguments),
        out_specs=[pl.BlockSpec(memory_space=pltpu.VMEM)] * (len(arguments) + 1),
        scratch_shapes=[pltpu.SemaphoreType.DMA((len(arguments) - 1 + PIECES,))],
    )
    first = trade(first)
    high, low, column, obs_grad, obs_slot, table = call(
        functools.partial(transform_kernel, strips),
        [
            ((SLOTS * SOUNDS, STRIP), BF16),
            ((SLOTS * SOUNDS, STRIP), BF16),
            strip_rows,
            strip_rows,
            narrow,
            table_rows,
        ],
        flat,
        observed,
        rows,
        cols,
        block_count,
        bands,
        in_specs=[
            pl.BlockSpec(memory_space=pltpu.SMEM if i == 4 else pltpu.VMEM) for i in range(6)
        ],
    )
    tables = with_sectors(table)
    twin, start_grad, row_match, limit, send, strip_match, top_matrix, prepared, rank = call(
        functools.partial(prepare_kernel, strips, owners),
        [
            strip_rows,
            strip_rows,
            ((SLOTS, SLOTS * SOUNDS), F32),
            strip_rows,
            ((owners * ROWS, 3 * 4 * SLOTS), BF16),
            ((SLOTS, SLOTS), F32),
            narrow,
            message,
            narrow,
        ],
        column,
        obs_grad,
        table,
        weight,
    )
    point, top, second, hot, line_tops = call(
        functools.partial(first_step_kernel, strips, owners),
        [
            strip_rows,
            narrow,
            message,
            ((sectors * SLOTS, NBANDS), F32),
            ((strips * SLOTS, LANES), F32),
        ],
        first,
        column,
        twin,
        start_grad,
        limit,
        strip_match,
        top_matrix,
        decay,
        weight,
        prepared,
        *tables,
    )
    second = trade(second)
    grad, approx, lead = call(
        functools.partial(local_grad_kernel, strips),
        [strip_rows, ((ROWS, LANES), F32), narrow],
        point,
        high,
        low,
        row_match,
        obs_slot,
        strip_match,
        *tables,
    )
    third, values = call(
        functools.partial(second_step_kernel, strips, owners, betas[1]),
        [message, ((1, SLOTS * SOUNDS), F32)],
        first,
        second,
        column,
        twin,
        grad,
        limit,
        strip_match,
        top_matrix,
        decay,
        weight,
        hot,
        line_tops,
        lead,
        rank,
        send,
        point,
        top,
        high,
        low,
        row_match,
        obs_slot,
        *tables,
        *with_sectors(approx),
    )
    third = trade(third)
    placed_rows = (2 * strips + 2) * lines * WIN
    place, band_hot, scaled, differ, block_hot = call(
        functools.partial(place_kernel, strips, owners),
        [
            ((placed_rows, 3 * owners * ROWS), BF16),
            ((owners * ROWS, NBANDS), F32),
            ((owners * ROWS, LANES), F32),
            ((SB_DEV, SOUNDS), F32),
            ((SB_DEV, NBANDS), F32),
        ],
        second,
        table,
        values,
        observed,
        bands,
    )
    coeffs, misfit = call(
        functools.partial(finish_kernel, strips, owners),
        [((lines * WIN, strips * STRIP), F32), ((SB_DEV, SOUNDS), F32)],
        first,
        third,
        place,
        band_hot,
        scaled,
        decay,
        weight,
        differ,
        block_hot,
    )
    return (coeffs.reshape(lines, WIN, strips * STRIP), misfit)


def solution(mesh):
    return jax.shard_map(
        body,
        mesh=mesh,
        in_specs=(
            P(("ens", "tile"), None),
            P("tile", None, None),
            P("tile"),
            P("tile"),
            P("tile"),
            P("tile"),
            P(),
            P(),
        ),
        out_specs=(P(("ens", "tile"), None, None), P(("ens", "tile"), None)),
        check_vma=False,
    )
```

```python
import functools
import math

import jax
import jax.numpy as jnp
from jax import lax
from jax.experimental import pallas as pl
from jax.experimental.pallas import tpu as pltpu
from jax.sharding import PartitionSpec as P

WIN = 8
NLAT = 64
SEC_STRIPS = 2
STRIP = 256
SOUNDS = 64
SB_DEV = 32
NBANDS = 128
ITERS = 3
SLOTS = 16
LANES = 128
ROWS = 8
STEP = 0.2

F32 = jnp.float32
BF16 = jnp.bfloat16
HIGHEST = lax.Precision.HIGHEST

LINE, SPOT, BAND, TOTAL, ROW, COL, VALID = range(7)
LINE_ROW, SPOT_ROW, TOTAL_ROW, APPROX_ROW = range(SLOTS, SLOTS + 4)
TABLE_ROWS = SLOTS + ROWS


def momentum_weights(total_steps):
    weights = []
    current = 1.0
    for _ in range(total_steps):
        following = (1.0 + math.sqrt(1.0 + 4.0 * current * current)) / 2.0
        weights.append((current - 1.0) / following)
        current = following
    return weights


def iota(shape, axis):
    return lax.broadcasted_iota(jnp.int32, shape, axis)


def shrink(values, limit):
    return values - jnp.minimum(jnp.maximum(values, -limit), limit)


def to_col(row):
    n = row.shape[1]
    eye = iota((n, n), 0) == iota((n, n), 1)
    return jnp.sum(jnp.where(eye, row, 0.0), axis=1, keepdims=True)


def to_row(col):
    n = col.shape[0]
    eye = iota((n, n), 0) == iota((n, n), 1)
    return jnp.sum(jnp.where(eye, col, 0.0), axis=0, keepdims=True)


def exact_dot(left, right):
    return jnp.dot(left, right, precision=HIGHEST, preferred_element_type=F32)


def dot(left, right):
    return jnp.dot(left, right, preferred_element_type=F32)


def dot_nt(left, right):
    return lax.dot_general(left, right, (((1,), (1,)), ((), ())), preferred_element_type=F32)


def split(values):
    high = values.astype(BF16)
    return high, (values - high.astype(F32)).astype(BF16)


def split_rows(values):
    high = values.astype(BF16)
    rest = values - high.astype(F32)
    middle = rest.astype(BF16)
    return jnp.concatenate([high, middle, (rest - middle.astype(F32)).astype(BF16)], axis=0)


def haar_signs():
    coef = iota((1, STRIP), 1).astype(F32)
    level = jnp.zeros((1, STRIP), F32) + 1.0
    m = 2
    while m < STRIP:
        level = jnp.where(coef >= m, float(m), level)
        m *= 2
    first = coef == 0.0
    shift = jnp.where(first, 0.0, coef - level)
    half = jnp.where(first, 2.0, 0.5)
    within = iota((STRIP, STRIP), 0).astype(F32) * (level / STRIP) - shift
    inside = (within >= 0.0) & (within < 1.0)
    return jnp.where(inside, jnp.where(within < half, 1.0, -1.0), 0.0).astype(BF16)


def haar_scales():
    coef = iota((1, STRIP), 1)
    out = jnp.full((1, STRIP), math.sqrt(1.0 / STRIP), F32)
    m = 1
    while m < STRIP:
        out = jnp.where((coef >= m) & (coef < 2 * m), math.sqrt(m / STRIP), out)
        m *= 2
    return out


def top_entry(spot, index, strips):
    if index == 0:
        return jnp.full(spot.shape, math.sqrt(1.0 / strips), F32)
    m = 1 << (index.bit_length() - 1)
    span = strips // m
    start = float((index - m) * span)
    half = start + span / 2
    end = start + span
    scale = math.sqrt(m / strips)
    positive = (spot >= start) & (spot < half)
    negative = (spot >= half) & (spot < end)
    return jnp.where(positive, scale, jnp.where(negative, -scale, 0.0))


def weekly(rows, sectors):
    return [sum(rows[w * sectors + 1 : (w + 1) * sectors], rows[w * sectors]) for w in range(WIN)]


def scan_back(totals, decay):
    running = totals[WIN - 1]
    out = [running]
    for w in range(WIN - 2, -1, -1):
        running = running * decay + totals[w]
        out.insert(0, running)
    return out


def scan_ahead(totals, decay):
    running = totals[0]
    out = [running]
    for w in range(1, WIN):
        running = running * decay + totals[w]
        out.append(running)
    return out


def pick(rows, index):
    out = rows[0]
    for w in range(1, len(rows)):
        out = jnp.where(index == w, rows[w], out)
    return out


def background(first, partial_rows, decay, sectors):
    counts = weekly([first[t, 0:1, :] for t in range(WIN * sectors)], sectors)
    sums = weekly([first[t, 1:2, :] for t in range(WIN * sectors)], sectors)
    partials = weekly(partial_rows, sectors)
    carried = scan_ahead(partials, decay)
    back = [
        SOUNDS * partials[w] + (SOUNDS * counts[w]) * carried[w] - sums[w] for w in range(WIN)
    ]
    returned = scan_back(back, decay)
    return [carried[w] + returned[w] / SOUNDS for w in range(WIN)], carried


def one_hot_bands(band_col):
    return jnp.where(band_col == iota((band_col.shape[0], NBANDS), 1).astype(F32), 1.0, 0.0)


def own_block_mask(rows):
    return iota((rows, SLOTS * SOUNDS), 0) == iota((rows, SLOTS * SOUNDS), 1) // SOUNDS


def back_project(chosen, high_ref, low_ref):
    wide = jnp.concatenate([chosen] * (SLOTS * SOUNDS // LANES), axis=1)
    spread = jnp.where(own_block_mask(SLOTS), wide, 0.0)
    high, low = split(spread)
    both = dot(jnp.concatenate([high, low], axis=0), high_ref[...])
    return both[:SLOTS] + both[SLOTS:] + dot(high, low_ref[...])


def forward(point, high_ref, low_ref):
    high, low = split(point)
    both = dot_nt(jnp.concatenate([high, low], axis=0), high_ref[...])
    full = both[:SLOTS] + both[SLOTS:] + dot_nt(high, low_ref[...])
    return jnp.sum(jnp.where(own_block_mask(SLOTS), full, 0.0), axis=0, keepdims=True)


def fold(weights, values):
    product = weights * values
    total = product[:, :LANES]
    for start in range(LANES, SLOTS * SOUNDS, LANES):
        total = total + product[:, start : start + LANES]
    return total + pltpu.roll(total, SOUNDS, 1)


def start_kernel(*refs):
    fetched = (len(refs) - 3) // 2
    sources, targets = refs[:fetched], refs[fetched : 2 * fetched]
    out_ref, made_ref, sems = refs[2 * fetched :]
    copies = [
        pltpu.make_async_copy(source, target, sems.at[i])
        for i, (source, target) in enumerate(zip(sources, targets))
    ]
    for copy in copies:
        copy.start()
    copies[0].wait()
    copies[1].wait()
    band_ref, obs_ref = targets[:2]
    hot = one_hot_bands(to_col(band_ref[...].astype(F32)))
    sums = jnp.sum(obs_ref[...], axis=1, keepdims=True)
    counted = jnp.sum(hot, axis=0, keepdims=True)
    summed = jnp.sum(hot * sums, axis=0, keepdims=True)
    for t in range(made_ref.shape[0]):
        made_ref[t, 0:1, :] = counted
        made_ref[t, 1:2, :] = summed
    sent = pltpu.make_async_copy(made_ref, out_ref, sems.at[fetched])
    sent.start()
    for copy in copies[2:]:
        copy.wait()
    sent.wait()


def along_lanes(col):
    n = col.shape[0]
    here = iota((n, LANES), 0) == iota((n, LANES), 1)
    return jnp.sum(jnp.where(here, col, 0.0), axis=0, keepdims=True)


def transform_kernel(
    strips,
    jac_ref,
    obs_ref,
    row_ref,
    col_ref,
    count_ref,
    band_ref,
    high_ref,
    low_ref,
    column_ref,
    obs_grad_ref,
    obs_slot_ref,
    table_ref,
):
    sectors = strips // SEC_STRIPS
    sector = lax.rem(lax.axis_index("tile"), sectors).astype(F32)
    signs = haar_signs()
    scales = haar_scales()
    chunk = STRIP
    per = chunk // SOUNDS
    columns = []
    for start in range(0, SLOTS * SOUNDS, chunk):
        high, low = split(jac_ref[start : start + chunk, :])
        changed = (dot(high, signs) + dot(low, signs)) * scales
        high, low = split(changed)
        high_ref[start : start + chunk, :] = high
        low_ref[start : start + chunk, :] = low
        columns.append(jnp.sum(changed.reshape(per, SOUNDS, STRIP), axis=1))
    column = jnp.concatenate(columns, axis=0)

    row_of = to_col(row_ref[...].astype(F32))
    col_of = to_col(col_ref[...].astype(F32))
    valid = jnp.where(iota((SLOTS, 1), 0) < count_ref[0], 1.0, 0.0)
    line = jnp.floor(col_of / SEC_STRIPS)
    spot = sector * SEC_STRIPS + (col_of - line * SEC_STRIPS)
    row_hot = jnp.where(row_of == iota((SLOTS, SB_DEV), 1).astype(F32), 1.0, 0.0)
    band_row = band_ref[...].astype(F32)
    band = jnp.sum(row_hot * band_row, axis=1, keepdims=True)
    band = jnp.where(valid > 0.0, band, -1.0)
    observed = obs_ref[...]
    obs_slot = exact_dot(row_hot, jnp.concatenate([observed, observed], axis=1))
    obs_slot_ref[...] = obs_slot
    obs_grad = back_project(obs_slot, high_ref, low_ref)
    obs_grad_ref[...] = obs_grad
    column = column * valid
    column_ref[...] = column

    at = iota((SLOTS, LANES), 1)
    info = jnp.zeros((SLOTS, LANES), F32)
    for place, values in (
        (LINE, line),
        (SPOT, spot),
        (BAND, band),
        (TOTAL, column[:, 0:1]),
        (ROW, row_of),
        (COL, col_of),
        (VALID, valid),
    ):
        info = jnp.where(at == place, values, info)
    table_ref[0:SLOTS, :] = info
    table_ref[SLOTS:TABLE_ROWS, :] = jnp.zeros((TABLE_ROWS - SLOTS, LANES), F32)
    table_ref[LINE_ROW : LINE_ROW + 1, :] = along_lanes(line + 1.0)
    table_ref[SPOT_ROW : SPOT_ROW + 1, :] = along_lanes(spot + 1.0)
    table_ref[TOTAL_ROW : TOTAL_ROW + 1, :] = along_lanes(column[:, 0:1])
    table_ref[APPROX_ROW : APPROX_ROW + 1, :] = along_lanes(-obs_grad[:, 0:1] * valid)


def prepare_kernel(
    strips,
    owners,
    column_ref,
    obs_grad_ref,
    table_ref,
    weight_ref,
    twin_ref,
    start_grad_ref,
    row_match_ref,
    limit_ref,
    send_ref,
    strip_match_ref,
    top_matrix_ref,
    message_ref,
    rank_ref,
):
    strips_owner = NLAT * SEC_STRIPS // owners
    column = column_ref[...]
    info = table_ref[0:SLOTS, :]
    spot = info[:, SPOT : SPOT + 1]
    band = info[:, BAND : BAND + 1]
    row_of = info[:, ROW : ROW + 1]
    col_of = info[:, COL : COL + 1]
    valid = info[:, VALID : VALID + 1]
    col_row = to_row(col_of)
    valid_row = to_row(valid)

    lane = iota((SLOTS, SLOTS * SOUNDS), 1) // SOUNDS
    slot = iota((SLOTS, SLOTS * SOUNDS), 0)
    row_lane = jnp.sum(
        jnp.where(lane == slot, (row_of + 1.0) * valid - 1.0, 0.0), axis=0, keepdims=True
    )
    row_match_ref[...] = jnp.where(row_of == row_lane, 1.0, 0.0)

    same = jnp.where(col_of == col_row, 1.0, 0.0)
    before = jnp.where(iota((SLOTS, SLOTS), 1) < iota((SLOTS, SLOTS), 0), 1.0, 0.0)
    other = jnp.where(iota((SLOTS, SLOTS), 1) != iota((SLOTS, SLOTS), 0), same, 0.0)
    strip_match_ref[...] = same * valid_row
    start_grad_ref[...] = -exact_dot(same * valid_row, obs_grad_ref[...])
    twin_ref[...] = exact_dot(other, column)
    first = jnp.where(jnp.sum(same * before, axis=1, keepdims=True) > 0.0, 0.0, 1.0)
    owner = jnp.floor(col_of / strips_owner)
    owner_row = jnp.floor(col_row / strips_owner)
    rank = jnp.sum(jnp.where(owner == owner_row, before, 0.0), axis=1, keepdims=True)

    at = iota((SLOTS, LANES), 1)
    rank_ref[...] = jnp.where(at == 0, rank, jnp.where(at == 1, first, 0.0))
    matrix = jnp.zeros((SLOTS, LANES), F32)
    for t in range(strips):
        matrix = jnp.where(at == t, top_entry(spot, t, strips), matrix)
    top_matrix_ref[...] = matrix

    local = iota((1, LANES), 1)
    limits_low = jnp.zeros((SLOTS, LANES), F32)
    limits_high = jnp.zeros((SLOTS, LANES), F32)
    for j in range(strips):
        low_row = jnp.zeros((1, LANES), F32)
        m = 1
        while m < LANES:
            start = strips * m + j * m
            block = weight_ref[0:1, start // LANES * LANES : start // LANES * LANES + LANES]
            shift = (m - start % LANES) % LANES
            moved = pltpu.roll(jnp.broadcast_to(block, (ROWS, LANES)), shift, 1)[0:1] if shift else block
            low_row = jnp.where((local >= m) & (local < 2 * m), moved, low_row)
            m *= 2
        high_row = weight_ref[0:1, (strips + j) * LANES : (strips + j + 1) * LANES]
        limits_low = jnp.where(spot == float(j), low_row, limits_low)
        limits_high = jnp.where(spot == float(j), high_row, limits_high)
    limit_ref[:, :LANES] = STEP * limits_low
    limit_ref[:, LANES:] = STEP * limits_high

    shape = (owners * ROWS, 3 * 4 * SLOTS)
    target = (iota(shape, 0) // ROWS).astype(F32)
    kind = iota(shape, 0) % ROWS
    place = iota(shape, 1) % (4 * SLOTS)
    group = place // SLOTS
    slim_shape = (SLOTS, shape[1])
    slim = iota(slim_shape, 1) % SLOTS == iota(slim_shape, 0)
    owner_wide = jnp.sum(jnp.where(slim, owner, 0.0), axis=0, keepdims=True)
    rank_wide = jnp.sum(jnp.where(slim, rank, 0.0), axis=0, keepdims=True)
    kind_f = kind.astype(F32)
    hit = (group == 0) & (kind_f == 2.0 * rank_wide)
    hit = hit | ((group == 1) & (kind_f == 2.0 * rank_wide + 1.0))
    hit = hit | ((group == 2) & (kind == 5))
    hit = (hit & (owner_wide == target)) | ((place == 3 * SLOTS) & (kind == 4))
    send = jnp.where(hit, 1.0, 0.0).astype(BF16)
    send_ref[...] = send

    at_f = at.astype(F32)
    base = rank * (LANES // 2)
    meta = jnp.where(at_f == base, col_of - owner * strips_owner + 1.0, 0.0)
    meta = jnp.where(at_f == base + 1.0, band + 1.0, meta)
    message_ref[...] = message_rows(send, column, meta, None).reshape(message_ref.shape)


def message_rows(send, strips_part, meta, partial):
    if partial is None:
        bottom = jnp.zeros((SLOTS, LANES), F32)
    else:
        bottom = jnp.where(iota((SLOTS, LANES), 0) == 0, partial, 0.0)
    stacked = jnp.concatenate([strips_part[:, :LANES], strips_part[:, LANES:], meta, bottom], axis=0)
    return dot(send, split_rows(stacked))


def side_by_side(rows):
    out = rows[0]
    for i, row in enumerate(rows[1:], 1):
        wide = jnp.broadcast_to(row, (ROWS, LANES))
        out = out + pltpu.roll(wide, i * SLOTS, 1)[0:1]
    return out


def slot_scalars(hot, scalar):
    col = jnp.sum(hot * scalar, axis=1, keepdims=True)
    return col, along_lanes(col)


def advance(strips, col, row, grads, column, twin, same, approx_row, total_row, line_tops):
    other = jnp.sum(jnp.where(same > 0.0, row[:, :SLOTS], 0.0), axis=1, keepdims=True)
    full = grads + col[:SLOTS] * column + other * twin
    sources = approx_row + row * total_row
    at = iota((SLOTS, LANES), 1)
    top_grad = jnp.zeros((SLOTS, LANES), F32)
    for t in range(strips):
        value = jnp.sum(line_tops[t * SLOTS : (t + 1) * SLOTS] * sources, axis=1, keepdims=True)
        top_grad = jnp.where(at == t, value, top_grad)
    return full, top_grad


def with_approx(point, top, matrix):
    approx = jnp.sum(matrix * top, axis=1, keepdims=True)
    return jnp.where(iota((SLOTS, STRIP), 1) == 0, approx, point)


def band_partial(point, column, hot):
    dots = jnp.sum(point * column, axis=1, keepdims=True)
    return jnp.sum(hot * dots, axis=0, keepdims=True) / SOUNDS


def twins(strip_match):
    return jnp.where(iota((SLOTS, SLOTS), 0) == iota((SLOTS, SLOTS), 1), 0.0, strip_match)


def matched(match, grads):
    return dot(jnp.concatenate([match] * 3, axis=1).astype(BF16), split_rows(grads))


def first_step_kernel(
    strips,
    owners,
    first_ref,
    column_ref,
    twin_ref,
    grad_ref,
    limit_ref,
    strip_match_ref,
    top_matrix_ref,
    decay_ref,
    weight_ref,
    prepared_ref,
    high_ref,
    low_ref,
    row_match_ref,
    obs_slot_ref,
    *rest,
):
    sectors = strips // SEC_STRIPS
    tables = rest[:sectors]
    point_ref, top_ref, message_ref, hot_ref, line_tops_ref, grad_out_ref, lead_ref = rest[sectors:]
    my_index = lax.axis_index("tile")
    window = my_index // sectors
    sums = weekly([first_ref[t, 1:2, :] for t in range(owners)], sectors)
    returned = scan_back([-s for s in sums], decay_ref[...])
    scalar = pick(returned, window) / SOUNDS
    hot = jnp.concatenate([one_hot_bands(t[0:SLOTS, BAND : BAND + 1]) for t in tables], axis=0)
    hot_ref[...] = hot

    def row(index):
        return side_by_side([t[index : index + 1, :] for t in tables])

    spot_row = row(SPOT_ROW) - 1.0
    on_line = tables[0][0:SLOTS, LINE : LINE + 1] + 1.0 == row(LINE_ROW)
    line_tops = jnp.concatenate(
        [jnp.where(on_line, top_entry(spot_row, t, strips), 0.0) for t in range(strips)], axis=0
    )
    line_tops_ref[...] = line_tops
    column = column_ref[...]
    col, along = slot_scalars(hot, scalar)
    grads, top_grad = advance(
        strips,
        col,
        along,
        grad_ref[...],
        column,
        twin_ref[...],
        twins(strip_match_ref[...]),
        row(APPROX_ROW),
        row(TOTAL_ROW),
        line_tops,
    )
    updated = shrink(-STEP * grads, limit_ref[...])
    top = shrink(-STEP * top_grad, STEP * weight_ref[0:1, :LANES])
    point = with_approx(updated, top, top_matrix_ref[...])
    point_ref[...] = point
    top_ref[...] = top
    partial = band_partial(point, column, hot[:SLOTS])
    values = forward(point, high_ref, low_ref)
    chosen = fold(row_match_ref[...], values) - obs_slot_ref[...]
    grad = back_project(chosen, high_ref, low_ref)
    grad_out_ref[...] = matched(strip_match_ref[...], grad)
    info = tables[0][0:SLOTS, :]
    approx = along_lanes(grad[:, 0:1] * info[:, VALID : VALID + 1])
    kind = iota(message_ref.shape, 1)
    message_ref[...] = jnp.where(
        kind == 4,
        partial.reshape(1, 1, LANES),
        jnp.where(kind == 6, approx.reshape(1, 1, LANES), prepared_ref[...]),
    )

    sector = lax.rem(my_index, sectors).astype(F32)
    sector_row = jnp.floor(spot_row / SEC_STRIPS)
    lane = iota((SLOTS, LANES), 1)
    before = jnp.where(lane < iota((SLOTS, LANES), 0), 1.0, 0.0)
    earlier = jnp.where(lane < SLOTS, before, jnp.where(sector_row < sector, 1.0, 0.0))
    taken = jnp.sum(jnp.where(on_line, earlier, 0.0), axis=1, keepdims=True)
    lead_ref[...] = jnp.broadcast_to(jnp.where(taken > 0.0, 0.0, 1.0), lead_ref.shape)


def second_step_kernel(
    strips,
    owners,
    beta,
    first_ref,
    second_ref,
    column_ref,
    twin_ref,
    grad_ref,
    limit_ref,
    strip_match_ref,
    top_matrix_ref,
    decay_ref,
    weight_ref,
    hot_ref,
    line_tops_ref,
    lead_ref,
    rank_ref,
    send_ref,
    point_ref,
    top_ref,
    high_ref,
    low_ref,
    row_match_ref,
    obs_slot_ref,
    *rest,
):
    sectors = strips // SEC_STRIPS
    tables, rest = rest[:sectors], rest[sectors:]
    message_ref, values_ref = rest
    my_index = lax.axis_index("tile")
    window = my_index // sectors
    sector = lax.rem(my_index, sectors)
    approx_rows = []
    for shift in range(sectors):
        pair = window * sectors + lax.rem(sector + (sectors - shift), sectors)
        approx_rows.append(second_ref[pair, 6:7, :])
    combined, _ = background(
        first_ref, [second_ref[t, 4:5, :] for t in range(owners)], decay_ref[...], sectors
    )
    hot = hot_ref[...]
    column = column_ref[...]
    col, along = slot_scalars(hot, pick(combined, window))
    grads, top_grad = advance(
        strips,
        col,
        along,
        grad_ref[...],
        column,
        twin_ref[...],
        twins(strip_match_ref[...]),
        side_by_side(approx_rows),
        side_by_side([t[TOTAL_ROW : TOTAL_ROW + 1, :] for t in tables]),
        line_tops_ref[...],
    )
    old = point_ref[...]
    old_top = top_ref[...]
    updated = shrink(old - STEP * grads, limit_ref[...])
    top = shrink(old_top - STEP * top_grad, STEP * weight_ref[0:1, :LANES])
    point = updated + beta * (updated - old)
    top = top + beta * (top - old_top)
    point = with_approx(point, top, top_matrix_ref[...])
    values = forward(point, high_ref, low_ref)
    values_ref[...] = values
    chosen = fold(row_match_ref[...], values) - obs_slot_ref[...]
    grad = back_project(chosen, high_ref, low_ref)

    partial = band_partial(point, column, hot[:SLOTS])
    info = tables[0][0:SLOTS, :]
    valid = info[:, VALID : VALID + 1]
    top = top * lead_ref[:, 0:1]
    rank = rank_ref[:, 0:1]
    meta = jnp.where(rank == 0.0, pltpu.roll(top, ROWS, 1), pltpu.roll(top, LANES // 2 + ROWS, 1))
    kept = jnp.where(iota((SLOTS, STRIP), 1) == 0, 0.0, point * rank_ref[:, 1:2])
    rows = message_rows(send_ref[...], kept - STEP * (valid * grad), meta, partial)
    message_ref[...] = rows.reshape(message_ref.shape)


def placing(strips, owners, second_ref, table_ref, values_ref, obs_ref, band_ref):
    sectors = strips // SEC_STRIPS
    lines = NLAT // owners
    count = owners * ROWS
    meta = second_ref[:, 5, :]
    wide = (owners, count)
    pair_of = iota(wide, 1) // ROWS == iota(wide, 0)
    kind = iota((1, count), 1) % ROWS
    tall = (count, owners)
    tall_pair = iota(tall, 0) // ROWS == iota(tall, 1)
    tall_kind = iota((count, 1), 0) % ROWS
    strip_rows = []
    band_col = jnp.zeros((count, 1), F32)
    for q in range(2):
        strip = meta[:, q * (LANES // 2) : q * (LANES // 2) + 1]
        band = meta[:, q * (LANES // 2) + 1 : q * (LANES // 2) + 2]
        strip_rows.append(jnp.sum(jnp.where(pair_of, strip, 0.0), axis=0, keepdims=True) - 1.0)
        band_tall = jnp.sum(jnp.where(tall_pair, to_row(band), 0.0), axis=1, keepdims=True)
        band_col = jnp.where(tall_kind // 2 == q, band_tall, band_col)
    band_hot = one_hot_bands(band_col - 1.0)
    scaled = jnp.where(tall_kind < 4, STEP * second_ref[...].reshape(count, LANES), 0.0)

    def line_of(strip):
        return jnp.floor(strip / SEC_STRIPS)

    blocks = lines * WIN
    pair = iota((1, count), 1) // ROWS
    window = pair // sectors
    sector = (pair - window * sectors).astype(F32)
    line_col = (iota((blocks, 1), 0) // WIN).astype(F32)
    window_col = iota((blocks, 1), 0) % WIN
    strip_row = jnp.where(kind < 2, strip_rows[0], strip_rows[1])
    slot_line = line_of(strip_row)
    slot_spot = sector * SEC_STRIPS + strip_row - slot_line * SEC_STRIPS
    base = (window == window_col) & (slot_line == line_col) & (strip_row >= 0.0)
    base = jnp.where(base & (kind < 4), 1.0, 0.0)
    parts = []
    for half in range(2):
        part = jnp.where(kind % 2 == half, base, 0.0)
        for j in range(strips):
            parts.append(jnp.where(slot_spot == float(j), part, 0.0))
    for q in range(2):
        hit = (window == window_col) & (line_of(strip_rows[q]) == line_col) & (strip_rows[q] >= 0.0) & (kind == 5)
        parts.append(jnp.where(hit, 1.0, 0.0))
    place = jnp.concatenate(parts, axis=0).astype(BF16)
    place = jnp.concatenate([place, place, place], axis=1)

    info = table_ref[0:SLOTS, :]
    lane = iota((SLOTS, SLOTS * SOUNDS), 1) // SOUNDS
    slot = iota((SLOTS, SLOTS * SOUNDS), 0)
    row_lane = jnp.sum(
        jnp.where(lane == slot, (info[:, ROW : ROW + 1] + 1.0) * info[:, VALID : VALID + 1], 0.0),
        axis=0,
        keepdims=True,
    )
    per_row = jnp.where(iota((SB_DEV, SLOTS * SOUNDS), 0).astype(F32) + 1.0 == row_lane, 1.0, 0.0)
    differ = fold(per_row, values_ref[...])[:, :SOUNDS] - obs_ref[...]
    block_hot = one_hot_bands(to_col(band_ref[...].astype(F32)))
    return place, band_hot, scaled, differ, block_hot


def finish_kernel(
    strips,
    owners,
    first_ref,
    third_ref,
    second_ref,
    table_ref,
    values_ref,
    obs_ref,
    band_ref,
    decay_ref,
    weight_ref,
    out_ref,
    misfit_ref,
):
    sectors = strips // SEC_STRIPS
    blocks = NLAT // owners * WIN
    count = owners * ROWS
    window = lax.axis_index("tile") // sectors
    place, band_hot, scaled, differ, block_hot = placing(
        strips, owners, second_ref, table_ref, values_ref, obs_ref, band_ref
    )
    combined, carried = background(
        first_ref, [third_ref[t, 4:5, :] for t in range(owners)], decay_ref[...], sectors
    )
    spread = jnp.concatenate(
        [jnp.broadcast_to(row, (sectors * ROWS, NBANDS)) for row in combined], axis=0
    )
    scalars = jnp.sum(band_hot * spread, axis=1, keepdims=True)
    rows = third_ref[...].reshape(count, LANES) - scalars * scaled
    placed = dot(place, split_rows(rows))
    offset = jnp.sum(block_hot * pick(carried, window), axis=1, keepdims=True)
    misfit_ref[...] = differ + offset

    lane = iota((1, LANES), 1)
    for j in range(strips):
        start = (strips + j) * LANES
        values = placed[(strips + j) * blocks : (strips + j + 1) * blocks]
        out_ref[:, start : start + LANES] = shrink(values, STEP * weight_ref[0:1, start : start + LANES])

    low = [placed[j * blocks : (j + 1) * blocks] for j in range(strips)]
    tops = [placed[(2 * strips + q) * blocks : (2 * strips + q + 1) * blocks] for q in range(2)]
    top = pltpu.roll(tops[0], LANES - ROWS, 1) + pltpu.roll(tops[1], LANES // 2 - ROWS, 1)
    made = [jnp.zeros((blocks, LANES), F32) for _ in range(strips)]
    for t in range(strips):
        value = jnp.zeros((blocks, 1), F32)
        for j in range(strips):
            entry = top_value(j, t, strips)
            if entry:
                value = value + entry * low[j][:, 0:1]
        made[0] = jnp.where(lane == t, value + top, made[0])
    m = 1
    while m < LANES:
        for j in range(strips):
            start = strips * m + j * m
            block = start // LANES
            shift = (start % LANES - m) % LANES
            moved = pltpu.roll(low[j], shift, 1) if shift else low[j]
            inside = (lane >= start % LANES) & (lane < start % LANES + m)
            made[block] = jnp.where(inside, moved, made[block])
        m *= 2
    for block in range(strips):
        start = block * LANES
        out_ref[:, start : start + LANES] = shrink(made[block], STEP * weight_ref[0:1, start : start + LANES])


def top_value(spot, index, strips):
    if index == 0:
        return math.sqrt(1.0 / strips)
    m = 1 << (index.bit_length() - 1)
    span = strips // m
    within = spot - (index - m) * span
    if within < 0 or within >= span:
        return 0.0
    return math.sqrt(m / strips) * (1.0 if within < span // 2 else -1.0)


def call(kernel, outs, *operands, **kwargs):
    return pl.pallas_call(
        kernel,
        out_shape=[jax.ShapeDtypeStruct(shape, dtype) for shape, dtype in outs],
        compiler_params=pltpu.CompilerParams(vmem_limit_bytes=40 * 1024 * 1024),
        **kwargs,
    )(*operands)


def body(
    observations,
    jacobian,
    block_row,
    block_col,
    block_count,
    block_band,
    carry_decay,
    sparsity_weight,
):
    owners = lax.axis_size("tile")
    sectors = owners // WIN
    strips = sectors * SEC_STRIPS
    lines = NLAT // owners
    betas = momentum_weights(ITERS)
    arguments = [
        block_band.reshape(1, SB_DEV),
        observations,
        block_row.reshape(1, SLOTS),
        block_col.reshape(1, SLOTS),
        carry_decay.reshape(1, NBANDS),
        sparsity_weight.reshape(1, -1),
        jacobian.reshape(SLOTS * SOUNDS, STRIP),
    ]
    message = ((owners, ROWS, LANES), F32)
    narrow = ((SLOTS, LANES), F32)
    strip_rows = ((SLOTS, STRIP), F32)
    table_rows = ((TABLE_ROWS, LANES), F32)

    def trade(values):
        return lax.all_to_all(values, "tile", 0, 0, tiled=True)

    def with_sectors(values):
        found = [values]
        for shift in range(1, sectors):
            pairs = [
                (d, d // sectors * sectors + (d + shift) % sectors) for d in range(owners)
            ]
            found.append(lax.ppermute(values, "tile", pairs))
        return found

    arguments = [pltpu.with_memory_space_constraint(a, pltpu.HBM) for a in arguments]
    bands, observed, rows, cols, decay, weight, flat, first = call(
        start_kernel,
        [(a.shape, a.dtype) for a in arguments] + [((owners, 2, LANES), F32)],
        *arguments,
        in_specs=[pl.BlockSpec(memory_space=pltpu.HBM)] * len(arguments),
        out_specs=[pl.BlockSpec(memory_space=pltpu.VMEM)] * len(arguments)
        + [pl.BlockSpec(memory_space=pltpu.HBM)],
        scratch_shapes=[
            pltpu.VMEM((owners, 2, LANES), F32),
            pltpu.SemaphoreType.DMA((len(arguments) + 1,)),
        ],
    )
    first = trade(first)
    high, low, column, obs_grad, obs_slot, table = call(
        functools.partial(transform_kernel, strips),
        [
            ((SLOTS * SOUNDS, STRIP), BF16),
            ((SLOTS * SOUNDS, STRIP), BF16),
            strip_rows,
            strip_rows,
            narrow,
            table_rows,
        ],
        flat,
        observed,
        rows,
        cols,
        block_count,
        bands,
        in_specs=[
            pl.BlockSpec(memory_space=pltpu.SMEM if i == 4 else pltpu.VMEM) for i in range(6)
        ],
    )
    tables = with_sectors(table)
    twin, start_grad, row_match, limit, send, strip_match, top_matrix, prepared, rank = call(
        functools.partial(prepare_kernel, strips, owners),
        [
            strip_rows,
            strip_rows,
            ((SLOTS, SLOTS * SOUNDS), F32),
            strip_rows,
            ((owners * ROWS, 3 * 4 * SLOTS), BF16),
            ((SLOTS, SLOTS), F32),
            narrow,
            message,
            narrow,
        ],
        column,
        obs_grad,
        table,
        weight,
    )
    point, top, second, hot, line_tops, grad, lead = call(
        functools.partial(first_step_kernel, strips, owners),
        [
            strip_rows,
            narrow,
            message,
            ((sectors * SLOTS, NBANDS), F32),
            ((strips * SLOTS, LANES), F32),
            strip_rows,
            narrow,
        ],
        first,
        column,
        twin,
        start_grad,
        limit,
        strip_match,
        top_matrix,
        decay,
        weight,
        prepared,
        high,
        low,
        row_match,
        obs_slot,
        *tables,
    )
    second = trade(second)
    third, values = call(
        functools.partial(second_step_kernel, strips, owners, betas[1]),
        [message, ((1, SLOTS * SOUNDS), F32)],
        first,
        second,
        column,
        twin,
        grad,
        limit,
        strip_match,
        top_matrix,
        decay,
        weight,
        hot,
        line_tops,
        lead,
        rank,
        send,
        point,
        top,
        high,
        low,
        row_match,
        obs_slot,
        *tables,
    )
    third = trade(third)
    coeffs, misfit = call(
        functools.partial(finish_kernel, strips, owners),
        [((lines * WIN, strips * STRIP), F32), ((SB_DEV, SOUNDS), F32)],
        first,
        third,
        second,
        table,
        values,
        observed,
        bands,
        decay,
        weight,
    )
    return (coeffs.reshape(lines, WIN, strips * STRIP), misfit)


def solution(mesh):
    return jax.shard_map(
        body,
        mesh=mesh,
        in_specs=(
            P(("ens", "tile"), None),
            P("tile", None, None),
            P("tile"),
            P("tile"),
            P("tile"),
            P("tile"),
            P(),
            P(),
        ),
        out_specs=(P(("ens", "tile"), None, None), P(("ens", "tile"), None)),
        check_vma=False,
    )
```

```python
import functools
import math

import jax
import jax.numpy as jnp
from jax import lax
from jax.experimental import pallas as pl
from jax.experimental.pallas import tpu as pltpu
from jax.sharding import PartitionSpec as P

WIN = 8
NLAT = 64
SEC_STRIPS = 2
STRIP = 256
SOUNDS = 64
SB_DEV = 32
NBANDS = 128
ITERS = 3
SLOTS = 16
LANES = 128
ROWS = 8
STEP = 0.2
MISFIT = 32

F32 = jnp.float32
BF16 = jnp.bfloat16
HIGHEST = lax.Precision.HIGHEST

LINE, SPOT, BAND, TOTAL, ROW, COL, VALID = range(7)
LINE_ROW, SPOT_ROW, TOTAL_ROW, APPROX_ROW = range(SLOTS, SLOTS + 4)
TABLE_ROWS = SLOTS + ROWS


def momentum_weights(total_steps):
    weights = []
    current = 1.0
    for _ in range(total_steps):
        following = (1.0 + math.sqrt(1.0 + 4.0 * current * current)) / 2.0
        weights.append((current - 1.0) / following)
        current = following
    return weights


def iota(shape, axis):
    return lax.broadcasted_iota(jnp.int32, shape, axis)


def shrink(values, limit):
    return values - jnp.minimum(jnp.maximum(values, -limit), limit)


def to_col(row):
    n = row.shape[1]
    eye = iota((n, n), 0) == iota((n, n), 1)
    return jnp.sum(jnp.where(eye, row, 0.0), axis=1, keepdims=True)


def to_row(col):
    n = col.shape[0]
    eye = iota((n, n), 0) == iota((n, n), 1)
    return jnp.sum(jnp.where(eye, col, 0.0), axis=0, keepdims=True)


def exact_dot(left, right):
    return jnp.dot(left, right, precision=HIGHEST, preferred_element_type=F32)


def dot(left, right):
    return jnp.dot(left, right, preferred_element_type=F32)


def dot_nt(left, right):
    return lax.dot_general(left, right, (((1,), (1,)), ((), ())), preferred_element_type=F32)


def split(values):
    high = values.astype(BF16)
    return high, (values - high.astype(F32)).astype(BF16)


def split_rows(values):
    high = values.astype(BF16)
    rest = values - high.astype(F32)
    middle = rest.astype(BF16)
    return jnp.concatenate([high, middle, (rest - middle.astype(F32)).astype(BF16)], axis=0)


def haar_signs():
    coef = iota((1, STRIP), 1).astype(F32)
    level = jnp.zeros((1, STRIP), F32) + 1.0
    m = 2
    while m < STRIP:
        level = jnp.where(coef >= m, float(m), level)
        m *= 2
    first = coef == 0.0
    shift = jnp.where(first, 0.0, coef - level)
    half = jnp.where(first, 2.0, 0.5)
    within = iota((STRIP, STRIP), 0).astype(F32) * (level / STRIP) - shift
    inside = (within >= 0.0) & (within < 1.0)
    return jnp.where(inside, jnp.where(within < half, 1.0, -1.0), 0.0).astype(BF16)


def haar_scales():
    coef = iota((1, STRIP), 1)
    out = jnp.full((1, STRIP), math.sqrt(1.0 / STRIP), F32)
    m = 1
    while m < STRIP:
        out = jnp.where((coef >= m) & (coef < 2 * m), math.sqrt(m / STRIP), out)
        m *= 2
    return out


def top_entry(spot, index, strips):
    if index == 0:
        return jnp.full(spot.shape, math.sqrt(1.0 / strips), F32)
    m = 1 << (index.bit_length() - 1)
    span = strips // m
    start = float((index - m) * span)
    half = start + span / 2
    end = start + span
    scale = math.sqrt(m / strips)
    positive = (spot >= start) & (spot < half)
    negative = (spot >= half) & (spot < end)
    return jnp.where(positive, scale, jnp.where(negative, -scale, 0.0))


def weekly(rows, sectors):
    return [sum(rows[w * sectors + 1 : (w + 1) * sectors], rows[w * sectors]) for w in range(WIN)]


def scan_back(totals, decay):
    running = totals[WIN - 1]
    out = [running]
    for w in range(WIN - 2, -1, -1):
        running = running * decay + totals[w]
        out.insert(0, running)
    return out


def scan_ahead(totals, decay):
    running = totals[0]
    out = [running]
    for w in range(1, WIN):
        running = running * decay + totals[w]
        out.append(running)
    return out


def pick(rows, index):
    out = rows[0]
    for w in range(1, len(rows)):
        out = jnp.where(index == w, rows[w], out)
    return out


def background(first, partial_rows, decay, sectors):
    counts = weekly([first[t, 0:1, :] for t in range(WIN * sectors)], sectors)
    sums = weekly([first[t, 1:2, :] for t in range(WIN * sectors)], sectors)
    partials = weekly(partial_rows, sectors)
    carried = scan_ahead(partials, decay)
    back = [
        SOUNDS * partials[w] + (SOUNDS * counts[w]) * carried[w] - sums[w] for w in range(WIN)
    ]
    returned = scan_back(back, decay)
    return [carried[w] + returned[w] / SOUNDS for w in range(WIN)], carried


def one_hot_bands(band_col):
    return jnp.where(band_col == iota((band_col.shape[0], NBANDS), 1).astype(F32), 1.0, 0.0)


def forward(point, blocks_ref, mix):
    total = None
    for k in range(SLOTS):
        product = blocks_ref[k * SOUNDS : (k + 1) * SOUNDS, :] * point[k : k + 1, :]
        values = jnp.sum(product[:, :LANES] + product[:, LANES:], axis=1, keepdims=True)
        term = values * mix[k : k + 1, :]
        total = term if total is None else total + term
    return total


def back_rows(chosen, blocks_ref):
    return [
        jnp.sum(
            blocks_ref[k * SOUNDS : (k + 1) * SOUNDS, :] * chosen[:, k : k + 1],
            axis=0,
            keepdims=True,
        )
        for k in range(SLOTS)
    ]


def stack_rows(rows):
    at = iota((SLOTS, STRIP), 0)
    out = jnp.broadcast_to(rows[0], (SLOTS, STRIP))
    for k in range(1, SLOTS):
        out = jnp.where(at == k, rows[k], out)
    return out


def mix_rows(match, rows):
    out = match[:, 0:1] * rows[0]
    for k in range(1, SLOTS):
        out = out + match[:, k : k + 1] * rows[k]
    return out


def start_kernel(*refs):
    fetched = (len(refs) - 3) // 2
    sources, targets = refs[:fetched], refs[fetched : 2 * fetched]
    out_ref, made_ref, sems = refs[2 * fetched :]
    copies = [
        pltpu.make_async_copy(source, target, sems.at[i])
        for i, (source, target) in enumerate(zip(sources, targets))
    ]
    for copy in copies:
        copy.start()
    copies[0].wait()
    copies[1].wait()
    band_ref, obs_ref = targets[:2]
    hot = one_hot_bands(to_col(band_ref[...].astype(F32)))
    sums = jnp.sum(obs_ref[...], axis=1, keepdims=True)
    counted = jnp.sum(hot, axis=0, keepdims=True)
    summed = jnp.sum(hot * sums, axis=0, keepdims=True)
    for t in range(made_ref.shape[0]):
        made_ref[t, 0:1, :] = counted
        made_ref[t, 1:2, :] = summed
    sent = pltpu.make_async_copy(made_ref, out_ref, sems.at[fetched])
    sent.start()
    for copy in copies[2:]:
        copy.wait()
    sent.wait()


def along_lanes(col):
    n = col.shape[0]
    here = iota((n, LANES), 0) == iota((n, LANES), 1)
    return jnp.sum(jnp.where(here, col, 0.0), axis=0, keepdims=True)


def transform_kernel(
    strips,
    jac_ref,
    obs_ref,
    row_ref,
    col_ref,
    count_ref,
    band_ref,
    blocks_ref,
    column_ref,
    obs_grad_ref,
    obs_slot_ref,
    mix_ref,
    table_ref,
):
    sectors = strips // SEC_STRIPS
    sector = lax.rem(lax.axis_index("tile"), sectors).astype(F32)
    signs = haar_signs()
    scales = haar_scales()
    chunk = STRIP
    for start in range(0, SLOTS * SOUNDS, chunk):
        high, low = split(jac_ref[start : start + chunk, :])
        blocks_ref[start : start + chunk, :] = (dot(high, signs) + dot(low, signs)) * scales

    row_of = to_col(row_ref[...].astype(F32))
    col_of = to_col(col_ref[...].astype(F32))
    valid = jnp.where(iota((SLOTS, 1), 0) < count_ref[0], 1.0, 0.0)
    line = jnp.floor(col_of / SEC_STRIPS)
    spot = sector * SEC_STRIPS + (col_of - line * SEC_STRIPS)
    row_hot = jnp.where(row_of == iota((SLOTS, SB_DEV), 1).astype(F32), 1.0, 0.0)
    band_row = band_ref[...].astype(F32)
    band = jnp.sum(row_hot * band_row, axis=1, keepdims=True)
    band = jnp.where(valid > 0.0, band, -1.0)
    lane = iota((1, LANES), 1)
    wanted = jnp.where(lane < SLOTS, along_lanes(row_of), -1.0)
    wanted_hot = jnp.where(iota((SB_DEV, LANES), 0).astype(F32) == wanted, 1.0, 0.0)
    obs_slot = exact_dot(obs_ref[...].T, wanted_hot)
    obs_slot_ref[...] = obs_slot
    block_lane = (lane >= MISFIT) & (lane < MISFIT + SB_DEV)
    wanted = jnp.where(block_lane, (lane - MISFIT).astype(F32), wanted)
    mix_ref[...] = jnp.where(row_of == wanted, valid, 0.0)
    obs_grad = stack_rows(back_rows(obs_slot, blocks_ref))
    obs_grad_ref[...] = obs_grad
    ones = [
        jnp.sum(blocks_ref[k * SOUNDS : (k + 1) * SOUNDS, :], axis=0, keepdims=True)
        for k in range(SLOTS)
    ]
    column = stack_rows(ones) * valid
    column_ref[...] = column

    at = iota((SLOTS, LANES), 1)
    info = jnp.zeros((SLOTS, LANES), F32)
    for place, values in (
        (LINE, line),
        (SPOT, spot),
        (BAND, band),
        (TOTAL, column[:, 0:1]),
        (ROW, row_of),
        (COL, col_of),
        (VALID, valid),
    ):
        info = jnp.where(at == place, values, info)
    table_ref[0:SLOTS, :] = info
    table_ref[SLOTS:TABLE_ROWS, :] = jnp.zeros((TABLE_ROWS - SLOTS, LANES), F32)
    table_ref[LINE_ROW : LINE_ROW + 1, :] = along_lanes(line + 1.0)
    table_ref[SPOT_ROW : SPOT_ROW + 1, :] = along_lanes(spot + 1.0)
    table_ref[TOTAL_ROW : TOTAL_ROW + 1, :] = along_lanes(column[:, 0:1])
    table_ref[APPROX_ROW : APPROX_ROW + 1, :] = along_lanes(-obs_grad[:, 0:1] * valid)


def prepare_kernel(
    strips,
    owners,
    column_ref,
    obs_grad_ref,
    table_ref,
    weight_ref,
    twin_ref,
    start_grad_ref,
    limit_ref,
    send_ref,
    strip_match_ref,
    top_matrix_ref,
    message_ref,
    rank_ref,
):
    strips_owner = NLAT * SEC_STRIPS // owners
    column = column_ref[...]
    info = table_ref[0:SLOTS, :]
    spot = info[:, SPOT : SPOT + 1]
    band = info[:, BAND : BAND + 1]
    col_of = info[:, COL : COL + 1]
    valid = info[:, VALID : VALID + 1]
    col_row = to_row(col_of)
    valid_row = to_row(valid)

    same = jnp.where(col_of == col_row, 1.0, 0.0)
    before = jnp.where(iota((SLOTS, SLOTS), 1) < iota((SLOTS, SLOTS), 0), 1.0, 0.0)
    other = jnp.where(iota((SLOTS, SLOTS), 1) != iota((SLOTS, SLOTS), 0), same, 0.0)
    strip_match_ref[...] = same * valid_row
    start_grad_ref[...] = -exact_dot(same * valid_row, obs_grad_ref[...])
    twin_ref[...] = exact_dot(other, column)
    first = jnp.where(jnp.sum(same * before, axis=1, keepdims=True) > 0.0, 0.0, 1.0)
    owner = jnp.floor(col_of / strips_owner)
    owner_row = jnp.floor(col_row / strips_owner)
    rank = jnp.sum(jnp.where(owner == owner_row, before, 0.0), axis=1, keepdims=True)

    at = iota((SLOTS, LANES), 1)
    rank_ref[...] = jnp.where(at == 0, rank, jnp.where(at == 1, first, 0.0))
    matrix = jnp.zeros((SLOTS, LANES), F32)
    for t in range(strips):
        matrix = jnp.where(at == t, top_entry(spot, t, strips), matrix)
    top_matrix_ref[...] = matrix

    local = iota((1, LANES), 1)
    limits_low = jnp.zeros((SLOTS, LANES), F32)
    limits_high = jnp.zeros((SLOTS, LANES), F32)
    for j in range(strips):
        low_row = jnp.zeros((1, LANES), F32)
        m = 1
        while m < LANES:
            start = strips * m + j * m
            block = weight_ref[0:1, start // LANES * LANES : start // LANES * LANES + LANES]
            shift = (m - start % LANES) % LANES
            moved = pltpu.roll(jnp.broadcast_to(block, (ROWS, LANES)), shift, 1)[0:1] if shift else block
            low_row = jnp.where((local >= m) & (local < 2 * m), moved, low_row)
            m *= 2
        high_row = weight_ref[0:1, (strips + j) * LANES : (strips + j + 1) * LANES]
        limits_low = jnp.where(spot == float(j), low_row, limits_low)
        limits_high = jnp.where(spot == float(j), high_row, limits_high)
    limit_ref[:, :LANES] = STEP * limits_low
    limit_ref[:, LANES:] = STEP * limits_high

    shape = (owners * ROWS, 3 * 4 * SLOTS)
    target = (iota(shape, 0) // ROWS).astype(F32)
    kind = iota(shape, 0) % ROWS
    place = iota(shape, 1) % (4 * SLOTS)
    group = place // SLOTS
    slim_shape = (SLOTS, shape[1])
    slim = iota(slim_shape, 1) % SLOTS == iota(slim_shape, 0)
    owner_wide = jnp.sum(jnp.where(slim, owner, 0.0), axis=0, keepdims=True)
    rank_wide = jnp.sum(jnp.where(slim, rank, 0.0), axis=0, keepdims=True)
    kind_f = kind.astype(F32)
    hit = (group == 0) & (kind_f == 2.0 * rank_wide)
    hit = hit | ((group == 1) & (kind_f == 2.0 * rank_wide + 1.0))
    hit = hit | ((group == 2) & (kind == 5))
    hit = (hit & (owner_wide == target)) | ((place == 3 * SLOTS) & (kind == 4))
    send = jnp.where(hit, 1.0, 0.0).astype(BF16)
    send_ref[...] = send

    at_f = at.astype(F32)
    base = rank * (LANES // 2)
    meta = jnp.where(at_f == base, col_of - owner * strips_owner + 1.0, 0.0)
    meta = jnp.where(at_f == base + 1.0, band + 1.0, meta)
    message_ref[...] = message_rows(send, column, meta, None).reshape(message_ref.shape)


def message_rows(send, strips_part, meta, partial):
    if partial is None:
        bottom = jnp.zeros((SLOTS, LANES), F32)
    else:
        bottom = jnp.where(iota((SLOTS, LANES), 0) == 0, partial, 0.0)
    stacked = jnp.concatenate([strips_part[:, :LANES], strips_part[:, LANES:], meta, bottom], axis=0)
    return dot(send, split_rows(stacked))


def side_by_side(rows):
    out = rows[0]
    for i, row in enumerate(rows[1:], 1):
        wide = jnp.broadcast_to(row, (ROWS, LANES))
        out = out + pltpu.roll(wide, i * SLOTS, 1)[0:1]
    return out


def slot_scalars(hot, scalar):
    col = jnp.sum(hot * scalar, axis=1, keepdims=True)
    return col, along_lanes(col)


def advance(strips, col, row, grads, column, twin, same, approx_row, total_row, line_tops):
    other = jnp.sum(jnp.where(same > 0.0, row[:, :SLOTS], 0.0), axis=1, keepdims=True)
    full = grads + col[:SLOTS] * column + other * twin
    sources = approx_row + row * total_row
    at = iota((SLOTS, LANES), 1)
    top_grad = jnp.zeros((SLOTS, LANES), F32)
    for t in range(strips):
        value = jnp.sum(line_tops[t * SLOTS : (t + 1) * SLOTS] * sources, axis=1, keepdims=True)
        top_grad = jnp.where(at == t, value, top_grad)
    return full, top_grad


def with_approx(point, top, matrix):
    approx = jnp.sum(matrix * top, axis=1, keepdims=True)
    return jnp.where(iota((SLOTS, STRIP), 1) == 0, approx, point)


def band_partial(point, column, hot):
    dots = jnp.sum(point * column, axis=1, keepdims=True)
    return jnp.sum(hot * dots, axis=0, keepdims=True) / SOUNDS


def twins(strip_match):
    return jnp.where(iota((SLOTS, SLOTS), 0) == iota((SLOTS, SLOTS), 1), 0.0, strip_match)


def first_step_kernel(
    strips,
    owners,
    first_ref,
    column_ref,
    twin_ref,
    grad_ref,
    limit_ref,
    strip_match_ref,
    top_matrix_ref,
    decay_ref,
    weight_ref,
    prepared_ref,
    blocks_ref,
    mix_ref,
    obs_slot_ref,
    *rest,
):
    sectors = strips // SEC_STRIPS
    tables = rest[:sectors]
    point_ref, top_ref, message_ref, hot_ref, line_tops_ref, grad_out_ref, lead_ref = rest[sectors:]
    my_index = lax.axis_index("tile")
    window = my_index // sectors
    sums = weekly([first_ref[t, 1:2, :] for t in range(owners)], sectors)
    returned = scan_back([-s for s in sums], decay_ref[...])
    scalar = pick(returned, window) / SOUNDS
    hot = jnp.concatenate([one_hot_bands(t[0:SLOTS, BAND : BAND + 1]) for t in tables], axis=0)
    hot_ref[...] = hot

    def row(index):
        return side_by_side([t[index : index + 1, :] for t in tables])

    spot_row = row(SPOT_ROW) - 1.0
    on_line = tables[0][0:SLOTS, LINE : LINE + 1] + 1.0 == row(LINE_ROW)
    line_tops = jnp.concatenate(
        [jnp.where(on_line, top_entry(spot_row, t, strips), 0.0) for t in range(strips)], axis=0
    )
    line_tops_ref[...] = line_tops
    column = column_ref[...]
    col, along = slot_scalars(hot, scalar)
    grads, top_grad = advance(
        strips,
        col,
        along,
        grad_ref[...],
        column,
        twin_ref[...],
        twins(strip_match_ref[...]),
        row(APPROX_ROW),
        row(TOTAL_ROW),
        line_tops,
    )
    updated = shrink(-STEP * grads, limit_ref[...])
    top = shrink(-STEP * top_grad, STEP * weight_ref[0:1, :LANES])
    point = with_approx(updated, top, top_matrix_ref[...])
    point_ref[...] = point
    top_ref[...] = top
    partial = band_partial(point, column, hot[:SLOTS])
    chosen = forward(point, blocks_ref, mix_ref[...]) - obs_slot_ref[...]
    rows = back_rows(chosen, blocks_ref)
    grad_out_ref[...] = mix_rows(strip_match_ref[...], rows)
    info = tables[0][0:SLOTS, :]
    at = iota((SLOTS, LANES), 0)
    fronts = jnp.broadcast_to(rows[0][:, :LANES], (SLOTS, LANES))
    for k in range(1, SLOTS):
        fronts = jnp.where(at == k, rows[k][:, :LANES], fronts)
    approx = along_lanes(fronts[:, 0:1] * info[:, VALID : VALID + 1])
    kind = iota(message_ref.shape, 1)
    message_ref[...] = jnp.where(
        kind == 4,
        partial.reshape(1, 1, LANES),
        jnp.where(kind == 6, approx.reshape(1, 1, LANES), prepared_ref[...]),
    )

    sector = lax.rem(my_index, sectors).astype(F32)
    sector_row = jnp.floor(spot_row / SEC_STRIPS)
    lane = iota((SLOTS, LANES), 1)
    before = jnp.where(lane < iota((SLOTS, LANES), 0), 1.0, 0.0)
    earlier = jnp.where(lane < SLOTS, before, jnp.where(sector_row < sector, 1.0, 0.0))
    taken = jnp.sum(jnp.where(on_line, earlier, 0.0), axis=1, keepdims=True)
    lead_ref[...] = jnp.broadcast_to(jnp.where(taken > 0.0, 0.0, 1.0), lead_ref.shape)


def second_step_kernel(
    strips,
    owners,
    beta,
    first_ref,
    second_ref,
    column_ref,
    twin_ref,
    grad_ref,
    limit_ref,
    strip_match_ref,
    top_matrix_ref,
    decay_ref,
    weight_ref,
    hot_ref,
    line_tops_ref,
    lead_ref,
    rank_ref,
    send_ref,
    point_ref,
    top_ref,
    blocks_ref,
    mix_ref,
    obs_slot_ref,
    *rest,
):
    sectors = strips // SEC_STRIPS
    tables, rest = rest[:sectors], rest[sectors:]
    message_ref, values_ref = rest
    my_index = lax.axis_index("tile")
    window = my_index // sectors
    sector = lax.rem(my_index, sectors)
    approx_rows = []
    for shift in range(sectors):
        pair = window * sectors + lax.rem(sector + (sectors - shift), sectors)
        approx_rows.append(second_ref[pair, 6:7, :])
    combined, _ = background(
        first_ref, [second_ref[t, 4:5, :] for t in range(owners)], decay_ref[...], sectors
    )
    hot = hot_ref[...]
    column = column_ref[...]
    col, along = slot_scalars(hot, pick(combined, window))
    grads, top_grad = advance(
        strips,
        col,
        along,
        grad_ref[...],
        column,
        twin_ref[...],
        twins(strip_match_ref[...]),
        side_by_side(approx_rows),
        side_by_side([t[TOTAL_ROW : TOTAL_ROW + 1, :] for t in tables]),
        line_tops_ref[...],
    )
    old = point_ref[...]
    old_top = top_ref[...]
    updated = shrink(old - STEP * grads, limit_ref[...])
    top = shrink(old_top - STEP * top_grad, STEP * weight_ref[0:1, :LANES])
    point = updated + beta * (updated - old)
    top = top + beta * (top - old_top)
    point = with_approx(point, top, top_matrix_ref[...])
    values = forward(point, blocks_ref, mix_ref[...])
    values_ref[...] = values
    grad = stack_rows(back_rows(values - obs_slot_ref[...], blocks_ref))

    partial = band_partial(point, column, hot[:SLOTS])
    info = tables[0][0:SLOTS, :]
    valid = info[:, VALID : VALID + 1]
    top = top * lead_ref[:, 0:1]
    rank = rank_ref[:, 0:1]
    meta = jnp.where(rank == 0.0, pltpu.roll(top, ROWS, 1), pltpu.roll(top, LANES // 2 + ROWS, 1))
    kept = jnp.where(iota((SLOTS, STRIP), 1) == 0, 0.0, point * rank_ref[:, 1:2])
    rows = message_rows(send_ref[...], kept - STEP * (valid * grad), meta, partial)
    message_ref[...] = rows.reshape(message_ref.shape)


def placing(strips, owners, second_ref, values_ref, obs_ref, band_ref):
    sectors = strips // SEC_STRIPS
    lines = NLAT // owners
    count = owners * ROWS
    meta = second_ref[:, 5, :]
    wide = (owners, count)
    pair_of = iota(wide, 1) // ROWS == iota(wide, 0)
    kind = iota((1, count), 1) % ROWS
    tall = (count, owners)
    tall_pair = iota(tall, 0) // ROWS == iota(tall, 1)
    tall_kind = iota((count, 1), 0) % ROWS
    strip_rows = []
    band_col = jnp.zeros((count, 1), F32)
    for q in range(2):
        strip = meta[:, q * (LANES // 2) : q * (LANES // 2) + 1]
        band = meta[:, q * (LANES // 2) + 1 : q * (LANES // 2) + 2]
        strip_rows.append(jnp.sum(jnp.where(pair_of, strip, 0.0), axis=0, keepdims=True) - 1.0)
        band_tall = jnp.sum(jnp.where(tall_pair, to_row(band), 0.0), axis=1, keepdims=True)
        band_col = jnp.where(tall_kind // 2 == q, band_tall, band_col)
    band_hot = one_hot_bands(band_col - 1.0)
    scaled = jnp.where(tall_kind < 4, STEP * second_ref[...].reshape(count, LANES), 0.0)

    def line_of(strip):
        return jnp.floor(strip / SEC_STRIPS)

    blocks = lines * WIN
    pair = iota((1, count), 1) // ROWS
    window = pair // sectors
    sector = (pair - window * sectors).astype(F32)
    line_col = (iota((blocks, 1), 0) // WIN).astype(F32)
    window_col = iota((blocks, 1), 0) % WIN
    strip_row = jnp.where(kind < 2, strip_rows[0], strip_rows[1])
    slot_line = line_of(strip_row)
    slot_spot = sector * SEC_STRIPS + strip_row - slot_line * SEC_STRIPS
    base = (window == window_col) & (slot_line == line_col) & (strip_row >= 0.0)
    base = jnp.where(base & (kind < 4), 1.0, 0.0)
    parts = []
    for half in range(2):
        part = jnp.where(kind % 2 == half, base, 0.0)
        for j in range(strips):
            parts.append(jnp.where(slot_spot == float(j), part, 0.0))
    for q in range(2):
        hit = (window == window_col) & (line_of(strip_rows[q]) == line_col) & (strip_rows[q] >= 0.0) & (kind == 5)
        parts.append(jnp.where(hit, 1.0, 0.0))
    place = jnp.concatenate(parts, axis=0).astype(BF16)
    place = jnp.concatenate([place, place, place], axis=1)

    differ = values_ref[...].T[MISFIT : MISFIT + SB_DEV, :] - obs_ref[...]
    block_hot = one_hot_bands(to_col(band_ref[...].astype(F32)))
    return place, band_hot, scaled, differ, block_hot


def finish_kernel(
    strips,
    owners,
    first_ref,
    third_ref,
    second_ref,
    values_ref,
    obs_ref,
    band_ref,
    decay_ref,
    weight_ref,
    out_ref,
    misfit_ref,
):
    sectors = strips // SEC_STRIPS
    blocks = NLAT // owners * WIN
    count = owners * ROWS
    window = lax.axis_index("tile") // sectors
    place, band_hot, scaled, differ, block_hot = placing(
        strips, owners, second_ref, values_ref, obs_ref, band_ref
    )
    combined, carried = background(
        first_ref, [third_ref[t, 4:5, :] for t in range(owners)], decay_ref[...], sectors
    )
    spread = jnp.concatenate(
        [jnp.broadcast_to(row, (sectors * ROWS, NBANDS)) for row in combined], axis=0
    )
    scalars = jnp.sum(band_hot * spread, axis=1, keepdims=True)
    rows = third_ref[...].reshape(count, LANES) - scalars * scaled
    placed = dot(place, split_rows(rows))
    offset = jnp.sum(block_hot * pick(carried, window), axis=1, keepdims=True)
    misfit_ref[...] = differ + offset

    lane = iota((1, LANES), 1)
    for j in range(strips):
        start = (strips + j) * LANES
        values = placed[(strips + j) * blocks : (strips + j + 1) * blocks]
        out_ref[:, start : start + LANES] = shrink(values, STEP * weight_ref[0:1, start : start + LANES])

    low = [placed[j * blocks : (j + 1) * blocks] for j in range(strips)]
    tops = [placed[(2 * strips + q) * blocks : (2 * strips + q + 1) * blocks] for q in range(2)]
    top = pltpu.roll(tops[0], LANES - ROWS, 1) + pltpu.roll(tops[1], LANES // 2 - ROWS, 1)
    made = [jnp.zeros((blocks, LANES), F32) for _ in range(strips)]
    for t in range(strips):
        value = jnp.zeros((blocks, 1), F32)
        for j in range(strips):
            entry = top_value(j, t, strips)
            if entry:
                value = value + entry * low[j][:, 0:1]
        made[0] = jnp.where(lane == t, value + top, made[0])
    m = 1
    while m < LANES:
        for j in range(strips):
            start = strips * m + j * m
            block = start // LANES
            shift = (start % LANES - m) % LANES
            moved = pltpu.roll(low[j], shift, 1) if shift else low[j]
            inside = (lane >= start % LANES) & (lane < start % LANES + m)
            made[block] = jnp.where(inside, moved, made[block])
        m *= 2
    for block in range(strips):
        start = block * LANES
        out_ref[:, start : start + LANES] = shrink(made[block], STEP * weight_ref[0:1, start : start + LANES])


def top_value(spot, index, strips):
    if index == 0:
        return math.sqrt(1.0 / strips)
    m = 1 << (index.bit_length() - 1)
    span = strips // m
    within = spot - (index - m) * span
    if within < 0 or within >= span:
        return 0.0
    return math.sqrt(m / strips) * (1.0 if within < span // 2 else -1.0)


def call(kernel, outs, *operands, **kwargs):
    return pl.pallas_call(
        kernel,
        out_shape=[jax.ShapeDtypeStruct(shape, dtype) for shape, dtype in outs],
        compiler_params=pltpu.CompilerParams(vmem_limit_bytes=40 * 1024 * 1024),
        **kwargs,
    )(*operands)


def body(
    observations,
    jacobian,
    block_row,
    block_col,
    block_count,
    block_band,
    carry_decay,
    sparsity_weight,
):
    owners = lax.axis_size("tile")
    sectors = owners // WIN
    strips = sectors * SEC_STRIPS
    lines = NLAT // owners
    betas = momentum_weights(ITERS)
    arguments = [
        block_band.reshape(1, SB_DEV),
        observations,
        block_row.reshape(1, SLOTS),
        block_col.reshape(1, SLOTS),
        carry_decay.reshape(1, NBANDS),
        sparsity_weight.reshape(1, -1),
        jacobian.reshape(SLOTS * SOUNDS, STRIP),
    ]
    message = ((owners, ROWS, LANES), F32)
    narrow = ((SLOTS, LANES), F32)
    strip_rows = ((SLOTS, STRIP), F32)
    table_rows = ((TABLE_ROWS, LANES), F32)

    def trade(values):
        return lax.all_to_all(values, "tile", 0, 0, tiled=True)

    def with_sectors(values):
        found = [values]
        for shift in range(1, sectors):
            pairs = [
                (d, d // sectors * sectors + (d + shift) % sectors) for d in range(owners)
            ]
            found.append(lax.ppermute(values, "tile", pairs))
        return found

    arguments = [pltpu.with_memory_space_constraint(a, pltpu.HBM) for a in arguments]
    bands, observed, rows, cols, decay, weight, flat, first = call(
        start_kernel,
        [(a.shape, a.dtype) for a in arguments] + [((owners, 2, LANES), F32)],
        *arguments,
        in_specs=[pl.BlockSpec(memory_space=pltpu.HBM)] * len(arguments),
        out_specs=[pl.BlockSpec(memory_space=pltpu.VMEM)] * len(arguments)
        + [pl.BlockSpec(memory_space=pltpu.HBM)],
        scratch_shapes=[
            pltpu.VMEM((owners, 2, LANES), F32),
            pltpu.SemaphoreType.DMA((len(arguments) + 1,)),
        ],
    )
    first = trade(first)
    blocks, column, obs_grad, obs_slot, mix, table = call(
        functools.partial(transform_kernel, strips),
        [
            ((SLOTS * SOUNDS, STRIP), F32),
            strip_rows,
            strip_rows,
            ((SOUNDS, LANES), F32),
            narrow,
            table_rows,
        ],
        flat,
        observed,
        rows,
        cols,
        block_count,
        bands,
        in_specs=[
            pl.BlockSpec(memory_space=pltpu.SMEM if i == 4 else pltpu.VMEM) for i in range(6)
        ],
    )
    tables = with_sectors(table)
    twin, start_grad, limit, send, strip_match, top_matrix, prepared, rank = call(
        functools.partial(prepare_kernel, strips, owners),
        [
            strip_rows,
            strip_rows,
            strip_rows,
            ((owners * ROWS, 3 * 4 * SLOTS), BF16),
            ((SLOTS, SLOTS), F32),
            narrow,
            message,
            narrow,
        ],
        column,
        obs_grad,
        table,
        weight,
    )
    point, top, second, hot, line_tops, grad, lead = call(
        functools.partial(first_step_kernel, strips, owners),
        [
            strip_rows,
            narrow,
            message,
            ((sectors * SLOTS, NBANDS), F32),
            ((strips * SLOTS, LANES), F32),
            strip_rows,
            narrow,
        ],
        first,
        column,
        twin,
        start_grad,
        limit,
        strip_match,
        top_matrix,
        decay,
        weight,
        prepared,
        blocks,
        mix,
        obs_slot,
        *tables,
    )
    second = trade(second)
    third, values = call(
        functools.partial(second_step_kernel, strips, owners, betas[1]),
        [message, ((SOUNDS, LANES), F32)],
        first,
        second,
        column,
        twin,
        grad,
        limit,
        strip_match,
        top_matrix,
        decay,
        weight,
        hot,
        line_tops,
        lead,
        rank,
        send,
        point,
        top,
        blocks,
        mix,
        obs_slot,
        *tables,
    )
    third = trade(third)
    coeffs, misfit = call(
        functools.partial(finish_kernel, strips, owners),
        [((lines * WIN, strips * STRIP), F32), ((SB_DEV, SOUNDS), F32)],
        first,
        third,
        second,
        values,
        observed,
        bands,
        decay,
        weight,
    )
    return (coeffs.reshape(lines, WIN, strips * STRIP), misfit)


def solution(mesh):
    return jax.shard_map(
        body,
        mesh=mesh,
        in_specs=(
            P(("ens", "tile"), None),
            P("tile", None, None),
            P("tile"),
            P("tile"),
            P("tile"),
            P("tile"),
            P(),
            P(),
        ),
        out_specs=(P(("ens", "tile"), None, None), P(("ens", "tile"), None)),
        check_vma=False,
    )
```

```python
import functools
import math

import jax
import jax.numpy as jnp
from jax import lax
from jax.experimental import pallas as pl
from jax.experimental.pallas import tpu as pltpu
from jax.sharding import PartitionSpec as P

WIN = 8
NLAT = 64
SEC_STRIPS = 2
STRIP = 256
SOUNDS = 64
SB_DEV = 32
NBANDS = 128
ITERS = 3
SLOTS = 16
LANES = 128
ROWS = 8
STEP = 0.2
MISFIT = 32

F32 = jnp.float32
BF16 = jnp.bfloat16
HIGHEST = lax.Precision.HIGHEST

LINE, SPOT, BAND, COL, VALID = range(5)
GRADS, COLUMNS, GROUP = 0, SLOTS, 2 * SLOTS
COUNTS, META, SUMS, SLOT_ROW = (GROUP + 4 + i for i in range(4))
FIRST_ROWS = GROUP + ROWS
S_STRIP, S_SPOT, S_BAND, S_VALID, S_TOTAL, S_APPROX = (i * SLOTS for i in range(6))


def momentum_weights(total_steps):
    weights = []
    current = 1.0
    for _ in range(total_steps):
        following = (1.0 + math.sqrt(1.0 + 4.0 * current * current)) / 2.0
        weights.append((current - 1.0) / following)
        current = following
    return weights


def iota(shape, axis):
    return lax.broadcasted_iota(jnp.int32, shape, axis)


def shrink(values, limit):
    return values - jnp.minimum(jnp.maximum(values, -limit), limit)


def to_col(row):
    n = row.shape[1]
    eye = iota((n, n), 0) == iota((n, n), 1)
    return jnp.sum(jnp.where(eye, row, 0.0), axis=1, keepdims=True)


def to_row(col):
    n = col.shape[0]
    eye = iota((n, n), 0) == iota((n, n), 1)
    return jnp.sum(jnp.where(eye, col, 0.0), axis=0, keepdims=True)


def exact_dot(left, right):
    return jnp.dot(left, right, precision=HIGHEST, preferred_element_type=F32)


def dot(left, right):
    return jnp.dot(left, right, preferred_element_type=F32)


def dot_nt(left, right):
    return lax.dot_general(left, right, (((1,), (1,)), ((), ())), preferred_element_type=F32)


def split(values):
    high = values.astype(BF16)
    return high, (values - high.astype(F32)).astype(BF16)


def split_parts(values):
    high = values.astype(BF16)
    rest = values - high.astype(F32)
    middle = rest.astype(BF16)
    return [high, middle, (rest - middle.astype(F32)).astype(BF16)]


def split_rows(values):
    return jnp.concatenate(split_parts(values), axis=0)


def haar_signs():
    coef = iota((1, STRIP), 1).astype(F32)
    level = jnp.zeros((1, STRIP), F32) + 1.0
    m = 2
    while m < STRIP:
        level = jnp.where(coef >= m, float(m), level)
        m *= 2
    first = coef == 0.0
    shift = jnp.where(first, 0.0, coef - level)
    half = jnp.where(first, 2.0, 0.5)
    within = iota((STRIP, STRIP), 0).astype(F32) * (level / STRIP) - shift
    inside = (within >= 0.0) & (within < 1.0)
    return jnp.where(inside, jnp.where(within < half, 1.0, -1.0), 0.0).astype(BF16)


def haar_scales():
    coef = iota((1, STRIP), 1)
    out = jnp.full((1, STRIP), math.sqrt(1.0 / STRIP), F32)
    m = 1
    while m < STRIP:
        out = jnp.where((coef >= m) & (coef < 2 * m), math.sqrt(m / STRIP), out)
        m *= 2
    return out


def top_entry(spot, index, strips):
    if index == 0:
        return jnp.full(spot.shape, math.sqrt(1.0 / strips), F32)
    m = 1 << (index.bit_length() - 1)
    span = strips // m
    start = float((index - m) * span)
    half = start + span / 2
    end = start + span
    scale = math.sqrt(m / strips)
    positive = (spot >= start) & (spot < half)
    negative = (spot >= half) & (spot < end)
    return jnp.where(positive, scale, jnp.where(negative, -scale, 0.0))


def weekly(rows, sectors):
    return [sum(rows[w * sectors + 1 : (w + 1) * sectors], rows[w * sectors]) for w in range(WIN)]


def scan_back(totals, decay):
    running = totals[WIN - 1]
    out = [running]
    for w in range(WIN - 2, -1, -1):
        running = running * decay + totals[w]
        out.insert(0, running)
    return out


def scan_ahead(totals, decay):
    running = totals[0]
    out = [running]
    for w in range(1, WIN):
        running = running * decay + totals[w]
        out.append(running)
    return out


def pick(rows, index):
    out = rows[0]
    for w in range(1, len(rows)):
        out = jnp.where(index == w, rows[w], out)
    return out


def background(first, partials, decay, sectors):
    pairs = range(WIN * sectors)
    counts = weekly([first[t, COUNTS : COUNTS + 1, :] for t in pairs], sectors)
    sums = weekly([first[t, SUMS : SUMS + 1, :] for t in pairs], sectors)
    carried = scan_ahead(partials, decay)
    back = [
        SOUNDS * partials[w] + (SOUNDS * counts[w]) * carried[w] - sums[w] for w in range(WIN)
    ]
    returned = scan_back(back, decay)
    return [carried[w] + returned[w] / SOUNDS for w in range(WIN)], carried


def one_hot_bands(band_col):
    return jnp.where(band_col == iota((band_col.shape[0], NBANDS), 1).astype(F32), 1.0, 0.0)


def forward(point, blocks_ref, mix):
    total = None
    for k in range(SLOTS):
        product = blocks_ref[k * SOUNDS : (k + 1) * SOUNDS, :] * point[k : k + 1, :]
        values = jnp.sum(product[:, :LANES] + product[:, LANES:], axis=1, keepdims=True)
        term = values * mix[k : k + 1, :]
        total = term if total is None else total + term
    return total


def back_rows(chosen, blocks_ref):
    return [
        jnp.sum(
            blocks_ref[k * SOUNDS : (k + 1) * SOUNDS, :] * chosen[:, k : k + 1],
            axis=0,
            keepdims=True,
        )
        for k in range(SLOTS)
    ]


def stack_rows(rows):
    at = iota((SLOTS, STRIP), 0)
    out = jnp.broadcast_to(rows[0], (SLOTS, STRIP))
    for k in range(1, SLOTS):
        out = jnp.where(at == k, rows[k], out)
    return out


def mix_rows(match, rows):
    out = match[:, 0:1] * rows[0]
    for k in range(1, SLOTS):
        out = out + match[:, k : k + 1] * rows[k]
    return out


def along_lanes(col):
    n = col.shape[0]
    here = iota((n, LANES), 0) == iota((n, LANES), 1)
    return jnp.sum(jnp.where(here, col, 0.0), axis=0, keepdims=True)


def open_kernel(
    strips,
    owners,
    band_in,
    obs_in,
    row_in,
    col_in,
    weight_in,
    decay_in,
    jac_in,
    count_ref,
    band_ref,
    obs_ref,
    weight_ref,
    decay_ref,
    blocks_ref,
    column_ref,
    twin_ref,
    start_grad_ref,
    obs_slot_ref,
    mix_ref,
    info_ref,
    limit_ref,
    limit_rows_ref,
    send_ref,
    strip_match_ref,
    top_matrix_ref,
    rank_ref,
    message_ref,
    row_ref,
    col_ref,
    jac_ref,
    sems,
):
    half = SLOTS * SOUNDS // 2
    moves = [
        (band_in, band_ref),
        (obs_in, obs_ref),
        (row_in, row_ref),
        (col_in, col_ref),
        (weight_in, weight_ref),
        (decay_in, decay_ref),
        (jac_in.at[:half], jac_ref.at[:half]),
        (jac_in.at[half:], jac_ref.at[half:]),
    ]
    copies = [pltpu.make_async_copy(a, b, sems.at[i]) for i, (a, b) in enumerate(moves)]
    for copy in copies:
        copy.start()
    sectors = strips // SEC_STRIPS
    strips_owner = NLAT * SEC_STRIPS // owners
    sector = lax.rem(lax.axis_index("tile"), sectors).astype(F32)
    signs = haar_signs()
    scales = haar_scales()
    for copy in copies[:6]:
        copy.wait()

    band_row = band_ref[...].astype(F32)
    block_hot = one_hot_bands(to_col(band_row))
    counted = jnp.sum(block_hot, axis=0, keepdims=True)
    summed = jnp.sum(block_hot * jnp.sum(obs_ref[...], axis=1, keepdims=True), axis=0, keepdims=True)
    row_of = to_col(row_ref[...].astype(F32))
    col_row = col_ref[...].astype(F32)
    col_of = to_col(col_row)
    valid = jnp.where(iota((SLOTS, 1), 0) < count_ref[0], 1.0, 0.0)
    valid_row = jnp.where(iota((1, SLOTS), 1) < count_ref[0], 1.0, 0.0)
    line = jnp.floor(col_of / SEC_STRIPS)
    spot = sector * SEC_STRIPS + (col_of - line * SEC_STRIPS)
    row_hot = jnp.where(row_of == iota((SLOTS, SB_DEV), 1).astype(F32), 1.0, 0.0)
    band = jnp.sum(row_hot * band_row, axis=1, keepdims=True)
    band = jnp.where(valid > 0.0, band, -1.0)
    lane = iota((1, LANES), 1)
    wanted = jnp.where(lane < SLOTS, along_lanes(row_of), -1.0)
    wanted_hot = jnp.where(iota((SB_DEV, LANES), 0).astype(F32) == wanted, 1.0, 0.0)
    obs_slot = exact_dot(obs_ref[...].T, wanted_hot)
    obs_slot_ref[...] = obs_slot
    block_lane = (lane >= MISFIT) & (lane < MISFIT + SB_DEV)
    wanted = jnp.where(block_lane, (lane - MISFIT).astype(F32), wanted)
    mix_ref[...] = jnp.where(row_of == wanted, valid, 0.0)

    same = jnp.where(col_of == col_row, 1.0, 0.0)
    before = jnp.where(iota((SLOTS, SLOTS), 1) < iota((SLOTS, SLOTS), 0), 1.0, 0.0)
    other = jnp.where(iota((SLOTS, SLOTS), 1) != iota((SLOTS, SLOTS), 0), same, 0.0)
    strip_match_ref[...] = same * valid_row
    first = jnp.where(jnp.sum(same * before, axis=1, keepdims=True) > 0.0, 0.0, 1.0)
    owner = jnp.floor(col_of / strips_owner)
    owner_row = jnp.floor(col_row / strips_owner)
    rank = jnp.sum(jnp.where(owner == owner_row, before, 0.0), axis=1, keepdims=True)

    at = iota((SLOTS, LANES), 1)
    rank_ref[...] = jnp.where(at == 0, rank, jnp.where(at == 1, first, 0.0))
    info = jnp.zeros((SLOTS, LANES), F32)
    for place, values in ((LINE, line), (SPOT, spot), (BAND, band), (COL, col_of), (VALID, valid)):
        info = jnp.where(at == place, values, info)
    info_ref[...] = info
    matrix = jnp.zeros((SLOTS, LANES), F32)
    for t in range(strips):
        matrix = jnp.where(at == t, top_entry(spot, t, strips), matrix)
    top_matrix_ref[...] = matrix

    local = iota((1, LANES), 1)
    limits_low = jnp.zeros((SLOTS, LANES), F32)
    limits_high = jnp.zeros((SLOTS, LANES), F32)
    for j in range(strips):
        low_row = jnp.zeros((1, LANES), F32)
        m = 1
        while m < LANES:
            start = strips * m + j * m
            block = weight_ref[0:1, start // LANES * LANES : start // LANES * LANES + LANES]
            shift = (m - start % LANES) % LANES
            moved = pltpu.roll(jnp.broadcast_to(block, (ROWS, LANES)), shift, 1)[0:1] if shift else block
            low_row = jnp.where((local >= m) & (local < 2 * m), moved, low_row)
            m *= 2
        high_row = weight_ref[0:1, (strips + j) * LANES : (strips + j + 1) * LANES]
        limit_rows_ref[j : j + 1, :] = STEP * low_row
        limit_rows_ref[strips + j : strips + j + 1, :] = STEP * high_row
        limits_low = jnp.where(spot == float(j), low_row, limits_low)
        limits_high = jnp.where(spot == float(j), high_row, limits_high)
    limit_ref[:, :LANES] = STEP * limits_low
    limit_ref[:, LANES:] = STEP * limits_high

    shape = (owners * ROWS, 3 * 4 * SLOTS)
    target = (iota(shape, 0) // ROWS).astype(F32)
    kind = iota(shape, 0) % ROWS
    place = iota(shape, 1) % (4 * SLOTS)
    group = place // SLOTS
    slim_shape = (SLOTS, shape[1])
    slim = iota(slim_shape, 1) % SLOTS == iota(slim_shape, 0)
    owner_wide = jnp.sum(jnp.where(slim, owner, 0.0), axis=0, keepdims=True)
    rank_wide = jnp.sum(jnp.where(slim, rank, 0.0), axis=0, keepdims=True)
    kind_f = kind.astype(F32)
    hit = (group == 0) & (kind_f == 2.0 * rank_wide)
    hit = hit | ((group == 1) & (kind_f == 2.0 * rank_wide + 1.0))
    hit = hit | ((group == 2) & (kind == 5))
    hit = (hit & (owner_wide == target)) | ((place == 3 * SLOTS) & (kind == 4))
    send = jnp.where(hit, 1.0, 0.0).astype(BF16)
    send_ref[...] = send

    at_f = at.astype(F32)
    base = rank * (LANES // 2)
    meta = jnp.where(at_f == base, col_of - owner * strips_owner + 1.0, 0.0)
    meta = jnp.where(at_f == base + 1.0, band + 1.0, meta)

    per = SLOTS // 2
    grads = []
    ones = []
    for part in range(2):
        copies[6 + part].wait()
        for start in range(part * half, part * half + half, STRIP):
            high, low = split(jac_ref[start : start + STRIP, :])
            blocks_ref[start : start + STRIP, :] = (dot(high, signs) + dot(low, signs)) * scales
        for k in range(part * per, part * per + per):
            block = blocks_ref[k * SOUNDS : (k + 1) * SOUNDS, :]
            grads.append(jnp.sum(block * obs_slot[:, k : k + 1], axis=0, keepdims=True))
            ones.append(jnp.sum(block, axis=0, keepdims=True))
    obs_grad = -stack_rows(grads)
    column = stack_rows(ones) * valid
    column_ref[...] = column
    start_grad_ref[...] = mix_rows(same * valid_row, [-g for g in grads])
    twin_ref[...] = mix_rows(other, [column[k : k + 1, :] for k in range(SLOTS)])

    slots = jnp.zeros((1, LANES), F32)
    for base, values in (
        (S_STRIP, col_of),
        (S_SPOT, spot),
        (S_BAND, band),
        (S_VALID, valid),
        (S_TOTAL, column[:, 0:1]),
        (S_APPROX, obs_grad[:, 0:1] * valid),
    ):
        slots = slots + moved_lanes(along_lanes(values), base)
    group = message_rows(send, column, meta, None).reshape(owners, ROWS, LANES)
    kind = iota((owners, ROWS, LANES), 1)
    for at_kind, row in ((4, counted), (6, summed), (7, slots)):
        group = jnp.where(kind == at_kind, row.reshape(1, 1, LANES), group)
    message_ref[:, GROUP:, :] = group
    for t in range(owners):
        lanes = slice(t % 2 * LANES, t % 2 * LANES + LANES)
        message_ref[t, GRADS : GRADS + SLOTS, :] = obs_grad[:, lanes]
        message_ref[t, COLUMNS : COLUMNS + SLOTS, :] = column[:, lanes]


def moved_lanes(row, by):
    by = by % LANES
    return pltpu.roll(jnp.broadcast_to(row, (ROWS, LANES)), by, 1)[0:1] if by else row


def window_row(rows, base):
    lane = iota((1, LANES), 1)
    out = jnp.zeros((1, LANES), F32)
    for i, row in enumerate(rows):
        inside = (lane >= i * SLOTS) & (lane < (i + 1) * SLOTS)
        out = jnp.where(inside, moved_lanes(row, i * SLOTS - base), out)
    return out


def thrice(match):
    return jnp.concatenate([match] * 3, axis=1).astype(BF16)


def message_rows(send, strips_part, meta, partial):
    if partial is None:
        bottom = jnp.zeros((SLOTS, LANES), F32)
    else:
        bottom = jnp.where(iota((SLOTS, LANES), 0) == 0, partial, 0.0)
    stacked = jnp.concatenate([strips_part[:, :LANES], strips_part[:, LANES:], meta, bottom], axis=0)
    return dot(send, split_rows(stacked))


def side_by_side(rows):
    out = rows[0]
    for i, row in enumerate(rows[1:], 1):
        wide = jnp.broadcast_to(row, (ROWS, LANES))
        out = out + pltpu.roll(wide, i * SLOTS, 1)[0:1]
    return out


def slot_scalars(hot, scalar):
    col = jnp.sum(hot * scalar, axis=1, keepdims=True)
    return col, along_lanes(col)


def advance(strips, col, row, grads, column, twin, same, approx_row, total_row, line_tops):
    other = jnp.sum(jnp.where(same > 0.0, row[:, :SLOTS], 0.0), axis=1, keepdims=True)
    full = grads + col[:SLOTS] * column + other * twin
    sources = approx_row + row * total_row
    at = iota((SLOTS, LANES), 1)
    top_grad = jnp.zeros((SLOTS, LANES), F32)
    for t in range(strips):
        value = jnp.sum(line_tops[t * SLOTS : (t + 1) * SLOTS] * sources, axis=1, keepdims=True)
        top_grad = jnp.where(at == t, value, top_grad)
    return full, top_grad


def with_approx(point, top, matrix):
    approx = jnp.sum(matrix * top, axis=1, keepdims=True)
    return jnp.where(iota((SLOTS, STRIP), 1) == 0, approx, point)


def band_partial(point, column, hot):
    dots = jnp.sum(point * column, axis=1, keepdims=True)
    return jnp.sum(hot * dots, axis=0, keepdims=True) / SOUNDS


def twins(strip_match):
    return jnp.where(iota((SLOTS, SLOTS), 0) == iota((SLOTS, SLOTS), 1), 0.0, strip_match)


def everyones_step(strips, owners, first_ref, scalars, limit_rows_ref, top_limit, share_ref):
    sectors = strips // SEC_STRIPS
    odd = lax.rem(lax.axis_index("tile"), 2)
    lane = iota((1, LANES), 1)
    count = sectors * SLOTS
    slots = first_ref[:, SLOT_ROW, :]
    tall = slots.T

    def col(base):
        return jnp.concatenate([tall[base : base + SLOTS, d : d + 1] for d in range(owners)], axis=0)

    def rows(base):
        turned = []
        for i in range(sectors):
            by = (i * SLOTS - base) % LANES
            turned.append(pltpu.roll(slots, by, 1) if by else slots)
        out = []
        for w in range(WIN):
            row = turned[0][w * sectors : w * sectors + 1, :]
            for i in range(1, sectors):
                d = w * sectors + i
                row = jnp.where(lane >= i * SLOTS, turned[i][d : d + 1, :], row)
            out.append(row[:, :count])
        return out

    def part(values, w):
        return values[w * count : (w + 1) * count]

    strip = col(S_STRIP)
    spot = col(S_SPOT)
    hot = one_hot_bands(col(S_BAND))
    spread = jnp.concatenate([jnp.broadcast_to(s, (count, NBANDS)) for s in scalars], axis=0)
    along = jnp.sum(hot * spread, axis=1, keepdims=True)
    column = first_ref[:, COLUMNS : COLUMNS + SLOTS, :].reshape(owners * SLOTS, LANES)
    grads = first_ref[:, GRADS : GRADS + SLOTS, :].reshape(owners * SLOTS, LANES) + along * column
    matrix = jnp.zeros((owners * SLOTS, LANES), F32)
    limit = jnp.zeros((owners * SLOTS, LANES), F32)
    for j in range(strips):
        entries = jnp.zeros((1, LANES), F32)
        for t in range(strips):
            entries = jnp.where(lane == t, top_value(j, t, strips), entries)
        low, high = limit_rows_ref[j : j + 1, :], limit_rows_ref[strips + j : strips + j + 1, :]
        here = spot == float(j)
        matrix = jnp.where(here, entries, matrix)
        limit = jnp.where(here, jnp.where(odd == 0, low, high), limit)
    fronts = (grads[:, 0:1] * col(S_VALID)) * matrix
    parts = split(jnp.concatenate([grads, fronts], axis=1))
    strip_rows = rows(S_STRIP)
    spot_rows = rows(S_SPOT)
    valid_rows = rows(S_VALID)
    full = []
    top_grad = []
    for w in range(WIN):
        line = jnp.floor(part(strip, w) / SEC_STRIPS)
        same_line = line == jnp.floor(strip_rows[w] / SEC_STRIPS)
        same_strip = same_line & (part(spot, w) == spot_rows[w])
        match = jnp.concatenate(
            [jnp.where(same_strip, valid_rows[w], 0.0), jnp.where(same_line, 1.0, 0.0)], axis=0
        ).astype(BF16)
        both = dot(match, part(parts[0], w)) + dot(match, part(parts[1], w))
        full.append(both[:count, :LANES])
        top_grad.append(both[count:, LANES:])
    full = jnp.concatenate(full, axis=0)
    top = shrink(-STEP * jnp.concatenate(top_grad, axis=0), top_limit)
    approx = jnp.sum(matrix * top, axis=1, keepdims=True)
    point = shrink(-STEP * full, limit)
    point = jnp.where((lane == 0) & (odd == 0), approx, point)
    dots = jnp.sum(point * column, axis=1, keepdims=True)
    weighed = hot * dots
    for w in range(WIN):
        share_ref[w : w + 1, :] = jnp.sum(part(weighed, w), axis=0, keepdims=True) / SOUNDS


def window_slots(first_ref, sectors):
    my_index = lax.axis_index("tile")
    base = my_index - lax.rem(my_index, sectors)
    rows = []
    for shift in range(sectors):
        pair = base + lax.rem(my_index - base + (sectors - shift), sectors)
        rows.append(first_ref[pair, SLOT_ROW : SLOT_ROW + 1, :])
    return rows


def first_step_kernel(
    strips,
    owners,
    first_ref,
    info_ref,
    column_ref,
    twin_ref,
    grad_ref,
    limit_ref,
    limit_rows_ref,
    strip_match_ref,
    top_matrix_ref,
    decay_ref,
    weight_ref,
    blocks_ref,
    mix_ref,
    obs_slot_ref,
    point_ref,
    top_ref,
    share_ref,
    hot_ref,
    line_tops_ref,
    grad_out_ref,
    lead_ref,
):
    sectors = strips // SEC_STRIPS
    my_index = lax.axis_index("tile")
    window = my_index // sectors
    top_limit = STEP * weight_ref[0:1, :LANES]
    sums = weekly([first_ref[t, SUMS : SUMS + 1, :] for t in range(owners)], sectors)
    scalars = [r / SOUNDS for r in scan_back([-s for s in sums], decay_ref[...])]
    everyones_step(strips, owners, first_ref, scalars, limit_rows_ref, top_limit, share_ref)

    info = info_ref[...]
    slots = window_slots(first_ref, sectors)
    lane = iota((1, LANES), 1)
    count = sectors * SLOTS
    hot = one_hot_bands(to_col(window_row(slots, S_BAND)[:, :count]))
    hot_ref[...] = hot
    spot_row = window_row(slots, S_SPOT)
    line_row = jnp.where(lane < count, jnp.floor(window_row(slots, S_STRIP) / SEC_STRIPS), -1.0)
    on_line = info[:, LINE : LINE + 1] == line_row
    line_tops = jnp.concatenate(
        [jnp.where(on_line, top_entry(spot_row, t, strips), 0.0) for t in range(strips)], axis=0
    )
    line_tops_ref[...] = line_tops
    column = column_ref[...]
    col, along = slot_scalars(hot, pick(scalars, window))
    grads, top_grad = advance(
        strips,
        col,
        along,
        grad_ref[...],
        column,
        twin_ref[...],
        twins(strip_match_ref[...]),
        window_row(slots, S_APPROX),
        window_row(slots, S_TOTAL),
        line_tops,
    )
    updated = shrink(-STEP * grads, limit_ref[...])
    top = shrink(-STEP * top_grad, top_limit)
    point = with_approx(updated, top, top_matrix_ref[...])
    point_ref[...] = point
    top_ref[...] = top
    chosen = forward(point, blocks_ref, mix_ref[...]) - obs_slot_ref[...]
    rows = back_rows(chosen, blocks_ref)
    grad_out_ref[...] = mix_rows(strip_match_ref[...], rows)
    at = iota((SLOTS, LANES), 0)
    fronts = jnp.broadcast_to(rows[0][:, :LANES], (SLOTS, LANES))
    for k in range(1, SLOTS):
        fronts = jnp.where(at == k, rows[k][:, :LANES], fronts)
    share_ref[WIN : WIN + 1, :] = along_lanes(fronts[:, 0:1] * info[:, VALID : VALID + 1])
    share_ref[WIN + 1 :, :] = jnp.zeros((ROWS - 1, LANES), F32)

    sector = lax.rem(my_index, sectors).astype(F32)
    sector_row = jnp.floor(spot_row / SEC_STRIPS)
    lane = iota((SLOTS, LANES), 1)
    before = jnp.where(lane < iota((SLOTS, LANES), 0), 1.0, 0.0)
    earlier = jnp.where(lane < SLOTS, before, jnp.where(sector_row < sector, 1.0, 0.0))
    taken = jnp.sum(jnp.where(on_line, earlier, 0.0), axis=1, keepdims=True)
    lead_ref[...] = jnp.broadcast_to(jnp.where(taken > 0.0, 0.0, 1.0), lead_ref.shape)


def second_step_kernel(
    strips,
    owners,
    beta,
    first_ref,
    info_ref,
    column_ref,
    twin_ref,
    grad_ref,
    limit_ref,
    strip_match_ref,
    top_matrix_ref,
    decay_ref,
    weight_ref,
    hot_ref,
    line_tops_ref,
    lead_ref,
    rank_ref,
    send_ref,
    point_ref,
    top_ref,
    blocks_ref,
    mix_ref,
    obs_slot_ref,
    *rest,
):
    sectors = strips // SEC_STRIPS
    shares, rest = rest[:sectors], rest[sectors:]
    message_ref, values_ref = rest
    my_index = lax.axis_index("tile")
    window = my_index // sectors
    odd = lax.rem(my_index, 2)
    totals = shares[0][0:WIN, :] + jnp.where(odd == 1, shares[1][0:WIN, :], shares[-1][0:WIN, :])
    combined, _ = background(first_ref, [totals[w : w + 1, :] for w in range(WIN)], decay_ref[...], sectors)
    hot = hot_ref[...]
    column = column_ref[...]
    col, along = slot_scalars(hot, pick(combined, window))
    grads, top_grad = advance(
        strips,
        col,
        along,
        grad_ref[...],
        column,
        twin_ref[...],
        twins(strip_match_ref[...]),
        side_by_side([share[WIN : WIN + 1, :] for share in shares]),
        window_row(window_slots(first_ref, sectors), S_TOTAL),
        line_tops_ref[...],
    )
    old = point_ref[...]
    old_top = top_ref[...]
    updated = shrink(old - STEP * grads, limit_ref[...])
    top = shrink(old_top - STEP * top_grad, STEP * weight_ref[0:1, :LANES])
    point = updated + beta * (updated - old)
    top = top + beta * (top - old_top)
    point = with_approx(point, top, top_matrix_ref[...])
    values = forward(point, blocks_ref, mix_ref[...])
    values_ref[...] = values
    grad = stack_rows(back_rows(values - obs_slot_ref[...], blocks_ref))

    partial = band_partial(point, column, hot[:SLOTS])
    info = info_ref[...]
    valid = info[:, VALID : VALID + 1]
    top = top * lead_ref[:, 0:1]
    rank = rank_ref[:, 0:1]
    meta = jnp.where(rank == 0.0, pltpu.roll(top, ROWS, 1), pltpu.roll(top, LANES // 2 + ROWS, 1))
    kept = jnp.where(iota((SLOTS, STRIP), 1) == 0, 0.0, point * rank_ref[:, 1:2])
    rows = message_rows(send_ref[...], kept - STEP * (valid * grad), meta, partial)
    message_ref[...] = rows.reshape(message_ref.shape)


def placing(strips, owners, first_ref, values_ref, obs_ref, band_ref):
    sectors = strips // SEC_STRIPS
    lines = NLAT // owners
    count = owners * ROWS
    meta = first_ref[:, META, :]
    wide = (owners, count)
    pair_of = iota(wide, 1) // ROWS == iota(wide, 0)
    kind = iota((1, count), 1) % ROWS
    tall = (count, owners)
    tall_pair = iota(tall, 0) // ROWS == iota(tall, 1)
    tall_kind = iota((count, 1), 0) % ROWS
    strip_rows = []
    band_col = jnp.zeros((count, 1), F32)
    for q in range(2):
        strip = meta[:, q * (LANES // 2) : q * (LANES // 2) + 1]
        band = meta[:, q * (LANES // 2) + 1 : q * (LANES // 2) + 2]
        strip_rows.append(jnp.sum(jnp.where(pair_of, strip, 0.0), axis=0, keepdims=True) - 1.0)
        band_tall = jnp.sum(jnp.where(tall_pair, to_row(band), 0.0), axis=1, keepdims=True)
        band_col = jnp.where(tall_kind // 2 == q, band_tall, band_col)
    band_hot = one_hot_bands(band_col - 1.0)
    scaled = jnp.where(tall_kind < 4, STEP * first_ref[:, GROUP:, :].reshape(count, LANES), 0.0)

    def line_of(strip):
        return jnp.floor(strip / SEC_STRIPS)

    blocks = lines * WIN
    pair = iota((1, count), 1) // ROWS
    window = pair // sectors
    sector = (pair - window * sectors).astype(F32)
    line_col = (iota((blocks, 1), 0) // WIN).astype(F32)
    window_col = iota((blocks, 1), 0) % WIN
    strip_row = jnp.where(kind < 2, strip_rows[0], strip_rows[1])
    slot_line = line_of(strip_row)
    slot_spot = sector * SEC_STRIPS + strip_row - slot_line * SEC_STRIPS
    base = (window == window_col) & (slot_line == line_col) & (strip_row >= 0.0)
    base = jnp.where(base & (kind < 4), 1.0, 0.0)
    parts = []
    for half in range(2):
        part = jnp.where(kind % 2 == half, base, 0.0)
        for j in range(strips):
            parts.append(jnp.where(slot_spot == float(j), part, 0.0))
    for q in range(2):
        hit = (window == window_col) & (line_of(strip_rows[q]) == line_col) & (strip_rows[q] >= 0.0) & (kind == 5)
        parts.append(jnp.where(hit, 1.0, 0.0))
    place = jnp.concatenate(parts, axis=0).astype(BF16)
    place = jnp.concatenate([place, place, place], axis=1)

    differ = values_ref[...].T[MISFIT : MISFIT + SB_DEV, :] - obs_ref[...]
    block_hot = one_hot_bands(to_col(band_ref[...].astype(F32)))
    return place, band_hot, scaled, differ, block_hot


def finish_kernel(
    strips,
    owners,
    first_ref,
    third_ref,
    values_ref,
    obs_ref,
    band_ref,
    decay_ref,
    weight_ref,
    out_ref,
    misfit_ref,
):
    sectors = strips // SEC_STRIPS
    blocks = NLAT // owners * WIN
    count = owners * ROWS
    window = lax.axis_index("tile") // sectors
    place, band_hot, scaled, differ, block_hot = placing(
        strips, owners, first_ref, values_ref, obs_ref, band_ref
    )
    partials = weekly([third_ref[t, 4:5, :] for t in range(owners)], sectors)
    combined, carried = background(first_ref, partials, decay_ref[...], sectors)
    spread = jnp.concatenate(
        [jnp.broadcast_to(row, (sectors * ROWS, NBANDS)) for row in combined], axis=0
    )
    scalars = jnp.sum(band_hot * spread, axis=1, keepdims=True)
    rows = third_ref[...].reshape(count, LANES) - scalars * scaled
    placed = dot(place, split_rows(rows))
    offset = jnp.sum(block_hot * pick(carried, window), axis=1, keepdims=True)
    misfit_ref[...] = differ + offset

    lane = iota((1, LANES), 1)
    for j in range(strips):
        start = (strips + j) * LANES
        values = placed[(strips + j) * blocks : (strips + j + 1) * blocks]
        out_ref[:, start : start + LANES] = shrink(values, STEP * weight_ref[0:1, start : start + LANES])

    low = [placed[j * blocks : (j + 1) * blocks] for j in range(strips)]
    tops = [placed[(2 * strips + q) * blocks : (2 * strips + q + 1) * blocks] for q in range(2)]
    top = pltpu.roll(tops[0], LANES - ROWS, 1) + pltpu.roll(tops[1], LANES // 2 - ROWS, 1)
    made = [jnp.zeros((blocks, LANES), F32) for _ in range(strips)]
    for t in range(strips):
        value = jnp.zeros((blocks, 1), F32)
        for j in range(strips):
            entry = top_value(j, t, strips)
            if entry:
                value = value + entry * low[j][:, 0:1]
        made[0] = jnp.where(lane == t, value + top, made[0])
    m = 1
    while m < LANES:
        for j in range(strips):
            start = strips * m + j * m
            block = start // LANES
            shift = (start % LANES - m) % LANES
            moved = pltpu.roll(low[j], shift, 1) if shift else low[j]
            inside = (lane >= start % LANES) & (lane < start % LANES + m)
            made[block] = jnp.where(inside, moved, made[block])
        m *= 2
    for block in range(strips):
        start = block * LANES
        out_ref[:, start : start + LANES] = shrink(made[block], STEP * weight_ref[0:1, start : start + LANES])


def top_value(spot, index, strips):
    if index == 0:
        return math.sqrt(1.0 / strips)
    m = 1 << (index.bit_length() - 1)
    span = strips // m
    within = spot - (index - m) * span
    if within < 0 or within >= span:
        return 0.0
    return math.sqrt(m / strips) * (1.0 if within < span // 2 else -1.0)


def call(kernel, outs, *operands, **kwargs):
    return pl.pallas_call(
        kernel,
        out_shape=[jax.ShapeDtypeStruct(shape, dtype) for shape, dtype in outs],
        compiler_params=pltpu.CompilerParams(vmem_limit_bytes=40 * 1024 * 1024),
        **kwargs,
    )(*operands)


def body(
    observations,
    jacobian,
    block_row,
    block_col,
    block_count,
    block_band,
    carry_decay,
    sparsity_weight,
):
    owners = lax.axis_size("tile")
    sectors = owners // WIN
    strips = sectors * SEC_STRIPS
    lines = NLAT // owners
    betas = momentum_weights(ITERS)
    arguments = [
        block_band.reshape(1, SB_DEV),
        observations,
        block_row.reshape(1, SLOTS),
        block_col.reshape(1, SLOTS),
        sparsity_weight.reshape(1, -1),
        carry_decay.reshape(1, NBANDS),
        jacobian.reshape(SLOTS * SOUNDS, STRIP),
    ]
    message = ((owners, ROWS, LANES), F32)
    narrow = ((SLOTS, LANES), F32)
    strip_rows = ((SLOTS, STRIP), F32)

    def trade(values):
        return lax.all_to_all(values, "tile", 0, 0, tiled=True)

    def with_sectors(values):
        found = [values]
        for shift in range(1, sectors):
            pairs = [
                (d, d // sectors * sectors + (d + shift) % sectors) for d in range(owners)
            ]
            found.append(lax.ppermute(values, "tile", pairs))
        return found

    arguments = [pltpu.with_memory_space_constraint(a, pltpu.HBM) for a in arguments]
    outs = [
        ((1, SB_DEV), jnp.int32),
        ((SB_DEV, SOUNDS), F32),
        ((1, strips * STRIP), F32),
        ((1, NBANDS), F32),
        ((SLOTS * SOUNDS, STRIP), F32),
        strip_rows,
        strip_rows,
        strip_rows,
        ((SOUNDS, LANES), F32),
        narrow,
        narrow,
        strip_rows,
        ((2 * strips, LANES), F32),
        ((owners * ROWS, 3 * 4 * SLOTS), BF16),
        ((SLOTS, SLOTS), F32),
        narrow,
        narrow,
        ((owners, FIRST_ROWS, LANES), F32),
    ]
    (
        bands,
        observed,
        weight,
        decay,
        blocks,
        column,
        twin,
        start_grad,
        obs_slot,
        mix,
        info,
        limit,
        limit_rows,
        send,
        strip_match,
        top_matrix,
        rank,
        first,
    ) = call(
        functools.partial(open_kernel, strips, owners),
        outs,
        *arguments,
        block_count,
        in_specs=[pl.BlockSpec(memory_space=pltpu.HBM)] * len(arguments)
        + [pl.BlockSpec(memory_space=pltpu.SMEM)],
        scratch_shapes=[
            pltpu.VMEM((1, SLOTS), jnp.int32),
            pltpu.VMEM((1, SLOTS), jnp.int32),
            pltpu.VMEM((SLOTS * SOUNDS, STRIP), F32),
            pltpu.SemaphoreType.DMA((len(arguments) + 1,)),
        ],
    )
    first = trade(first)
    point, top, share, hot, line_tops, grad, lead = call(
        functools.partial(first_step_kernel, strips, owners),
        [
            strip_rows,
            narrow,
            ((2 * ROWS, LANES), F32),
            ((sectors * SLOTS, NBANDS), F32),
            ((strips * SLOTS, LANES), F32),
            strip_rows,
            narrow,
        ],
        first,
        info,
        column,
        twin,
        start_grad,
        limit,
        limit_rows,
        strip_match,
        top_matrix,
        decay,
        weight,
        blocks,
        mix,
        obs_slot,
    )
    third, values = call(
        functools.partial(second_step_kernel, strips, owners, betas[1]),
        [message, ((SOUNDS, LANES), F32)],
        first,
        info,
        column,
        twin,
        grad,
        limit,
        strip_match,
        top_matrix,
        decay,
        weight,
        hot,
        line_tops,
        lead,
        rank,
        send,
        point,
        top,
        blocks,
        mix,
        obs_slot,
        *with_sectors(share),
    )
    third = trade(third)
    coeffs, misfit = call(
        functools.partial(finish_kernel, strips, owners),
        [((lines * WIN, strips * STRIP), F32), ((SB_DEV, SOUNDS), F32)],
        first,
        third,
        values,
        observed,
        bands,
        decay,
        weight,
    )
    return (coeffs.reshape(lines, WIN, strips * STRIP), misfit)


def solution(mesh):
    return jax.shard_map(
        body,
        mesh=mesh,
        in_specs=(
            P(("ens", "tile"), None),
            P("tile", None, None),
            P("tile"),
            P("tile"),
            P("tile"),
            P("tile"),
            P(),
            P(),
        ),
        out_specs=(P(("ens", "tile"), None, None), P(("ens", "tile"), None)),
        check_vma=False,
    )
```

```python
import functools
import math

import jax
import jax.numpy as jnp
from jax import lax
from jax.experimental import pallas as pl
from jax.experimental.pallas import tpu as pltpu
from jax.sharding import PartitionSpec as P

WIN = 8
NLAT = 64
SEC_STRIPS = 2
STRIP = 256
SOUNDS = 64
SB_DEV = 32
NBANDS = 128
ITERS = 3
SLOTS = 16
LANES = 128
ROWS = 8
STEP = 0.2
MISFIT = 32
PARTS = 6
PIECES = 1

F32 = jnp.float32
BF16 = jnp.bfloat16
HIGHEST = lax.Precision.HIGHEST

LINE, SPOT, BAND, COL, VALID = range(5)
BLOCK = 4
GRADS, COLUMNS, SINGLES = 0, SLOTS // BLOCK, 2 * SLOTS // BLOCK
COUNTS, SUMS, SLOT_ROW = range(3)
FIRST_BLOCKS = SINGLES + 1
S_STRIP, S_SPOT, S_BAND, S_VALID, S_TOTAL, S_APPROX = (i * SLOTS for i in range(6))


def momentum_weights(total_steps):
    weights = []
    current = 1.0
    for _ in range(total_steps):
        following = (1.0 + math.sqrt(1.0 + 4.0 * current * current)) / 2.0
        weights.append((current - 1.0) / following)
        current = following
    return weights


def iota(shape, axis):
    return lax.broadcasted_iota(jnp.int32, shape, axis)


def shrink(values, limit):
    return values - jnp.minimum(jnp.maximum(values, -limit), limit)


def to_col(row):
    n = row.shape[1]
    eye = iota((n, n), 0) == iota((n, n), 1)
    return jnp.sum(jnp.where(eye, row, 0.0), axis=1, keepdims=True)


def to_row(col):
    n = col.shape[0]
    eye = iota((n, n), 0) == iota((n, n), 1)
    return jnp.sum(jnp.where(eye, col, 0.0), axis=0, keepdims=True)


def exact_dot(left, right):
    return jnp.dot(left, right, precision=HIGHEST, preferred_element_type=F32)


def dot(left, right):
    return jnp.dot(left, right, preferred_element_type=F32)


def dot_nt(left, right):
    return lax.dot_general(left, right, (((1,), (1,)), ((), ())), preferred_element_type=F32)


def split(values):
    high = values.astype(BF16)
    return high, (values - high.astype(F32)).astype(BF16)


def split_parts(values):
    high = values.astype(BF16)
    rest = values - high.astype(F32)
    middle = rest.astype(BF16)
    return [high, middle, (rest - middle.astype(F32)).astype(BF16)]


def split_rows(values):
    return jnp.concatenate(split_parts(values), axis=0)


def haar_signs():
    coef = iota((1, STRIP), 1).astype(F32)
    level = jnp.zeros((1, STRIP), F32) + 1.0
    m = 2
    while m < STRIP:
        level = jnp.where(coef >= m, float(m), level)
        m *= 2
    first = coef == 0.0
    shift = jnp.where(first, 0.0, coef - level)
    half = jnp.where(first, 2.0, 0.5)
    within = iota((STRIP, STRIP), 0).astype(F32) * (level / STRIP) - shift
    inside = (within >= 0.0) & (within < 1.0)
    return jnp.where(inside, jnp.where(within < half, 1.0, -1.0), 0.0).astype(BF16)


def haar_scales():
    coef = iota((1, STRIP), 1)
    out = jnp.full((1, STRIP), math.sqrt(1.0 / STRIP), F32)
    m = 1
    while m < STRIP:
        out = jnp.where((coef >= m) & (coef < 2 * m), math.sqrt(m / STRIP), out)
        m *= 2
    return out


def top_entry(spot, index, strips):
    if index == 0:
        return jnp.full(spot.shape, math.sqrt(1.0 / strips), F32)
    m = 1 << (index.bit_length() - 1)
    span = strips // m
    start = float((index - m) * span)
    half = start + span / 2
    end = start + span
    scale = math.sqrt(m / strips)
    positive = (spot >= start) & (spot < half)
    negative = (spot >= half) & (spot < end)
    return jnp.where(positive, scale, jnp.where(negative, -scale, 0.0))


def weekly(rows, sectors):
    return [sum(rows[w * sectors + 1 : (w + 1) * sectors], rows[w * sectors]) for w in range(WIN)]


def scan_back(totals, decay):
    running = totals[WIN - 1]
    out = [running]
    for w in range(WIN - 2, -1, -1):
        running = running * decay + totals[w]
        out.insert(0, running)
    return out


def scan_ahead(totals, decay):
    running = totals[0]
    out = [running]
    for w in range(1, WIN):
        running = running * decay + totals[w]
        out.append(running)
    return out


def pick(rows, index):
    out = rows[0]
    for w in range(1, len(rows)):
        out = jnp.where(index == w, rows[w], out)
    return out


def background(first, partials, decay, sectors):
    pairs = range(WIN * sectors)
    counts = weekly([first[t, SINGLES, COUNTS : COUNTS + 1, :] for t in pairs], sectors)
    sums = weekly([first[t, SINGLES, SUMS : SUMS + 1, :] for t in pairs], sectors)
    carried = scan_ahead(partials, decay)
    back = [
        SOUNDS * partials[w] + (SOUNDS * counts[w]) * carried[w] - sums[w] for w in range(WIN)
    ]
    returned = scan_back(back, decay)
    return [carried[w] + returned[w] / SOUNDS for w in range(WIN)], carried


def one_hot_bands(band_col):
    return jnp.where(band_col == iota((band_col.shape[0], NBANDS), 1).astype(F32), 1.0, 0.0)


def forward(point, blocks_ref, mix):
    total = None
    for k in range(SLOTS):
        product = blocks_ref[k * SOUNDS : (k + 1) * SOUNDS, :] * point[k : k + 1, :]
        values = jnp.sum(product[:, :LANES] + product[:, LANES:], axis=1, keepdims=True)
        term = values * mix[k : k + 1, :]
        total = term if total is None else total + term
    return total


def back_rows(chosen, blocks_ref):
    return [
        jnp.sum(
            blocks_ref[k * SOUNDS : (k + 1) * SOUNDS, :] * chosen[:, k : k + 1],
            axis=0,
            keepdims=True,
        )
        for k in range(SLOTS)
    ]


def stack_rows(rows):
    at = iota((SLOTS, STRIP), 0)
    out = jnp.broadcast_to(rows[0], (SLOTS, STRIP))
    for k in range(1, SLOTS):
        out = jnp.where(at == k, rows[k], out)
    return out


def mix_rows(match, rows):
    out = match[:, 0:1] * rows[0]
    for k in range(1, SLOTS):
        out = out + match[:, k : k + 1] * rows[k]
    return out


def along_lanes(col):
    n = col.shape[0]
    here = iota((n, LANES), 0) == iota((n, LANES), 1)
    return jnp.sum(jnp.where(here, col, 0.0), axis=0, keepdims=True)


def open_kernel(
    strips,
    owners,
    band_in,
    obs_in,
    row_in,
    col_in,
    weight_in,
    decay_in,
    jac_in,
    count_ref,
    band_ref,
    obs_ref,
    weight_ref,
    decay_ref,
    blocks_ref,
    column_ref,
    twin_ref,
    start_grad_ref,
    obs_slot_ref,
    mix_ref,
    info_ref,
    limit_ref,
    limit_rows_ref,
    send_ref,
    strip_match_ref,
    top_matrix_ref,
    rank_ref,
    message_ref,
    row_ref,
    col_ref,
    jac_ref,
    sems,
):
    piece = SLOTS * SOUNDS // PIECES
    moves = [
        (band_in, band_ref),
        (obs_in, obs_ref),
        (row_in, row_ref),
        (col_in, col_ref),
        (weight_in, weight_ref),
        (decay_in, decay_ref),
    ]
    for start in range(0, SLOTS * SOUNDS, piece):
        moves.append((jac_in.at[start : start + piece], jac_ref.at[start : start + piece]))
    copies = [pltpu.make_async_copy(a, b, sems.at[i]) for i, (a, b) in enumerate(moves)]
    for copy in copies:
        copy.start()
    sectors = strips // SEC_STRIPS
    strips_owner = NLAT * SEC_STRIPS // owners
    sector = lax.rem(lax.axis_index("tile"), sectors).astype(F32)
    signs = haar_signs()
    scales = haar_scales()
    for copy in copies[:6]:
        copy.wait()

    band_row = band_ref[...].astype(F32)
    block_hot = one_hot_bands(to_col(band_row))
    counted = jnp.sum(block_hot, axis=0, keepdims=True)
    summed = jnp.sum(block_hot * jnp.sum(obs_ref[...], axis=1, keepdims=True), axis=0, keepdims=True)
    row_of = to_col(row_ref[...].astype(F32))
    col_row = col_ref[...].astype(F32)
    col_of = to_col(col_row)
    valid = jnp.where(iota((SLOTS, 1), 0) < count_ref[0], 1.0, 0.0)
    valid_row = jnp.where(iota((1, SLOTS), 1) < count_ref[0], 1.0, 0.0)
    line = jnp.floor(col_of / SEC_STRIPS)
    spot = sector * SEC_STRIPS + (col_of - line * SEC_STRIPS)
    row_hot = jnp.where(row_of == iota((SLOTS, SB_DEV), 1).astype(F32), 1.0, 0.0)
    band = jnp.sum(row_hot * band_row, axis=1, keepdims=True)
    band = jnp.where(valid > 0.0, band, -1.0)
    lane = iota((1, LANES), 1)
    wanted = jnp.where(lane < SLOTS, along_lanes(row_of), -1.0)
    wanted_hot = jnp.where(iota((SB_DEV, LANES), 0).astype(F32) == wanted, 1.0, 0.0)
    obs_slot = exact_dot(obs_ref[...].T, wanted_hot)
    obs_slot_ref[...] = obs_slot
    block_lane = (lane >= MISFIT) & (lane < MISFIT + SB_DEV)
    wanted = jnp.where(block_lane, (lane - MISFIT).astype(F32), wanted)
    mix_ref[...] = jnp.where(row_of == wanted, valid, 0.0)

    same = jnp.where(col_of == col_row, 1.0, 0.0)
    before = jnp.where(iota((SLOTS, SLOTS), 1) < iota((SLOTS, SLOTS), 0), 1.0, 0.0)
    other = jnp.where(iota((SLOTS, SLOTS), 1) != iota((SLOTS, SLOTS), 0), same, 0.0)
    strip_match_ref[...] = same * valid_row
    first = jnp.where(jnp.sum(same * before, axis=1, keepdims=True) > 0.0, 0.0, 1.0)
    owner = jnp.floor(col_of / strips_owner)
    owner_row = jnp.floor(col_row / strips_owner)
    rank = jnp.sum(jnp.where(owner == owner_row, before, 0.0), axis=1, keepdims=True)

    at = iota((SLOTS, LANES), 1)
    rank_ref[...] = jnp.where(at == 0, rank, jnp.where(at == 1, first, 0.0))
    info = jnp.zeros((SLOTS, LANES), F32)
    for place, values in ((LINE, line), (SPOT, spot), (BAND, band), (COL, col_of), (VALID, valid)):
        info = jnp.where(at == place, values, info)
    info_ref[...] = info
    matrix = jnp.zeros((SLOTS, LANES), F32)
    for t in range(strips):
        matrix = jnp.where(at == t, top_entry(spot, t, strips), matrix)
    top_matrix_ref[...] = matrix

    local = iota((1, LANES), 1)
    limits_low = jnp.zeros((SLOTS, LANES), F32)
    limits_high = jnp.zeros((SLOTS, LANES), F32)
    for j in range(strips):
        low_row = jnp.zeros((1, LANES), F32)
        m = 1
        while m < LANES:
            start = strips * m + j * m
            block = weight_ref[0:1, start // LANES * LANES : start // LANES * LANES + LANES]
            shift = (m - start % LANES) % LANES
            moved = pltpu.roll(jnp.broadcast_to(block, (ROWS, LANES)), shift, 1)[0:1] if shift else block
            low_row = jnp.where((local >= m) & (local < 2 * m), moved, low_row)
            m *= 2
        high_row = weight_ref[0:1, (strips + j) * LANES : (strips + j + 1) * LANES]
        limit_rows_ref[j : j + 1, :] = STEP * low_row
        limit_rows_ref[strips + j : strips + j + 1, :] = STEP * high_row
        limits_low = jnp.where(spot == float(j), low_row, limits_low)
        limits_high = jnp.where(spot == float(j), high_row, limits_high)
    limit_ref[:, :LANES] = STEP * limits_low
    limit_ref[:, LANES:] = STEP * limits_high

    shape = (owners * ROWS, 3 * PARTS * SLOTS)
    target = (iota(shape, 0) // ROWS).astype(F32)
    kind = iota(shape, 0) % ROWS
    place = iota(shape, 1) % (PARTS * SLOTS)
    group = place // SLOTS
    slim_shape = (SLOTS, shape[1])
    slim = iota(slim_shape, 1) % SLOTS == iota(slim_shape, 0)
    owner_wide = jnp.sum(jnp.where(slim, owner, 0.0), axis=0, keepdims=True)
    rank_wide = jnp.sum(jnp.where(slim, rank, 0.0), axis=0, keepdims=True)
    kind_f = kind.astype(F32)
    hit = (group == 0) & (kind_f == 2.0 * rank_wide)
    hit = hit | ((group == 1) & (kind_f == 2.0 * rank_wide + 1.0))
    hit = hit | ((group == 2) & (kind == 5))
    even = iota(shape, 0) // ROWS % 2 == 0
    hit = hit | ((group == 4) & (kind_f == 6.0 + rank_wide) & ~even)
    hit = hit | ((group == 5) & (kind_f == 6.0 + rank_wide) & even)
    hit = (hit & (owner_wide == target)) | ((place == 3 * SLOTS) & (kind == 4))
    send = jnp.where(hit, 1.0, 0.0).astype(BF16)
    send_ref[...] = send

    per = SLOTS // PIECES
    grads = []
    ones = []
    for part in range(PIECES):
        copies[6 + part].wait()
        for start in range(part * piece, part * piece + piece, STRIP):
            high, low = split(jac_ref[start : start + STRIP, :])
            blocks_ref[start : start + STRIP, :] = (dot(high, signs) + dot(low, signs)) * scales
        for k in range(part * per, part * per + per):
            block = blocks_ref[k * SOUNDS : (k + 1) * SOUNDS, :]
            grads.append(jnp.sum(block * obs_slot[:, k : k + 1], axis=0, keepdims=True))
            ones.append(jnp.sum(block, axis=0, keepdims=True))
    obs_grad = -stack_rows(grads)
    column = stack_rows(ones) * valid
    column_ref[...] = column
    start_grad_ref[...] = mix_rows(same * valid_row, [-g for g in grads])
    twin_ref[...] = mix_rows(other, [column[k : k + 1, :] for k in range(SLOTS)])

    slots = jnp.zeros((1, LANES), F32)
    for base, values in (
        (S_STRIP, col_of),
        (S_SPOT, spot),
        (S_BAND, band),
        (S_VALID, valid),
        (S_TOTAL, column[:, 0:1]),
        (S_APPROX, obs_grad[:, 0:1] * valid),
    ):
        slots = slots + moved_lanes(along_lanes(values), base)
    singles = jnp.concatenate([counted, summed, slots, jnp.zeros((1, LANES), F32)], axis=0)
    for t in range(owners):
        lanes = slice(t % 2 * LANES, t % 2 * LANES + LANES)
        for i in range(SLOTS // BLOCK):
            rows = slice(i * BLOCK, (i + 1) * BLOCK)
            message_ref[t, GRADS + i] = obs_grad[rows, lanes]
            message_ref[t, COLUMNS + i] = column[rows, lanes]
        message_ref[t, SINGLES] = singles


def moved_lanes(row, by):
    by = by % LANES
    return pltpu.roll(jnp.broadcast_to(row, (ROWS, LANES)), by, 1)[0:1] if by else row


def window_row(rows, base):
    lane = iota((1, LANES), 1)
    out = jnp.zeros((1, LANES), F32)
    for i, row in enumerate(rows):
        inside = (lane >= i * SLOTS) & (lane < (i + 1) * SLOTS)
        out = jnp.where(inside, moved_lanes(row, i * SLOTS - base), out)
    return out


def thrice(match):
    return jnp.concatenate([match] * 3, axis=1).astype(BF16)


def message_rows(send, strips_part, meta, partial, column):
    bottom = jnp.where(iota((SLOTS, LANES), 0) == 0, partial, 0.0)
    stacked = jnp.concatenate(
        [
            strips_part[:, :LANES],
            strips_part[:, LANES:],
            meta,
            bottom,
            column[:, :LANES],
            column[:, LANES:],
        ],
        axis=0,
    )
    return dot(send, split_rows(stacked))


def side_by_side(rows):
    out = rows[0]
    for i, row in enumerate(rows[1:], 1):
        wide = jnp.broadcast_to(row, (ROWS, LANES))
        out = out + pltpu.roll(wide, i * SLOTS, 1)[0:1]
    return out


def slot_scalars(hot, scalar):
    col = jnp.sum(hot * scalar, axis=1, keepdims=True)
    return col, along_lanes(col)


def advance(strips, col, row, grads, column, twin, same, approx_row, total_row, line_tops):
    other = jnp.sum(jnp.where(same > 0.0, row[:, :SLOTS], 0.0), axis=1, keepdims=True)
    full = grads + col[:SLOTS] * column + other * twin
    sources = approx_row + row * total_row
    at = iota((SLOTS, LANES), 1)
    top_grad = jnp.zeros((SLOTS, LANES), F32)
    for t in range(strips):
        value = jnp.sum(line_tops[t * SLOTS : (t + 1) * SLOTS] * sources, axis=1, keepdims=True)
        top_grad = jnp.where(at == t, value, top_grad)
    return full, top_grad


def with_approx(point, top, matrix):
    approx = jnp.sum(matrix * top, axis=1, keepdims=True)
    return jnp.where(iota((SLOTS, STRIP), 1) == 0, approx, point)


def band_partial(point, column, hot):
    dots = jnp.sum(point * column, axis=1, keepdims=True)
    return jnp.sum(hot * dots, axis=0, keepdims=True) / SOUNDS


def twins(strip_match):
    return jnp.where(iota((SLOTS, SLOTS), 0) == iota((SLOTS, SLOTS), 1), 0.0, strip_match)


def all_slots(first_ref, start):
    return jnp.concatenate(
        [first_ref[d, start + i] for d in range(first_ref.shape[0]) for i in range(SLOTS // BLOCK)], axis=0
    )


def everyones_step(strips, owners, first_ref, scalars, limit_rows_ref, top_limit, share_ref):
    sectors = strips // SEC_STRIPS
    odd = lax.rem(lax.axis_index("tile"), 2)
    lane = iota((1, LANES), 1)
    count = sectors * SLOTS
    slots = first_ref[:, SINGLES, SLOT_ROW, :]
    tall = slots.T

    def col(base):
        return jnp.concatenate([tall[base : base + SLOTS, d : d + 1] for d in range(owners)], axis=0)

    def rows(base):
        turned = []
        for i in range(sectors):
            by = (i * SLOTS - base) % LANES
            turned.append(pltpu.roll(slots, by, 1) if by else slots)
        out = []
        for w in range(WIN):
            row = turned[0][w * sectors : w * sectors + 1, :]
            for i in range(1, sectors):
                d = w * sectors + i
                row = jnp.where(lane >= i * SLOTS, turned[i][d : d + 1, :], row)
            out.append(row[:, :count])
        return out

    def part(values, w):
        return values[w * count : (w + 1) * count]

    strip = col(S_STRIP)
    spot = col(S_SPOT)
    hot = one_hot_bands(col(S_BAND))
    spread = jnp.concatenate([jnp.broadcast_to(s, (count, NBANDS)) for s in scalars], axis=0)
    along = jnp.sum(hot * spread, axis=1, keepdims=True)
    column = all_slots(first_ref, COLUMNS)
    grads = all_slots(first_ref, GRADS) + along * column
    matrix = jnp.zeros((owners * SLOTS, LANES), F32)
    limit = jnp.zeros((owners * SLOTS, LANES), F32)
    for j in range(strips):
        entries = jnp.zeros((1, LANES), F32)
        for t in range(strips):
            entries = jnp.where(lane == t, top_value(j, t, strips), entries)
        low, high = limit_rows_ref[j : j + 1, :], limit_rows_ref[strips + j : strips + j + 1, :]
        here = spot == float(j)
        matrix = jnp.where(here, entries, matrix)
        limit = jnp.where(here, jnp.where(odd == 0, low, high), limit)
    fronts = (grads[:, 0:1] * col(S_VALID)) * matrix
    parts = split(jnp.concatenate([grads, fronts], axis=1))
    strip_rows = rows(S_STRIP)
    spot_rows = rows(S_SPOT)
    valid_rows = rows(S_VALID)
    full = []
    top_grad = []
    for w in range(WIN):
        line = jnp.floor(part(strip, w) / SEC_STRIPS)
        same_line = line == jnp.floor(strip_rows[w] / SEC_STRIPS)
        same_strip = same_line & (part(spot, w) == spot_rows[w])
        match = jnp.concatenate(
            [jnp.where(same_strip, valid_rows[w], 0.0), jnp.where(same_line, 1.0, 0.0)], axis=0
        ).astype(BF16)
        both = dot(match, part(parts[0], w)) + dot(match, part(parts[1], w))
        full.append(both[:count, :LANES])
        top_grad.append(both[count:, LANES:])
    full = jnp.concatenate(full, axis=0)
    top = shrink(-STEP * jnp.concatenate(top_grad, axis=0), top_limit)
    approx = jnp.sum(matrix * top, axis=1, keepdims=True)
    point = shrink(-STEP * full, limit)
    point = jnp.where((lane == 0) & (odd == 0), approx, point)
    dots = jnp.sum(point * column, axis=1, keepdims=True)
    weighed = hot * dots
    for w in range(WIN):
        share_ref[w : w + 1, :] = jnp.sum(part(weighed, w), axis=0, keepdims=True) / SOUNDS


def window_slots(first_ref, sectors):
    my_index = lax.axis_index("tile")
    base = my_index - lax.rem(my_index, sectors)
    rows = []
    for shift in range(sectors):
        pair = base + lax.rem(my_index - base + (sectors - shift), sectors)
        rows.append(first_ref[pair, SINGLES, SLOT_ROW : SLOT_ROW + 1, :])
    return rows


def first_step_kernel(
    strips,
    owners,
    first_ref,
    info_ref,
    column_ref,
    twin_ref,
    grad_ref,
    limit_ref,
    limit_rows_ref,
    strip_match_ref,
    top_matrix_ref,
    decay_ref,
    weight_ref,
    blocks_ref,
    mix_ref,
    obs_slot_ref,
    point_ref,
    top_ref,
    share_ref,
    hot_ref,
    line_tops_ref,
    grad_out_ref,
    lead_ref,
):
    sectors = strips // SEC_STRIPS
    my_index = lax.axis_index("tile")
    window = my_index // sectors
    top_limit = STEP * weight_ref[0:1, :LANES]
    sums = weekly([first_ref[t, SINGLES, SUMS : SUMS + 1, :] for t in range(owners)], sectors)
    scalars = [r / SOUNDS for r in scan_back([-s for s in sums], decay_ref[...])]
    everyones_step(strips, owners, first_ref, scalars, limit_rows_ref, top_limit, share_ref)

    info = info_ref[...]
    slots = window_slots(first_ref, sectors)
    lane = iota((1, LANES), 1)
    count = sectors * SLOTS
    hot = one_hot_bands(to_col(window_row(slots, S_BAND)[:, :count]))
    hot_ref[...] = hot
    spot_row = window_row(slots, S_SPOT)
    line_row = jnp.where(lane < count, jnp.floor(window_row(slots, S_STRIP) / SEC_STRIPS), -1.0)
    on_line = info[:, LINE : LINE + 1] == line_row
    line_tops = jnp.concatenate(
        [jnp.where(on_line, top_entry(spot_row, t, strips), 0.0) for t in range(strips)], axis=0
    )
    line_tops_ref[...] = line_tops
    column = column_ref[...]
    col, along = slot_scalars(hot, pick(scalars, window))
    grads, top_grad = advance(
        strips,
        col,
        along,
        grad_ref[...],
        column,
        twin_ref[...],
        twins(strip_match_ref[...]),
        window_row(slots, S_APPROX),
        window_row(slots, S_TOTAL),
        line_tops,
    )
    updated = shrink(-STEP * grads, limit_ref[...])
    top = shrink(-STEP * top_grad, top_limit)
    point = with_approx(updated, top, top_matrix_ref[...])
    point_ref[...] = point
    top_ref[...] = top
    chosen = forward(point, blocks_ref, mix_ref[...]) - obs_slot_ref[...]
    rows = back_rows(chosen, blocks_ref)
    grad_out_ref[...] = mix_rows(strip_match_ref[...], rows)
    at = iota((SLOTS, LANES), 0)
    fronts = jnp.broadcast_to(rows[0][:, :LANES], (SLOTS, LANES))
    for k in range(1, SLOTS):
        fronts = jnp.where(at == k, rows[k][:, :LANES], fronts)
    share_ref[WIN : WIN + 1, :] = along_lanes(fronts[:, 0:1] * info[:, VALID : VALID + 1])
    share_ref[WIN + 1 :, :] = jnp.zeros((ROWS - 1, LANES), F32)

    sector = lax.rem(my_index, sectors).astype(F32)
    sector_row = jnp.floor(spot_row / SEC_STRIPS)
    lane = iota((SLOTS, LANES), 1)
    before = jnp.where(lane < iota((SLOTS, LANES), 0), 1.0, 0.0)
    earlier = jnp.where(lane < SLOTS, before, jnp.where(sector_row < sector, 1.0, 0.0))
    taken = jnp.sum(jnp.where(on_line, earlier, 0.0), axis=1, keepdims=True)
    lead_ref[...] = jnp.broadcast_to(jnp.where(taken > 0.0, 0.0, 1.0), lead_ref.shape)


def second_step_kernel(
    strips,
    owners,
    beta,
    first_ref,
    info_ref,
    column_ref,
    twin_ref,
    grad_ref,
    limit_ref,
    strip_match_ref,
    top_matrix_ref,
    decay_ref,
    weight_ref,
    hot_ref,
    line_tops_ref,
    lead_ref,
    rank_ref,
    send_ref,
    point_ref,
    top_ref,
    blocks_ref,
    mix_ref,
    obs_slot_ref,
    _,
    *rest,
):
    sectors = strips // SEC_STRIPS
    shares, rest = rest[:sectors], rest[sectors:]
    message_ref, values_ref = rest
    my_index = lax.axis_index("tile")
    window = my_index // sectors
    odd = lax.rem(my_index, 2)
    totals = shares[0][0:WIN, :] + jnp.where(odd == 1, shares[1][0:WIN, :], shares[-1][0:WIN, :])
    combined, _ = background(first_ref, [totals[w : w + 1, :] for w in range(WIN)], decay_ref[...], sectors)
    hot = hot_ref[...]
    column = column_ref[...]
    col, along = slot_scalars(hot, pick(combined, window))
    grads, top_grad = advance(
        strips,
        col,
        along,
        grad_ref[...],
        column,
        twin_ref[...],
        twins(strip_match_ref[...]),
        side_by_side([share[WIN : WIN + 1, :] for share in shares]),
        window_row(window_slots(first_ref, sectors), S_TOTAL),
        line_tops_ref[...],
    )
    old = point_ref[...]
    old_top = top_ref[...]
    updated = shrink(old - STEP * grads, limit_ref[...])
    top = shrink(old_top - STEP * top_grad, STEP * weight_ref[0:1, :LANES])
    point = updated + beta * (updated - old)
    top = top + beta * (top - old_top)
    point = with_approx(point, top, top_matrix_ref[...])
    values = forward(point, blocks_ref, mix_ref[...])
    values_ref[...] = values
    grad = stack_rows(back_rows(values - obs_slot_ref[...], blocks_ref))

    partial = band_partial(point, column, hot[:SLOTS])
    info = info_ref[...]
    valid = info[:, VALID : VALID + 1]
    top = top * lead_ref[:, 0:1]
    rank = rank_ref[:, 0:1]
    meta = jnp.where(rank == 0.0, pltpu.roll(top, ROWS, 1), pltpu.roll(top, LANES // 2 + ROWS, 1))
    kept = jnp.where(iota((SLOTS, STRIP), 1) == 0, 0.0, point * rank_ref[:, 1:2])
    rows = message_rows(send_ref[...], kept - STEP * (valid * grad), meta, partial, column)
    message_ref[...] = rows.reshape(message_ref.shape)


def place_kernel(
    strips,
    owners,
    first_ref,
    band_ref,
    place_ref,
    band_hot_ref,
    scaled_ref,
    block_hot_ref,
):
    sectors = strips // SEC_STRIPS
    lines = NLAT // owners
    count = owners * ROWS
    my_index = lax.axis_index("tile")
    odd = lax.rem(my_index, 2)
    mine_at = my_index.astype(F32)
    strips_owner = NLAT * SEC_STRIPS // owners
    slots = first_ref[:, SINGLES, SLOT_ROW, :]
    lane = iota((owners, LANES), 1).astype(F32)
    mine = (lane < SLOTS) & (jnp.floor(slots / strips_owner) == mine_at)
    front = jnp.min(jnp.where(mine, lane, float(LANES)), axis=1, keepdims=True)
    back = jnp.max(jnp.where(mine, lane, -1.0), axis=1, keepdims=True)
    back = jnp.where(back > front, back, float(LANES))
    wide = (owners, count)
    pair_of = iota(wide, 1) // ROWS == iota(wide, 0)
    kind = iota((1, count), 1) % ROWS
    tall = (count, owners)
    tall_pair = iota(tall, 0) // ROWS == iota(tall, 1)
    tall_kind = iota((count, 1), 0) % ROWS
    strip_rows = []
    band_col = jnp.zeros((count, 1), F32)
    slot_col = jnp.zeros((count, 1), F32) - 1.0
    for q, at in enumerate((front, back)):
        strip = jnp.sum(jnp.where(lane == at, slots - mine_at * strips_owner + 1.0, 0.0), axis=1, keepdims=True)
        band = jnp.sum(jnp.where((lane == at + S_BAND) & (at < SLOTS), slots + 1.0, 0.0), axis=1, keepdims=True)
        strip_rows.append(jnp.sum(jnp.where(pair_of, strip, 0.0), axis=0, keepdims=True) - 1.0)
        band_tall = jnp.sum(jnp.where(tall_pair, to_row(band), 0.0), axis=1, keepdims=True)
        slot_tall = jnp.sum(jnp.where(tall_pair, to_row(at), 0.0), axis=1, keepdims=True)
        own_kind = (tall_kind == 2 * q) | (tall_kind == 2 * q + 1)
        band_col = jnp.where(own_kind | (tall_kind == 6 + q), band_tall, band_col)
        slot_col = jnp.where(tall_kind == 2 * q + odd, slot_tall, slot_col)
    band_hot_ref[...] = one_hot_bands(band_col - 1.0)
    square = (count, owners * SLOTS)
    of_pair = iota(square, 1) // SLOTS == iota(square, 0) // ROWS
    of_slot = (iota(square, 1) % SLOTS).astype(F32) == slot_col
    chosen = thrice(jnp.where(of_pair & of_slot, 1.0, 0.0))
    scaled_ref[...] = STEP * dot(chosen, split_rows(all_slots(first_ref, COLUMNS)))

    def line_of(strip):
        return jnp.floor(strip / SEC_STRIPS)

    blocks = lines * WIN
    pair = iota((1, count), 1) // ROWS
    window = pair // sectors
    sector = (pair - window * sectors).astype(F32)
    line_col = (iota((blocks, 1), 0) // WIN).astype(F32)
    window_col = iota((blocks, 1), 0) % WIN
    strip_row = jnp.where((kind < 2) | (kind == 6), strip_rows[0], strip_rows[1])
    half_of = jnp.where(kind < 4, kind % 2, 1 - odd)
    slot_line = line_of(strip_row)
    slot_spot = sector * SEC_STRIPS + strip_row - slot_line * SEC_STRIPS
    base = (window == window_col) & (slot_line == line_col) & (strip_row >= 0.0)
    base = jnp.where(base & ((kind < 4) | (kind >= 6)), 1.0, 0.0)
    parts = []
    for half in range(2):
        part = jnp.where(half_of == half, base, 0.0)
        for j in range(strips):
            parts.append(jnp.where(slot_spot == float(j), part, 0.0))
    for q in range(2):
        hit = (window == window_col) & (line_of(strip_rows[q]) == line_col) & (strip_rows[q] >= 0.0) & (kind == 5)
        parts.append(jnp.where(hit, 1.0, 0.0))
    place = jnp.concatenate(parts, axis=0).astype(BF16)
    place_ref[...] = jnp.concatenate([place, place, place], axis=1)

    block_hot_ref[...] = one_hot_bands(to_col(band_ref[...].astype(F32)))


def finish_kernel(
    strips,
    owners,
    first_ref,
    third_ref,
    values_ref,
    obs_ref,
    place_ref,
    band_hot_ref,
    scaled_ref,
    block_hot_ref,
    decay_ref,
    weight_ref,
    out_ref,
    misfit_ref,
):
    sectors = strips // SEC_STRIPS
    blocks = NLAT // owners * WIN
    count = owners * ROWS
    window = lax.axis_index("tile") // sectors
    differ = values_ref[...].T[MISFIT : MISFIT + SB_DEV, :] - obs_ref[...]
    partials = weekly([third_ref[t, 4:5, :] for t in range(owners)], sectors)
    combined, carried = background(first_ref, partials, decay_ref[...], sectors)
    spread = jnp.concatenate(
        [jnp.broadcast_to(row, (sectors * ROWS, NBANDS)) for row in combined], axis=0
    )
    scalars = jnp.sum(band_hot_ref[...] * spread, axis=1, keepdims=True)
    third = third_ref[...].reshape(count, LANES)
    kind = iota((count, 1), 0) % ROWS
    rows = jnp.where(kind >= 6, -STEP * (scalars * third), third - scalars * scaled_ref[...])
    placed = dot(place_ref[...], split_rows(rows))
    offset = jnp.sum(block_hot_ref[...] * pick(carried, window), axis=1, keepdims=True)
    misfit_ref[...] = differ + offset

    lane = iota((1, LANES), 1)
    for j in range(strips):
        start = (strips + j) * LANES
        values = placed[(strips + j) * blocks : (strips + j + 1) * blocks]
        out_ref[:, start : start + LANES] = shrink(values, STEP * weight_ref[0:1, start : start + LANES])

    low = [placed[j * blocks : (j + 1) * blocks] for j in range(strips)]
    tops = [placed[(2 * strips + q) * blocks : (2 * strips + q + 1) * blocks] for q in range(2)]
    top = pltpu.roll(tops[0], LANES - ROWS, 1) + pltpu.roll(tops[1], LANES // 2 - ROWS, 1)
    made = [jnp.zeros((blocks, LANES), F32) for _ in range(strips)]
    for t in range(strips):
        value = jnp.zeros((blocks, 1), F32)
        for j in range(strips):
            entry = top_value(j, t, strips)
            if entry:
                value = value + entry * low[j][:, 0:1]
        made[0] = jnp.where(lane == t, value + top, made[0])
    m = 1
    while m < LANES:
        for j in range(strips):
            start = strips * m + j * m
            block = start // LANES
            shift = (start % LANES - m) % LANES
            moved = pltpu.roll(low[j], shift, 1) if shift else low[j]
            inside = (lane >= start % LANES) & (lane < start % LANES + m)
            made[block] = jnp.where(inside, moved, made[block])
        m *= 2
    for block in range(strips):
        start = block * LANES
        out_ref[:, start : start + LANES] = shrink(made[block], STEP * weight_ref[0:1, start : start + LANES])


def top_value(spot, index, strips):
    if index == 0:
        return math.sqrt(1.0 / strips)
    m = 1 << (index.bit_length() - 1)
    span = strips // m
    within = spot - (index - m) * span
    if within < 0 or within >= span:
        return 0.0
    return math.sqrt(m / strips) * (1.0 if within < span // 2 else -1.0)


def call(kernel, outs, *operands, **kwargs):
    return pl.pallas_call(
        kernel,
        out_shape=[jax.ShapeDtypeStruct(shape, dtype) for shape, dtype in outs],
        compiler_params=pltpu.CompilerParams(vmem_limit_bytes=40 * 1024 * 1024),
        **kwargs,
    )(*operands)


def body(
    observations,
    jacobian,
    block_row,
    block_col,
    block_count,
    block_band,
    carry_decay,
    sparsity_weight,
):
    owners = lax.axis_size("tile")
    sectors = owners // WIN
    strips = sectors * SEC_STRIPS
    lines = NLAT // owners
    betas = momentum_weights(ITERS)
    arguments = [
        block_band.reshape(1, SB_DEV),
        observations,
        block_row.reshape(1, SLOTS),
        block_col.reshape(1, SLOTS),
        sparsity_weight.reshape(1, -1),
        carry_decay.reshape(1, NBANDS),
        jacobian.reshape(SLOTS * SOUNDS, STRIP),
    ]
    message = ((owners, ROWS, LANES), F32)
    narrow = ((SLOTS, LANES), F32)
    strip_rows = ((SLOTS, STRIP), F32)

    def trade(values):
        return lax.all_to_all(values, "tile", 0, 0, tiled=True)

    def with_sectors(values):
        found = [values]
        for shift in range(1, sectors):
            pairs = [
                (d, d // sectors * sectors + (d + shift) % sectors) for d in range(owners)
            ]
            found.append(lax.ppermute(values, "tile", pairs))
        return found

    arguments = [pltpu.with_memory_space_constraint(a, pltpu.HBM) for a in arguments]
    outs = [
        ((1, SB_DEV), jnp.int32),
        ((SB_DEV, SOUNDS), F32),
        ((1, strips * STRIP), F32),
        ((1, NBANDS), F32),
        ((SLOTS * SOUNDS, STRIP), F32),
        strip_rows,
        strip_rows,
        strip_rows,
        ((SOUNDS, LANES), F32),
        narrow,
        narrow,
        strip_rows,
        ((2 * strips, LANES), F32),
        ((owners * ROWS, 3 * PARTS * SLOTS), BF16),
        ((SLOTS, SLOTS), F32),
        narrow,
        narrow,
        ((owners, FIRST_BLOCKS, BLOCK, LANES), F32),
    ]
    (
        bands,
        observed,
        weight,
        decay,
        blocks,
        column,
        twin,
        start_grad,
        obs_slot,
        mix,
        info,
        limit,
        limit_rows,
        send,
        strip_match,
        top_matrix,
        rank,
        first,
    ) = call(
        functools.partial(open_kernel, strips, owners),
        outs,
        *arguments,
        block_count,
        in_specs=[pl.BlockSpec(memory_space=pltpu.HBM)] * len(arguments)
        + [pl.BlockSpec(memory_space=pltpu.SMEM)],
        scratch_shapes=[
            pltpu.VMEM((1, SLOTS), jnp.int32),
            pltpu.VMEM((1, SLOTS), jnp.int32),
            pltpu.VMEM((SLOTS * SOUNDS, STRIP), F32),
            pltpu.SemaphoreType.DMA((len(arguments) - 1 + PIECES,)),
        ],
    )
    first = trade(first)
    point, top, share, hot, line_tops, grad, lead = call(
        functools.partial(first_step_kernel, strips, owners),
        [
            strip_rows,
            narrow,
            ((2 * ROWS, LANES), F32),
            ((sectors * SLOTS, NBANDS), F32),
            ((strips * SLOTS, LANES), F32),
            strip_rows,
            narrow,
        ],
        first,
        info,
        column,
        twin,
        start_grad,
        limit,
        limit_rows,
        strip_match,
        top_matrix,
        decay,
        weight,
        blocks,
        mix,
        obs_slot,
    )
    placed_rows = (2 * strips + 2) * lines * WIN
    tables = call(
        functools.partial(place_kernel, strips, owners),
        [
            ((placed_rows, 3 * owners * ROWS), BF16),
            ((owners * ROWS, NBANDS), F32),
            ((owners * ROWS, LANES), F32),
            ((SB_DEV, NBANDS), F32),
        ],
        first,
        bands,
    )
    third, values = call(
        functools.partial(second_step_kernel, strips, owners, betas[1]),
        [message, ((SOUNDS, LANES), F32)],
        first,
        info,
        column,
        twin,
        grad,
        limit,
        strip_match,
        top_matrix,
        decay,
        weight,
        hot,
        line_tops,
        lead,
        rank,
        send,
        point,
        top,
        blocks,
        mix,
        obs_slot,
        tables[-1],
        *with_sectors(share),
    )
    third = trade(third)
    coeffs, misfit = call(
        functools.partial(finish_kernel, strips, owners),
        [((lines * WIN, strips * STRIP), F32), ((SB_DEV, SOUNDS), F32)],
        first,
        third,
        values,
        observed,
        *tables,
        decay,
        weight,
    )
    return (coeffs.reshape(lines, WIN, strips * STRIP), misfit)


def solution(mesh):
    return jax.shard_map(
        body,
        mesh=mesh,
        in_specs=(
            P(("ens", "tile"), None),
            P("tile", None, None),
            P("tile"),
            P("tile"),
            P("tile"),
            P("tile"),
            P(),
            P(),
        ),
        out_specs=(P(("ens", "tile"), None, None), P(("ens", "tile"), None)),
        check_vma=False,
    )
```

```python
import functools
import math

import jax
import jax.numpy as jnp
from jax import lax
from jax.experimental import pallas as pl
from jax.experimental.pallas import tpu as pltpu
from jax.sharding import PartitionSpec as P

WIN = 8
NLAT = 64
SEC_STRIPS = 2
STRIP = 256
SOUNDS = 64
SB_DEV = 32
NBANDS = 128
ITERS = 3
SLOTS = 16
LANES = 128
ROWS = 8
STEP = 0.2
MISFIT = 32
PARTS = 6
PIECES = 1

F32 = jnp.float32
BF16 = jnp.bfloat16
HIGHEST = lax.Precision.HIGHEST

LINE, SPOT, BAND, COL, VALID = range(5)
BLOCK = 4
GRADS, COLUMNS, SINGLES = 0, SLOTS // BLOCK, 2 * SLOTS // BLOCK
COUNTS, SUMS, SLOT_ROW = range(3)
FIRST_BLOCKS = SINGLES + 1
S_STRIP, S_SPOT, S_BAND, S_VALID, S_TOTAL, S_APPROX = (i * SLOTS for i in range(6))


def momentum_weights(total_steps):
    weights = []
    current = 1.0
    for _ in range(total_steps):
        following = (1.0 + math.sqrt(1.0 + 4.0 * current * current)) / 2.0
        weights.append((current - 1.0) / following)
        current = following
    return weights


def iota(shape, axis):
    return lax.broadcasted_iota(jnp.int32, shape, axis)


def shrink(values, limit):
    return values - jnp.minimum(jnp.maximum(values, -limit), limit)


def to_col(row):
    n = row.shape[1]
    eye = iota((n, n), 0) == iota((n, n), 1)
    return jnp.sum(jnp.where(eye, row, 0.0), axis=1, keepdims=True)


def to_row(col):
    n = col.shape[0]
    eye = iota((n, n), 0) == iota((n, n), 1)
    return jnp.sum(jnp.where(eye, col, 0.0), axis=0, keepdims=True)


def exact_dot(left, right):
    return jnp.dot(left, right, precision=HIGHEST, preferred_element_type=F32)


def dot(left, right):
    return jnp.dot(left, right, preferred_element_type=F32)


def dot_nt(left, right):
    return lax.dot_general(left, right, (((1,), (1,)), ((), ())), preferred_element_type=F32)


def split(values):
    high = values.astype(BF16)
    return high, (values - high.astype(F32)).astype(BF16)


def split_parts(values):
    high = values.astype(BF16)
    rest = values - high.astype(F32)
    middle = rest.astype(BF16)
    return [high, middle, (rest - middle.astype(F32)).astype(BF16)]


def split_rows(values):
    return jnp.concatenate(split_parts(values), axis=0)


def haar_signs():
    coef = iota((1, STRIP), 1).astype(F32)
    level = jnp.zeros((1, STRIP), F32) + 1.0
    m = 2
    while m < STRIP:
        level = jnp.where(coef >= m, float(m), level)
        m *= 2
    first = coef == 0.0
    shift = jnp.where(first, 0.0, coef - level)
    half = jnp.where(first, 2.0, 0.5)
    within = iota((STRIP, STRIP), 0).astype(F32) * (level / STRIP) - shift
    inside = (within >= 0.0) & (within < 1.0)
    return jnp.where(inside, jnp.where(within < half, 1.0, -1.0), 0.0).astype(BF16)


def haar_scales():
    coef = iota((1, STRIP), 1)
    out = jnp.full((1, STRIP), math.sqrt(1.0 / STRIP), F32)
    m = 1
    while m < STRIP:
        out = jnp.where((coef >= m) & (coef < 2 * m), math.sqrt(m / STRIP), out)
        m *= 2
    return out


def top_entry(spot, index, strips):
    if index == 0:
        return jnp.full(spot.shape, math.sqrt(1.0 / strips), F32)
    m = 1 << (index.bit_length() - 1)
    span = strips // m
    start = float((index - m) * span)
    half = start + span / 2
    end = start + span
    scale = math.sqrt(m / strips)
    positive = (spot >= start) & (spot < half)
    negative = (spot >= half) & (spot < end)
    return jnp.where(positive, scale, jnp.where(negative, -scale, 0.0))


def weekly(rows, sectors):
    return [sum(rows[w * sectors + 1 : (w + 1) * sectors], rows[w * sectors]) for w in range(WIN)]


def scan_back(totals, decay):
    running = totals[WIN - 1]
    out = [running]
    for w in range(WIN - 2, -1, -1):
        running = running * decay + totals[w]
        out.insert(0, running)
    return out


def scan_ahead(totals, decay):
    running = totals[0]
    out = [running]
    for w in range(1, WIN):
        running = running * decay + totals[w]
        out.append(running)
    return out


def pick(rows, index):
    out = rows[0]
    for w in range(1, len(rows)):
        out = jnp.where(index == w, rows[w], out)
    return out


def background(first, partials, decay, sectors):
    pairs = range(WIN * sectors)
    counts = weekly([first[t, SINGLES, COUNTS : COUNTS + 1, :] for t in pairs], sectors)
    sums = weekly([first[t, SINGLES, SUMS : SUMS + 1, :] for t in pairs], sectors)
    carried = scan_ahead(partials, decay)
    back = [
        SOUNDS * partials[w] + (SOUNDS * counts[w]) * carried[w] - sums[w] for w in range(WIN)
    ]
    returned = scan_back(back, decay)
    return [carried[w] + returned[w] / SOUNDS for w in range(WIN)], carried


def one_hot_bands(band_col):
    return jnp.where(band_col == iota((band_col.shape[0], NBANDS), 1).astype(F32), 1.0, 0.0)


def forward(point, blocks_ref, mix):
    total = None
    for k in range(SLOTS):
        product = blocks_ref[k * SOUNDS : (k + 1) * SOUNDS, :] * point[k : k + 1, :]
        values = jnp.sum(product[:, :LANES] + product[:, LANES:], axis=1, keepdims=True)
        term = values * mix[k : k + 1, :]
        total = term if total is None else total + term
    return total


def back_rows(chosen, blocks_ref):
    return [
        jnp.sum(
            blocks_ref[k * SOUNDS : (k + 1) * SOUNDS, :] * chosen[:, k : k + 1],
            axis=0,
            keepdims=True,
        )
        for k in range(SLOTS)
    ]


def stack_rows(rows):
    at = iota((SLOTS, STRIP), 0)
    out = jnp.broadcast_to(rows[0], (SLOTS, STRIP))
    for k in range(1, SLOTS):
        out = jnp.where(at == k, rows[k], out)
    return out


def mix_rows(match, rows):
    out = match[:, 0:1] * rows[0]
    for k in range(1, SLOTS):
        out = out + match[:, k : k + 1] * rows[k]
    return out


def along_lanes(col):
    n = col.shape[0]
    here = iota((n, LANES), 0) == iota((n, LANES), 1)
    return jnp.sum(jnp.where(here, col, 0.0), axis=0, keepdims=True)


def open_kernel(
    strips,
    owners,
    band_in,
    obs_in,
    row_in,
    col_in,
    weight_in,
    decay_in,
    jac_in,
    count_ref,
    band_ref,
    obs_ref,
    weight_ref,
    decay_ref,
    blocks_ref,
    column_ref,
    twin_ref,
    start_grad_ref,
    obs_slot_ref,
    mix_ref,
    info_ref,
    limit_ref,
    limit_rows_ref,
    strip_match_ref,
    top_matrix_ref,
    message_ref,
    row_ref,
    col_ref,
    jac_ref,
    sems,
):
    piece = SLOTS * SOUNDS // PIECES
    moves = [
        (band_in, band_ref),
        (obs_in, obs_ref),
        (row_in, row_ref),
        (col_in, col_ref),
        (weight_in, weight_ref),
        (decay_in, decay_ref),
    ]
    for start in range(0, SLOTS * SOUNDS, piece):
        moves.append((jac_in.at[start : start + piece], jac_ref.at[start : start + piece]))
    copies = [pltpu.make_async_copy(a, b, sems.at[i]) for i, (a, b) in enumerate(moves)]
    for copy in copies:
        copy.start()
    sectors = strips // SEC_STRIPS
    sector = lax.rem(lax.axis_index("tile"), sectors).astype(F32)
    signs = haar_signs()
    scales = haar_scales()
    for copy in copies[:6]:
        copy.wait()

    band_row = band_ref[...].astype(F32)
    block_hot = one_hot_bands(to_col(band_row))
    counted = jnp.sum(block_hot, axis=0, keepdims=True)
    summed = jnp.sum(block_hot * jnp.sum(obs_ref[...], axis=1, keepdims=True), axis=0, keepdims=True)
    row_of = to_col(row_ref[...].astype(F32))
    col_row = col_ref[...].astype(F32)
    col_of = to_col(col_row)
    valid = jnp.where(iota((SLOTS, 1), 0) < count_ref[0], 1.0, 0.0)
    valid_row = jnp.where(iota((1, SLOTS), 1) < count_ref[0], 1.0, 0.0)
    line = jnp.floor(col_of / SEC_STRIPS)
    spot = sector * SEC_STRIPS + (col_of - line * SEC_STRIPS)
    row_hot = jnp.where(row_of == iota((SLOTS, SB_DEV), 1).astype(F32), 1.0, 0.0)
    band = jnp.sum(row_hot * band_row, axis=1, keepdims=True)
    band = jnp.where(valid > 0.0, band, -1.0)
    lane = iota((1, LANES), 1)
    wanted = jnp.where(lane < SLOTS, along_lanes(row_of), -1.0)
    wanted_hot = jnp.where(iota((SB_DEV, LANES), 0).astype(F32) == wanted, 1.0, 0.0)
    obs_slot = exact_dot(obs_ref[...].T, wanted_hot)
    obs_slot_ref[...] = obs_slot
    block_lane = (lane >= MISFIT) & (lane < MISFIT + SB_DEV)
    wanted = jnp.where(block_lane, (lane - MISFIT).astype(F32), wanted)
    mix_ref[...] = jnp.where(row_of == wanted, valid, 0.0)

    same = jnp.where(col_of == col_row, 1.0, 0.0)
    other = jnp.where(iota((SLOTS, SLOTS), 1) != iota((SLOTS, SLOTS), 0), same, 0.0)
    strip_match_ref[...] = same * valid_row
    at = iota((SLOTS, LANES), 1)
    info = jnp.zeros((SLOTS, LANES), F32)
    for place, values in ((LINE, line), (SPOT, spot), (BAND, band), (COL, col_of), (VALID, valid)):
        info = jnp.where(at == place, values, info)
    info_ref[...] = info
    matrix = jnp.zeros((SLOTS, LANES), F32)
    for t in range(strips):
        matrix = jnp.where(at == t, top_entry(spot, t, strips), matrix)
    top_matrix_ref[...] = matrix

    local = iota((1, LANES), 1)
    limits_low = jnp.zeros((SLOTS, LANES), F32)
    limits_high = jnp.zeros((SLOTS, LANES), F32)
    for j in range(strips):
        low_row = jnp.zeros((1, LANES), F32)
        m = 1
        while m < LANES:
            start = strips * m + j * m
            block = weight_ref[0:1, start // LANES * LANES : start // LANES * LANES + LANES]
            shift = (m - start % LANES) % LANES
            moved = pltpu.roll(jnp.broadcast_to(block, (ROWS, LANES)), shift, 1)[0:1] if shift else block
            low_row = jnp.where((local >= m) & (local < 2 * m), moved, low_row)
            m *= 2
        high_row = weight_ref[0:1, (strips + j) * LANES : (strips + j + 1) * LANES]
        limit_rows_ref[j : j + 1, :] = STEP * low_row
        limit_rows_ref[strips + j : strips + j + 1, :] = STEP * high_row
        limits_low = jnp.where(spot == float(j), low_row, limits_low)
        limits_high = jnp.where(spot == float(j), high_row, limits_high)
    limit_ref[:, :LANES] = STEP * limits_low
    limit_ref[:, LANES:] = STEP * limits_high

    per = SLOTS // PIECES
    grads = []
    ones = []
    for part in range(PIECES):
        copies[6 + part].wait()
        for start in range(part * piece, part * piece + piece, STRIP):
            high, low = split(jac_ref[start : start + STRIP, :])
            blocks_ref[start : start + STRIP, :] = (dot(high, signs) + dot(low, signs)) * scales
        for k in range(part * per, part * per + per):
            block = blocks_ref[k * SOUNDS : (k + 1) * SOUNDS, :]
            grads.append(jnp.sum(block * obs_slot[:, k : k + 1], axis=0, keepdims=True))
            ones.append(jnp.sum(block, axis=0, keepdims=True))
    obs_grad = -stack_rows(grads)
    column = stack_rows(ones) * valid
    column_ref[...] = column
    start_grad_ref[...] = mix_rows(same * valid_row, [-g for g in grads])
    twin_ref[...] = mix_rows(other, [column[k : k + 1, :] for k in range(SLOTS)])

    slots = jnp.zeros((1, LANES), F32)
    for base, values in (
        (S_STRIP, col_of),
        (S_SPOT, spot),
        (S_BAND, band),
        (S_VALID, valid),
        (S_TOTAL, column[:, 0:1]),
        (S_APPROX, obs_grad[:, 0:1] * valid),
    ):
        slots = slots + moved_lanes(along_lanes(values), base)
    singles = jnp.concatenate([counted, summed, slots, jnp.zeros((1, LANES), F32)], axis=0)
    for t in range(owners):
        lanes = slice(t % 2 * LANES, t % 2 * LANES + LANES)
        for i in range(SLOTS // BLOCK):
            rows = slice(i * BLOCK, (i + 1) * BLOCK)
            message_ref[t, GRADS + i] = obs_grad[rows, lanes]
            message_ref[t, COLUMNS + i] = column[rows, lanes]
        message_ref[t, SINGLES] = singles


def moved_lanes(row, by):
    by = by % LANES
    return pltpu.roll(jnp.broadcast_to(row, (ROWS, LANES)), by, 1)[0:1] if by else row


def window_row(rows, base):
    lane = iota((1, LANES), 1)
    out = jnp.zeros((1, LANES), F32)
    for i, row in enumerate(rows):
        inside = (lane >= i * SLOTS) & (lane < (i + 1) * SLOTS)
        out = jnp.where(inside, moved_lanes(row, i * SLOTS - base), out)
    return out


def thrice(match):
    return jnp.concatenate([match] * 3, axis=1).astype(BF16)


def message_rows(send, strips_part, meta, partial, column):
    bottom = jnp.where(iota((SLOTS, LANES), 0) == 0, partial, 0.0)
    stacked = jnp.concatenate(
        [
            strips_part[:, :LANES],
            strips_part[:, LANES:],
            meta,
            bottom,
            column[:, :LANES],
            column[:, LANES:],
        ],
        axis=0,
    )
    return dot(send, split_rows(stacked))


def side_by_side(rows):
    out = rows[0]
    for i, row in enumerate(rows[1:], 1):
        wide = jnp.broadcast_to(row, (ROWS, LANES))
        out = out + pltpu.roll(wide, i * SLOTS, 1)[0:1]
    return out


def slot_scalars(hot, scalar):
    col = jnp.sum(hot * scalar, axis=1, keepdims=True)
    return col, along_lanes(col)


def advance(strips, col, row, grads, column, twin, same, approx_row, total_row, line_tops):
    other = jnp.sum(jnp.where(same > 0.0, row[:, :SLOTS], 0.0), axis=1, keepdims=True)
    full = grads + col[:SLOTS] * column + other * twin
    sources = approx_row + row * total_row
    at = iota((SLOTS, LANES), 1)
    top_grad = jnp.zeros((SLOTS, LANES), F32)
    for t in range(strips):
        value = jnp.sum(line_tops[t * SLOTS : (t + 1) * SLOTS] * sources, axis=1, keepdims=True)
        top_grad = jnp.where(at == t, value, top_grad)
    return full, top_grad


def with_approx(point, top, matrix):
    approx = jnp.sum(matrix * top, axis=1, keepdims=True)
    return jnp.where(iota((SLOTS, STRIP), 1) == 0, approx, point)


def band_partial(point, column, hot):
    dots = jnp.sum(point * column, axis=1, keepdims=True)
    return jnp.sum(hot * dots, axis=0, keepdims=True) / SOUNDS


def twins(strip_match):
    return jnp.where(iota((SLOTS, SLOTS), 0) == iota((SLOTS, SLOTS), 1), 0.0, strip_match)


def all_slots(first_ref, start):
    return jnp.concatenate(
        [first_ref[d, start + i] for d in range(first_ref.shape[0]) for i in range(SLOTS // BLOCK)], axis=0
    )


def everyones_step(strips, owners, first_ref, scalars, limit_rows_ref, top_limit, share_ref):
    sectors = strips // SEC_STRIPS
    odd = lax.rem(lax.axis_index("tile"), 2)
    lane = iota((1, LANES), 1)
    count = sectors * SLOTS
    slots = first_ref[:, SINGLES, SLOT_ROW, :]
    tall = slots.T

    def col(base):
        return jnp.concatenate([tall[base : base + SLOTS, d : d + 1] for d in range(owners)], axis=0)

    def rows(base):
        turned = []
        for i in range(sectors):
            by = (i * SLOTS - base) % LANES
            turned.append(pltpu.roll(slots, by, 1) if by else slots)
        out = []
        for w in range(WIN):
            row = turned[0][w * sectors : w * sectors + 1, :]
            for i in range(1, sectors):
                d = w * sectors + i
                row = jnp.where(lane >= i * SLOTS, turned[i][d : d + 1, :], row)
            out.append(row[:, :count])
        return out

    def part(values, w):
        return values[w * count : (w + 1) * count]

    strip = col(S_STRIP)
    spot = col(S_SPOT)
    hot = one_hot_bands(col(S_BAND))
    spread = jnp.concatenate([jnp.broadcast_to(s, (count, NBANDS)) for s in scalars], axis=0)
    along = jnp.sum(hot * spread, axis=1, keepdims=True)
    column = all_slots(first_ref, COLUMNS)
    grads = all_slots(first_ref, GRADS) + along * column
    matrix = jnp.zeros((owners * SLOTS, LANES), F32)
    limit = jnp.zeros((owners * SLOTS, LANES), F32)
    for j in range(strips):
        entries = jnp.zeros((1, LANES), F32)
        for t in range(strips):
            entries = jnp.where(lane == t, top_value(j, t, strips), entries)
        low, high = limit_rows_ref[j : j + 1, :], limit_rows_ref[strips + j : strips + j + 1, :]
        here = spot == float(j)
        matrix = jnp.where(here, entries, matrix)
        limit = jnp.where(here, jnp.where(odd == 0, low, high), limit)
    fronts = (grads[:, 0:1] * col(S_VALID)) * matrix
    parts = split(jnp.concatenate([grads, fronts], axis=1))
    strip_rows = rows(S_STRIP)
    spot_rows = rows(S_SPOT)
    valid_rows = rows(S_VALID)
    full = []
    top_grad = []
    for w in range(WIN):
        line = jnp.floor(part(strip, w) / SEC_STRIPS)
        same_line = line == jnp.floor(strip_rows[w] / SEC_STRIPS)
        same_strip = same_line & (part(spot, w) == spot_rows[w])
        match = jnp.concatenate(
            [jnp.where(same_strip, valid_rows[w], 0.0), jnp.where(same_line, 1.0, 0.0)], axis=0
        ).astype(BF16)
        both = dot(match, part(parts[0], w)) + dot(match, part(parts[1], w))
        full.append(both[:count, :LANES])
        top_grad.append(both[count:, LANES:])
    full = jnp.concatenate(full, axis=0)
    top = shrink(-STEP * jnp.concatenate(top_grad, axis=0), top_limit)
    approx = jnp.sum(matrix * top, axis=1, keepdims=True)
    point = shrink(-STEP * full, limit)
    point = jnp.where((lane == 0) & (odd == 0), approx, point)
    dots = jnp.sum(point * column, axis=1, keepdims=True)
    weighed = hot * dots
    for w in range(WIN):
        share_ref[w : w + 1, :] = jnp.sum(part(weighed, w), axis=0, keepdims=True) / SOUNDS


def window_slots(first_ref, sectors):
    my_index = lax.axis_index("tile")
    base = my_index - lax.rem(my_index, sectors)
    rows = []
    for shift in range(sectors):
        pair = base + lax.rem(my_index - base + (sectors - shift), sectors)
        rows.append(first_ref[pair, SINGLES, SLOT_ROW : SLOT_ROW + 1, :])
    return rows


def first_step_kernel(
    strips,
    owners,
    first_ref,
    info_ref,
    column_ref,
    twin_ref,
    grad_ref,
    limit_ref,
    limit_rows_ref,
    strip_match_ref,
    top_matrix_ref,
    decay_ref,
    weight_ref,
    blocks_ref,
    mix_ref,
    obs_slot_ref,
    point_ref,
    top_ref,
    share_ref,
    hot_ref,
    line_tops_ref,
    grad_out_ref,
):
    sectors = strips // SEC_STRIPS
    my_index = lax.axis_index("tile")
    window = my_index // sectors
    top_limit = STEP * weight_ref[0:1, :LANES]
    sums = weekly([first_ref[t, SINGLES, SUMS : SUMS + 1, :] for t in range(owners)], sectors)
    scalars = [r / SOUNDS for r in scan_back([-s for s in sums], decay_ref[...])]

    info = info_ref[...]
    slots = window_slots(first_ref, sectors)
    lane = iota((1, LANES), 1)
    count = sectors * SLOTS
    hot = one_hot_bands(to_col(window_row(slots, S_BAND)[:, :count]))
    hot_ref[...] = hot
    spot_row = window_row(slots, S_SPOT)
    line_row = jnp.where(lane < count, jnp.floor(window_row(slots, S_STRIP) / SEC_STRIPS), -1.0)
    on_line = info[:, LINE : LINE + 1] == line_row
    line_tops = jnp.concatenate(
        [jnp.where(on_line, top_entry(spot_row, t, strips), 0.0) for t in range(strips)], axis=0
    )
    line_tops_ref[...] = line_tops
    column = column_ref[...]
    col, along = slot_scalars(hot, pick(scalars, window))
    grads, top_grad = advance(
        strips,
        col,
        along,
        grad_ref[...],
        column,
        twin_ref[...],
        twins(strip_match_ref[...]),
        window_row(slots, S_APPROX),
        window_row(slots, S_TOTAL),
        line_tops,
    )
    updated = shrink(-STEP * grads, limit_ref[...])
    top = shrink(-STEP * top_grad, top_limit)
    point = with_approx(updated, top, top_matrix_ref[...])
    point_ref[...] = point
    top_ref[...] = top
    everyones_step(strips, owners, first_ref, scalars, limit_rows_ref, top_limit, share_ref)
    chosen = forward(point, blocks_ref, mix_ref[...]) - obs_slot_ref[...]
    rows = back_rows(chosen, blocks_ref)
    grad_out_ref[...] = mix_rows(strip_match_ref[...], rows)
    at = iota((SLOTS, LANES), 0)
    fronts = jnp.broadcast_to(rows[0][:, :LANES], (SLOTS, LANES))
    for k in range(1, SLOTS):
        fronts = jnp.where(at == k, rows[k][:, :LANES], fronts)
    share_ref[WIN : WIN + 1, :] = along_lanes(fronts[:, 0:1] * info[:, VALID : VALID + 1])
    share_ref[WIN + 1 :, :] = jnp.zeros((ROWS - 1, LANES), F32)

def second_step_kernel(
    strips,
    owners,
    beta,
    first_ref,
    info_ref,
    column_ref,
    twin_ref,
    grad_ref,
    limit_ref,
    strip_match_ref,
    top_matrix_ref,
    decay_ref,
    weight_ref,
    hot_ref,
    line_tops_ref,
    lead_ref,
    rank_ref,
    send_ref,
    point_ref,
    top_ref,
    blocks_ref,
    mix_ref,
    obs_slot_ref,
    *rest,
):
    sectors = strips // SEC_STRIPS
    shares, rest = rest[:sectors], rest[sectors:]
    message_ref, values_ref = rest
    my_index = lax.axis_index("tile")
    window = my_index // sectors
    odd = lax.rem(my_index, 2)
    totals = shares[0][0:WIN, :] + jnp.where(odd == 1, shares[1][0:WIN, :], shares[-1][0:WIN, :])
    combined, _ = background(first_ref, [totals[w : w + 1, :] for w in range(WIN)], decay_ref[...], sectors)
    hot = hot_ref[...]
    column = column_ref[...]
    col, along = slot_scalars(hot, pick(combined, window))
    grads, top_grad = advance(
        strips,
        col,
        along,
        grad_ref[...],
        column,
        twin_ref[...],
        twins(strip_match_ref[...]),
        side_by_side([share[WIN : WIN + 1, :] for share in shares]),
        window_row(window_slots(first_ref, sectors), S_TOTAL),
        line_tops_ref[...],
    )
    old = point_ref[...]
    old_top = top_ref[...]
    updated = shrink(old - STEP * grads, limit_ref[...])
    top = shrink(old_top - STEP * top_grad, STEP * weight_ref[0:1, :LANES])
    point = updated + beta * (updated - old)
    top = top + beta * (top - old_top)
    point = with_approx(point, top, top_matrix_ref[...])
    values = forward(point, blocks_ref, mix_ref[...])
    values_ref[...] = values
    grad = stack_rows(back_rows(values - obs_slot_ref[...], blocks_ref))

    partial = band_partial(point, column, hot[:SLOTS])
    info = info_ref[...]
    valid = info[:, VALID : VALID + 1]
    top = top * lead_ref[:, 0:1]
    rank = rank_ref[:, 0:1]
    meta = jnp.where(rank == 0.0, pltpu.roll(top, ROWS, 1), pltpu.roll(top, LANES // 2 + ROWS, 1))
    kept = jnp.where(iota((SLOTS, STRIP), 1) == 0, 0.0, point * rank_ref[:, 1:2])
    rows = message_rows(send_ref[...], kept - STEP * (valid * grad), meta, partial, column)
    message_ref[...] = rows.reshape(message_ref.shape)


def place_kernel(
    strips,
    owners,
    first_ref,
    band_ref,
    info_ref,
    place_ref,
    band_hot_ref,
    scaled_ref,
    block_hot_ref,
    send_ref,
    rank_ref,
    lead_ref,
):
    sectors = strips // SEC_STRIPS
    lines = NLAT // owners
    count = owners * ROWS
    my_index = lax.axis_index("tile")
    odd = lax.rem(my_index, 2)
    mine_at = my_index.astype(F32)
    strips_owner = NLAT * SEC_STRIPS // owners
    slots = first_ref[:, SINGLES, SLOT_ROW, :]
    lane = iota((owners, LANES), 1).astype(F32)
    mine = (lane < SLOTS) & (jnp.floor(slots / strips_owner) == mine_at)
    front = jnp.min(jnp.where(mine, lane, float(LANES)), axis=1, keepdims=True)
    back = jnp.max(jnp.where(mine, lane, -1.0), axis=1, keepdims=True)
    back = jnp.where(back > front, back, float(LANES))
    wide = (owners, count)
    pair_of = iota(wide, 1) // ROWS == iota(wide, 0)
    kind = iota((1, count), 1) % ROWS
    tall = (count, owners)
    tall_pair = iota(tall, 0) // ROWS == iota(tall, 1)
    tall_kind = iota((count, 1), 0) % ROWS
    strip_rows = []
    band_col = jnp.zeros((count, 1), F32)
    slot_col = jnp.zeros((count, 1), F32) - 1.0
    for q, at in enumerate((front, back)):
        strip = jnp.sum(jnp.where(lane == at, slots - mine_at * strips_owner + 1.0, 0.0), axis=1, keepdims=True)
        band = jnp.sum(jnp.where((lane == at + S_BAND) & (at < SLOTS), slots + 1.0, 0.0), axis=1, keepdims=True)
        strip_rows.append(jnp.sum(jnp.where(pair_of, strip, 0.0), axis=0, keepdims=True) - 1.0)
        band_tall = jnp.sum(jnp.where(tall_pair, to_row(band), 0.0), axis=1, keepdims=True)
        slot_tall = jnp.sum(jnp.where(tall_pair, to_row(at), 0.0), axis=1, keepdims=True)
        own_kind = (tall_kind == 2 * q) | (tall_kind == 2 * q + 1)
        band_col = jnp.where(own_kind | (tall_kind == 6 + q), band_tall, band_col)
        slot_col = jnp.where(tall_kind == 2 * q + odd, slot_tall, slot_col)
    band_hot_ref[...] = one_hot_bands(band_col - 1.0)
    square = (count, owners * SLOTS)
    of_pair = iota(square, 1) // SLOTS == iota(square, 0) // ROWS
    of_slot = (iota(square, 1) % SLOTS).astype(F32) == slot_col
    chosen = thrice(jnp.where(of_pair & of_slot, 1.0, 0.0))
    scaled_ref[...] = STEP * dot(chosen, split_rows(all_slots(first_ref, COLUMNS)))

    def line_of(strip):
        return jnp.floor(strip / SEC_STRIPS)

    blocks = lines * WIN
    pair = iota((1, count), 1) // ROWS
    window = pair // sectors
    sector = (pair - window * sectors).astype(F32)
    line_col = (iota((blocks, 1), 0) // WIN).astype(F32)
    window_col = iota((blocks, 1), 0) % WIN
    strip_row = jnp.where((kind < 2) | (kind == 6), strip_rows[0], strip_rows[1])
    half_of = jnp.where(kind < 4, kind % 2, 1 - odd)
    slot_line = line_of(strip_row)
    slot_spot = sector * SEC_STRIPS + strip_row - slot_line * SEC_STRIPS
    base = (window == window_col) & (slot_line == line_col) & (strip_row >= 0.0)
    base = jnp.where(base & ((kind < 4) | (kind >= 6)), 1.0, 0.0)
    parts = []
    for half in range(2):
        part = jnp.where(half_of == half, base, 0.0)
        for j in range(strips):
            parts.append(jnp.where(slot_spot == float(j), part, 0.0))
    for q in range(2):
        hit = (window == window_col) & (line_of(strip_rows[q]) == line_col) & (strip_rows[q] >= 0.0) & (kind == 5)
        parts.append(jnp.where(hit, 1.0, 0.0))
    place = jnp.concatenate(parts, axis=0).astype(BF16)
    place_ref[...] = jnp.concatenate([place, place, place], axis=1)

    block_hot_ref[...] = one_hot_bands(to_col(band_ref[...].astype(F32)))

    info = info_ref[...]
    col_of = info[:, COL : COL + 1]
    col_row = to_row(col_of)
    same = jnp.where(col_of == col_row, 1.0, 0.0)
    before = jnp.where(iota((SLOTS, SLOTS), 1) < iota((SLOTS, SLOTS), 0), 1.0, 0.0)
    first = jnp.where(jnp.sum(same * before, axis=1, keepdims=True) > 0.0, 0.0, 1.0)
    owner = jnp.floor(col_of / strips_owner)
    owner_row = jnp.floor(col_row / strips_owner)
    rank = jnp.sum(jnp.where(owner == owner_row, before, 0.0), axis=1, keepdims=True)

    at = iota((SLOTS, LANES), 1)
    rank_ref[...] = jnp.where(at == 0, rank, jnp.where(at == 1, first, 0.0))
    shape = (owners * ROWS, 3 * PARTS * SLOTS)
    target = (iota(shape, 0) // ROWS).astype(F32)
    kind = iota(shape, 0) % ROWS
    place = iota(shape, 1) % (PARTS * SLOTS)
    group = place // SLOTS
    slim_shape = (SLOTS, shape[1])
    slim = iota(slim_shape, 1) % SLOTS == iota(slim_shape, 0)
    owner_wide = jnp.sum(jnp.where(slim, owner, 0.0), axis=0, keepdims=True)
    rank_wide = jnp.sum(jnp.where(slim, rank, 0.0), axis=0, keepdims=True)
    kind_f = kind.astype(F32)
    hit = (group == 0) & (kind_f == 2.0 * rank_wide)
    hit = hit | ((group == 1) & (kind_f == 2.0 * rank_wide + 1.0))
    hit = hit | ((group == 2) & (kind == 5))
    even = iota(shape, 0) // ROWS % 2 == 0
    hit = hit | ((group == 4) & (kind_f == 6.0 + rank_wide) & ~even)
    hit = hit | ((group == 5) & (kind_f == 6.0 + rank_wide) & even)
    hit = (hit & (owner_wide == target)) | ((place == 3 * SLOTS) & (kind == 4))
    send = jnp.where(hit, 1.0, 0.0).astype(BF16)
    send_ref[...] = send

    window = window_slots(first_ref, sectors)
    spot_row = window_row(window, S_SPOT)
    lane = iota((1, LANES), 1)
    line_row = jnp.where(lane < sectors * SLOTS, jnp.floor(window_row(window, S_STRIP) / SEC_STRIPS), -1.0)
    on_line = info[:, LINE : LINE + 1] == line_row
    sector = lax.rem(my_index, sectors).astype(F32)
    sector_row = jnp.floor(spot_row / SEC_STRIPS)
    lane = iota((SLOTS, LANES), 1)
    before = jnp.where(lane < iota((SLOTS, LANES), 0), 1.0, 0.0)
    earlier = jnp.where(lane < SLOTS, before, jnp.where(sector_row < sector, 1.0, 0.0))
    taken = jnp.sum(jnp.where(on_line, earlier, 0.0), axis=1, keepdims=True)
    lead_ref[...] = jnp.broadcast_to(jnp.where(taken > 0.0, 0.0, 1.0), lead_ref.shape)


def finish_kernel(
    strips,
    owners,
    first_ref,
    third_ref,
    values_ref,
    obs_ref,
    place_ref,
    band_hot_ref,
    scaled_ref,
    block_hot_ref,
    decay_ref,
    weight_ref,
    out_ref,
    misfit_ref,
):
    sectors = strips // SEC_STRIPS
    blocks = NLAT // owners * WIN
    count = owners * ROWS
    window = lax.axis_index("tile") // sectors
    differ = values_ref[...].T[MISFIT : MISFIT + SB_DEV, :] - obs_ref[...]
    partials = weekly([third_ref[t, 4:5, :] for t in range(owners)], sectors)
    combined, carried = background(first_ref, partials, decay_ref[...], sectors)
    spread = jnp.concatenate(
        [jnp.broadcast_to(row, (sectors * ROWS, NBANDS)) for row in combined], axis=0
    )
    scalars = jnp.sum(band_hot_ref[...] * spread, axis=1, keepdims=True)
    third = third_ref[...].reshape(count, LANES)
    kind = iota((count, 1), 0) % ROWS
    rows = jnp.where(kind >= 6, -STEP * (scalars * third), third - scalars * scaled_ref[...])
    placed = dot(place_ref[...], split_rows(rows))
    offset = jnp.sum(block_hot_ref[...] * pick(carried, window), axis=1, keepdims=True)
    misfit_ref[...] = differ + offset

    lane = iota((1, LANES), 1)
    for j in range(strips):
        start = (strips + j) * LANES
        values = placed[(strips + j) * blocks : (strips + j + 1) * blocks]
        out_ref[:, start : start + LANES] = shrink(values, STEP * weight_ref[0:1, start : start + LANES])

    low = [placed[j * blocks : (j + 1) * blocks] for j in range(strips)]
    tops = [placed[(2 * strips + q) * blocks : (2 * strips + q + 1) * blocks] for q in range(2)]
    top = pltpu.roll(tops[0], LANES - ROWS, 1) + pltpu.roll(tops[1], LANES // 2 - ROWS, 1)
    made = [jnp.zeros((blocks, LANES), F32) for _ in range(strips)]
    for t in range(strips):
        value = jnp.zeros((blocks, 1), F32)
        for j in range(strips):
            entry = top_value(j, t, strips)
            if entry:
                value = value + entry * low[j][:, 0:1]
        made[0] = jnp.where(lane == t, value + top, made[0])
    m = 1
    while m < LANES:
        for j in range(strips):
            start = strips * m + j * m
            block = start // LANES
            shift = (start % LANES - m) % LANES
            moved = pltpu.roll(low[j], shift, 1) if shift else low[j]
            inside = (lane >= start % LANES) & (lane < start % LANES + m)
            made[block] = jnp.where(inside, moved, made[block])
        m *= 2
    for block in range(strips):
        start = block * LANES
        out_ref[:, start : start + LANES] = shrink(made[block], STEP * weight_ref[0:1, start : start + LANES])


def top_value(spot, index, strips):
    if index == 0:
        return math.sqrt(1.0 / strips)
    m = 1 << (index.bit_length() - 1)
    span = strips // m
    within = spot - (index - m) * span
    if within < 0 or within >= span:
        return 0.0
    return math.sqrt(m / strips) * (1.0 if within < span // 2 else -1.0)


def call(kernel, outs, *operands, **kwargs):
    return pl.pallas_call(
        kernel,
        out_shape=[jax.ShapeDtypeStruct(shape, dtype) for shape, dtype in outs],
        compiler_params=pltpu.CompilerParams(vmem_limit_bytes=40 * 1024 * 1024),
        **kwargs,
    )(*operands)


def body(
    observations,
    jacobian,
    block_row,
    block_col,
    block_count,
    block_band,
    carry_decay,
    sparsity_weight,
):
    owners = lax.axis_size("tile")
    sectors = owners // WIN
    strips = sectors * SEC_STRIPS
    lines = NLAT // owners
    betas = momentum_weights(ITERS)
    arguments = [
        block_band.reshape(1, SB_DEV),
        observations,
        block_row.reshape(1, SLOTS),
        block_col.reshape(1, SLOTS),
        sparsity_weight.reshape(1, -1),
        carry_decay.reshape(1, NBANDS),
        jacobian.reshape(SLOTS * SOUNDS, STRIP),
    ]
    message = ((owners, ROWS, LANES), F32)
    narrow = ((SLOTS, LANES), F32)
    strip_rows = ((SLOTS, STRIP), F32)

    def trade(values):
        return lax.all_to_all(values, "tile", 0, 0, tiled=True)

    def with_sectors(values):
        found = [values]
        for shift in range(1, sectors):
            pairs = [
                (d, d // sectors * sectors + (d + shift) % sectors) for d in range(owners)
            ]
            found.append(lax.ppermute(values, "tile", pairs))
        return found

    arguments = [pltpu.with_memory_space_constraint(a, pltpu.HBM) for a in arguments]
    outs = [
        ((1, SB_DEV), jnp.int32),
        ((SB_DEV, SOUNDS), F32),
        ((1, strips * STRIP), F32),
        ((1, NBANDS), F32),
        ((SLOTS * SOUNDS, STRIP), F32),
        strip_rows,
        strip_rows,
        strip_rows,
        ((SOUNDS, LANES), F32),
        narrow,
        narrow,
        strip_rows,
        ((2 * strips, LANES), F32),
        ((SLOTS, SLOTS), F32),
        narrow,
        ((owners, FIRST_BLOCKS, BLOCK, LANES), F32),
    ]
    (
        bands,
        observed,
        weight,
        decay,
        blocks,
        column,
        twin,
        start_grad,
        obs_slot,
        mix,
        info,
        limit,
        limit_rows,
        strip_match,
        top_matrix,
        first,
    ) = call(
        functools.partial(open_kernel, strips, owners),
        outs,
        *arguments,
        block_count,
        in_specs=[pl.BlockSpec(memory_space=pltpu.HBM)] * len(arguments)
        + [pl.BlockSpec(memory_space=pltpu.SMEM)],
        scratch_shapes=[
            pltpu.VMEM((1, SLOTS), jnp.int32),
            pltpu.VMEM((1, SLOTS), jnp.int32),
            pltpu.VMEM((SLOTS * SOUNDS, STRIP), F32),
            pltpu.SemaphoreType.DMA((len(arguments) - 1 + PIECES,)),
        ],
    )
    first = trade(first)
    point, top, share, hot, line_tops, grad = call(
        functools.partial(first_step_kernel, strips, owners),
        [
            strip_rows,
            narrow,
            ((2 * ROWS, LANES), F32),
            ((sectors * SLOTS, NBANDS), F32),
            ((strips * SLOTS, LANES), F32),
            strip_rows,
        ],
        first,
        info,
        column,
        twin,
        start_grad,
        limit,
        limit_rows,
        strip_match,
        top_matrix,
        decay,
        weight,
        blocks,
        mix,
        obs_slot,
    )
    placed_rows = (2 * strips + 2) * lines * WIN
    *tables, send, rank, lead = call(
        functools.partial(place_kernel, strips, owners),
        [
            ((placed_rows, 3 * owners * ROWS), BF16),
            ((owners * ROWS, NBANDS), F32),
            ((owners * ROWS, LANES), F32),
            ((SB_DEV, NBANDS), F32),
            ((owners * ROWS, 3 * PARTS * SLOTS), BF16),
            narrow,
            narrow,
        ],
        first,
        bands,
        info,
    )
    third, values = call(
        functools.partial(second_step_kernel, strips, owners, betas[1]),
        [message, ((SOUNDS, LANES), F32)],
        first,
        info,
        column,
        twin,
        grad,
        limit,
        strip_match,
        top_matrix,
        decay,
        weight,
        hot,
        line_tops,
        lead,
        rank,
        send,
        point,
        top,
        blocks,
        mix,
        obs_slot,
        *with_sectors(share),
    )
    third = trade(third)
    coeffs, misfit = call(
        functools.partial(finish_kernel, strips, owners),
        [((lines * WIN, strips * STRIP), F32), ((SB_DEV, SOUNDS), F32)],
        first,
        third,
        values,
        observed,
        *tables,
        decay,
        weight,
    )
    return (coeffs.reshape(lines, WIN, strips * STRIP), misfit)


def solution(mesh):
    return jax.shard_map(
        body,
        mesh=mesh,
        in_specs=(
            P(("ens", "tile"), None),
            P("tile", None, None),
            P("tile"),
            P("tile"),
            P("tile"),
            P("tile"),
            P(),
            P(),
        ),
        out_specs=(P(("ens", "tile"), None, None), P(("ens", "tile"), None)),
        check_vma=False,
    )
```

```python
import functools
import math

import jax
import jax.numpy as jnp
from jax import lax
from jax.experimental import pallas as pl
from jax.experimental.pallas import tpu as pltpu
from jax.sharding import PartitionSpec as P

WIN = 8
NLAT = 64
SEC_STRIPS = 2
STRIP = 256
SOUNDS = 64
SB_DEV = 32
NBANDS = 128
ITERS = 3
SLOTS = 16
LANES = 128
ROWS = 8
STEP = 0.2
MISFIT = 32
PARTS = 4
PIECES = 1

F32 = jnp.float32
BF16 = jnp.bfloat16
HIGHEST = lax.Precision.HIGHEST

LINE, SPOT, BAND, COL, VALID = range(5)
BLOCK = 4
GRADS, COLUMNS, SINGLES = 0, SLOTS // BLOCK, 2 * SLOTS // BLOCK
COUNTS, SUMS, SLOT_ROW = range(3)
FIRST_BLOCKS = SINGLES + 1
S_STRIP, S_SPOT, S_BAND, S_VALID, S_TOTAL, S_APPROX = (i * SLOTS for i in range(6))


def momentum_weights(total_steps):
    weights = []
    current = 1.0
    for _ in range(total_steps):
        following = (1.0 + math.sqrt(1.0 + 4.0 * current * current)) / 2.0
        weights.append((current - 1.0) / following)
        current = following
    return weights


def iota(shape, axis):
    return lax.broadcasted_iota(jnp.int32, shape, axis)


def shrink(values, limit):
    return values - jnp.minimum(jnp.maximum(values, -limit), limit)


def to_col(row):
    n = row.shape[1]
    eye = iota((n, n), 0) == iota((n, n), 1)
    return jnp.sum(jnp.where(eye, row, 0.0), axis=1, keepdims=True)


def to_row(col):
    n = col.shape[0]
    eye = iota((n, n), 0) == iota((n, n), 1)
    return jnp.sum(jnp.where(eye, col, 0.0), axis=0, keepdims=True)


def exact_dot(left, right):
    return jnp.dot(left, right, precision=HIGHEST, preferred_element_type=F32)


def dot(left, right):
    return jnp.dot(left, right, preferred_element_type=F32)


def dot_nt(left, right):
    return lax.dot_general(left, right, (((1,), (1,)), ((), ())), preferred_element_type=F32)


def split(values):
    high = values.astype(BF16)
    return high, (values - high.astype(F32)).astype(BF16)


def split_parts(values):
    high = values.astype(BF16)
    rest = values - high.astype(F32)
    middle = rest.astype(BF16)
    return [high, middle, (rest - middle.astype(F32)).astype(BF16)]


def split_rows(values):
    return jnp.concatenate(split_parts(values), axis=0)


def haar_signs():
    coef = iota((1, STRIP), 1).astype(F32)
    level = jnp.zeros((1, STRIP), F32) + 1.0
    m = 2
    while m < STRIP:
        level = jnp.where(coef >= m, float(m), level)
        m *= 2
    first = coef == 0.0
    shift = jnp.where(first, 0.0, coef - level)
    half = jnp.where(first, 2.0, 0.5)
    within = iota((STRIP, STRIP), 0).astype(F32) * (level / STRIP) - shift
    inside = (within >= 0.0) & (within < 1.0)
    return jnp.where(inside, jnp.where(within < half, 1.0, -1.0), 0.0).astype(BF16)


def haar_scales():
    coef = iota((1, STRIP), 1)
    out = jnp.full((1, STRIP), math.sqrt(1.0 / STRIP), F32)
    m = 1
    while m < STRIP:
        out = jnp.where((coef >= m) & (coef < 2 * m), math.sqrt(m / STRIP), out)
        m *= 2
    return out


def top_entry(spot, index, strips):
    if index == 0:
        return jnp.full(spot.shape, math.sqrt(1.0 / strips), F32)
    m = 1 << (index.bit_length() - 1)
    span = strips // m
    start = float((index - m) * span)
    half = start + span / 2
    end = start + span
    scale = math.sqrt(m / strips)
    positive = (spot >= start) & (spot < half)
    negative = (spot >= half) & (spot < end)
    return jnp.where(positive, scale, jnp.where(negative, -scale, 0.0))


def weekly(rows, sectors):
    return [sum(rows[w * sectors + 1 : (w + 1) * sectors], rows[w * sectors]) for w in range(WIN)]


def scan_back(totals, decay):
    running = totals[WIN - 1]
    out = [running]
    for w in range(WIN - 2, -1, -1):
        running = running * decay + totals[w]
        out.insert(0, running)
    return out


def scan_ahead(totals, decay):
    running = totals[0]
    out = [running]
    for w in range(1, WIN):
        running = running * decay + totals[w]
        out.append(running)
    return out


def pick(rows, index):
    out = rows[0]
    for w in range(1, len(rows)):
        out = jnp.where(index == w, rows[w], out)
    return out


def background(first, partials, decay, sectors):
    pairs = range(WIN * sectors)
    counts = weekly([first[t, SINGLES, COUNTS : COUNTS + 1, :] for t in pairs], sectors)
    sums = weekly([first[t, SINGLES, SUMS : SUMS + 1, :] for t in pairs], sectors)
    carried = scan_ahead(partials, decay)
    back = [
        SOUNDS * partials[w] + (SOUNDS * counts[w]) * carried[w] - sums[w] for w in range(WIN)
    ]
    returned = scan_back(back, decay)
    return [carried[w] + returned[w] / SOUNDS for w in range(WIN)], carried


def one_hot_bands(band_col):
    return jnp.where(band_col == iota((band_col.shape[0], NBANDS), 1).astype(F32), 1.0, 0.0)


def forward(point, blocks_ref, mix):
    total = None
    for k in range(SLOTS):
        product = blocks_ref[k * SOUNDS : (k + 1) * SOUNDS, :] * point[k : k + 1, :]
        values = jnp.sum(product[:, :LANES] + product[:, LANES:], axis=1, keepdims=True)
        term = values * mix[k : k + 1, :]
        total = term if total is None else total + term
    return total


def back_rows(chosen, blocks_ref):
    return [
        jnp.sum(
            blocks_ref[k * SOUNDS : (k + 1) * SOUNDS, :] * chosen[:, k : k + 1],
            axis=0,
            keepdims=True,
        )
        for k in range(SLOTS)
    ]


def stack_rows(rows):
    at = iota((SLOTS, STRIP), 0)
    out = jnp.broadcast_to(rows[0], (SLOTS, STRIP))
    for k in range(1, SLOTS):
        out = jnp.where(at == k, rows[k], out)
    return out


def mix_rows(match, rows):
    out = match[:, 0:1] * rows[0]
    for k in range(1, SLOTS):
        out = out + match[:, k : k + 1] * rows[k]
    return out


def along_lanes(col):
    n = col.shape[0]
    here = iota((n, LANES), 0) == iota((n, LANES), 1)
    return jnp.sum(jnp.where(here, col, 0.0), axis=0, keepdims=True)


def open_kernel(
    strips,
    owners,
    band_in,
    obs_in,
    row_in,
    col_in,
    weight_in,
    decay_in,
    jac_in,
    count_ref,
    band_ref,
    obs_ref,
    weight_ref,
    decay_ref,
    blocks_ref,
    column_ref,
    twin_ref,
    start_grad_ref,
    obs_slot_ref,
    mix_ref,
    info_ref,
    limit_ref,
    limit_rows_ref,
    strip_match_ref,
    top_matrix_ref,
    message_ref,
    row_ref,
    col_ref,
    jac_ref,
    sems,
):
    piece = SLOTS * SOUNDS // PIECES
    moves = [
        (band_in, band_ref),
        (obs_in, obs_ref),
        (row_in, row_ref),
        (col_in, col_ref),
        (weight_in, weight_ref),
        (decay_in, decay_ref),
    ]
    for start in range(0, SLOTS * SOUNDS, piece):
        moves.append((jac_in.at[start : start + piece], jac_ref.at[start : start + piece]))
    copies = [pltpu.make_async_copy(a, b, sems.at[i]) for i, (a, b) in enumerate(moves)]
    for copy in copies:
        copy.start()
    sectors = strips // SEC_STRIPS
    sector = lax.rem(lax.axis_index("tile"), sectors).astype(F32)
    signs = haar_signs()
    scales = haar_scales()
    for copy in copies[:6]:
        copy.wait()

    band_row = band_ref[...].astype(F32)
    block_hot = one_hot_bands(to_col(band_row))
    counted = jnp.sum(block_hot, axis=0, keepdims=True)
    summed = jnp.sum(block_hot * jnp.sum(obs_ref[...], axis=1, keepdims=True), axis=0, keepdims=True)
    row_of = to_col(row_ref[...].astype(F32))
    col_row = col_ref[...].astype(F32)
    col_of = to_col(col_row)
    valid = jnp.where(iota((SLOTS, 1), 0) < count_ref[0], 1.0, 0.0)
    valid_row = jnp.where(iota((1, SLOTS), 1) < count_ref[0], 1.0, 0.0)
    line = jnp.floor(col_of / SEC_STRIPS)
    spot = sector * SEC_STRIPS + (col_of - line * SEC_STRIPS)
    row_hot = jnp.where(row_of == iota((SLOTS, SB_DEV), 1).astype(F32), 1.0, 0.0)
    band = jnp.sum(row_hot * band_row, axis=1, keepdims=True)
    band = jnp.where(valid > 0.0, band, -1.0)
    lane = iota((1, LANES), 1)
    wanted = jnp.where(lane < SLOTS, along_lanes(row_of), -1.0)
    wanted_hot = jnp.where(iota((SB_DEV, LANES), 0).astype(F32) == wanted, 1.0, 0.0)
    obs_slot = exact_dot(obs_ref[...].T, wanted_hot)
    obs_slot_ref[...] = obs_slot
    block_lane = (lane >= MISFIT) & (lane < MISFIT + SB_DEV)
    wanted = jnp.where(block_lane, (lane - MISFIT).astype(F32), wanted)
    mix_ref[...] = jnp.where(row_of == wanted, valid, 0.0)

    same = jnp.where(col_of == col_row, 1.0, 0.0)
    other = jnp.where(iota((SLOTS, SLOTS), 1) != iota((SLOTS, SLOTS), 0), same, 0.0)
    strip_match_ref[...] = same * valid_row
    at = iota((SLOTS, LANES), 1)
    info = jnp.zeros((SLOTS, LANES), F32)
    for place, values in ((LINE, line), (SPOT, spot), (BAND, band), (COL, col_of), (VALID, valid)):
        info = jnp.where(at == place, values, info)
    info_ref[...] = info
    matrix = jnp.zeros((SLOTS, LANES), F32)
    for t in range(strips):
        matrix = jnp.where(at == t, top_entry(spot, t, strips), matrix)
    top_matrix_ref[...] = matrix

    local = iota((1, LANES), 1)
    limits_low = jnp.zeros((SLOTS, LANES), F32)
    limits_high = jnp.zeros((SLOTS, LANES), F32)
    for j in range(strips):
        low_row = jnp.zeros((1, LANES), F32)
        m = 1
        while m < LANES:
            start = strips * m + j * m
            block = weight_ref[0:1, start // LANES * LANES : start // LANES * LANES + LANES]
            shift = (m - start % LANES) % LANES
            moved = pltpu.roll(jnp.broadcast_to(block, (ROWS, LANES)), shift, 1)[0:1] if shift else block
            low_row = jnp.where((local >= m) & (local < 2 * m), moved, low_row)
            m *= 2
        high_row = weight_ref[0:1, (strips + j) * LANES : (strips + j + 1) * LANES]
        limit_rows_ref[j : j + 1, :] = STEP * low_row
        limit_rows_ref[strips + j : strips + j + 1, :] = STEP * high_row
        limits_low = jnp.where(spot == float(j), low_row, limits_low)
        limits_high = jnp.where(spot == float(j), high_row, limits_high)
    limit_ref[:, :LANES] = STEP * limits_low
    limit_ref[:, LANES:] = STEP * limits_high

    per = SLOTS // PIECES
    grads = []
    ones = []
    for part in range(PIECES):
        copies[6 + part].wait()
        for start in range(part * piece, part * piece + piece, STRIP):
            high, low = split(jac_ref[start : start + STRIP, :])
            blocks_ref[start : start + STRIP, :] = (dot(high, signs) + dot(low, signs)) * scales
        for k in range(part * per, part * per + per):
            block = blocks_ref[k * SOUNDS : (k + 1) * SOUNDS, :]
            grads.append(jnp.sum(block * obs_slot[:, k : k + 1], axis=0, keepdims=True))
            ones.append(jnp.sum(block, axis=0, keepdims=True))
    obs_grad = -stack_rows(grads)
    column = stack_rows(ones) * valid
    column_ref[...] = column
    start_grad_ref[...] = mix_rows(same * valid_row, [-g for g in grads])
    twin_ref[...] = mix_rows(other, [column[k : k + 1, :] for k in range(SLOTS)])

    slots = jnp.zeros((1, LANES), F32)
    for base, values in (
        (S_STRIP, col_of),
        (S_SPOT, spot),
        (S_BAND, band),
        (S_VALID, valid),
        (S_TOTAL, column[:, 0:1]),
        (S_APPROX, obs_grad[:, 0:1] * valid),
    ):
        slots = slots + moved_lanes(along_lanes(values), base)
    singles = jnp.concatenate([counted, summed, slots, jnp.zeros((1, LANES), F32)], axis=0)
    for t in range(owners):
        lanes = slice(t % 2 * LANES, t % 2 * LANES + LANES)
        for i in range(SLOTS // BLOCK):
            rows = slice(i * BLOCK, (i + 1) * BLOCK)
            message_ref[t, GRADS + i] = obs_grad[rows, lanes]
            message_ref[t, COLUMNS + i] = column[rows, lanes]
        message_ref[t, SINGLES] = singles


def moved_lanes(row, by):
    by = by % LANES
    return pltpu.roll(jnp.broadcast_to(row, (ROWS, LANES)), by, 1)[0:1] if by else row


def window_row(rows, base):
    lane = iota((1, LANES), 1)
    out = jnp.zeros((1, LANES), F32)
    for i, row in enumerate(rows):
        inside = (lane >= i * SLOTS) & (lane < (i + 1) * SLOTS)
        out = jnp.where(inside, moved_lanes(row, i * SLOTS - base), out)
    return out


def thrice(match):
    return jnp.concatenate([match] * 3, axis=1).astype(BF16)


def message_rows(send, strips_part, meta, partial):
    bottom = jnp.where(iota((SLOTS, LANES), 0) == 0, partial, 0.0)
    stacked = jnp.concatenate([strips_part[:, :LANES], strips_part[:, LANES:], meta, bottom], axis=0)
    return dot(send, split_rows(stacked))


def side_by_side(rows):
    out = rows[0]
    for i, row in enumerate(rows[1:], 1):
        wide = jnp.broadcast_to(row, (ROWS, LANES))
        out = out + pltpu.roll(wide, i * SLOTS, 1)[0:1]
    return out


def slot_scalars(hot, scalar):
    col = jnp.sum(hot * scalar, axis=1, keepdims=True)
    return col, along_lanes(col)


def advance(strips, col, row, grads, column, twin, same, approx_row, total_row, line_tops):
    other = jnp.sum(jnp.where(same > 0.0, row[:, :SLOTS], 0.0), axis=1, keepdims=True)
    full = grads + col[:SLOTS] * column + other * twin
    sources = approx_row + row * total_row
    at = iota((SLOTS, LANES), 1)
    top_grad = jnp.zeros((SLOTS, LANES), F32)
    for t in range(strips):
        value = jnp.sum(line_tops[t * SLOTS : (t + 1) * SLOTS] * sources, axis=1, keepdims=True)
        top_grad = jnp.where(at == t, value, top_grad)
    return full, top_grad


def with_approx(point, top, matrix):
    approx = jnp.sum(matrix * top, axis=1, keepdims=True)
    return jnp.where(iota((SLOTS, STRIP), 1) == 0, approx, point)


def band_partial(point, column, hot):
    dots = jnp.sum(point * column, axis=1, keepdims=True)
    return jnp.sum(hot * dots, axis=0, keepdims=True) / SOUNDS


def twins(strip_match):
    return jnp.where(iota((SLOTS, SLOTS), 0) == iota((SLOTS, SLOTS), 1), 0.0, strip_match)


def all_slots(first_ref, start):
    return jnp.concatenate(
        [first_ref[d, start + i] for d in range(first_ref.shape[0]) for i in range(SLOTS // BLOCK)], axis=0
    )


def everyones_step(strips, owners, first_ref, scalars, limit_rows_ref, top_limit, share_ref):
    sectors = strips // SEC_STRIPS
    odd = lax.rem(lax.axis_index("tile"), 2)
    lane = iota((1, LANES), 1)
    count = sectors * SLOTS
    slots = first_ref[:, SINGLES, SLOT_ROW, :]
    tall = slots.T

    def col(base):
        return jnp.concatenate([tall[base : base + SLOTS, d : d + 1] for d in range(owners)], axis=0)

    def rows(base):
        turned = []
        for i in range(sectors):
            by = (i * SLOTS - base) % LANES
            turned.append(pltpu.roll(slots, by, 1) if by else slots)
        out = []
        for w in range(WIN):
            row = turned[0][w * sectors : w * sectors + 1, :]
            for i in range(1, sectors):
                d = w * sectors + i
                row = jnp.where(lane >= i * SLOTS, turned[i][d : d + 1, :], row)
            out.append(row[:, :count])
        return out

    def part(values, w):
        return values[w * count : (w + 1) * count]

    strip = col(S_STRIP)
    spot = col(S_SPOT)
    hot = one_hot_bands(col(S_BAND))
    spread = jnp.concatenate([jnp.broadcast_to(s, (count, NBANDS)) for s in scalars], axis=0)
    along = jnp.sum(hot * spread, axis=1, keepdims=True)
    column = all_slots(first_ref, COLUMNS)
    grads = all_slots(first_ref, GRADS) + along * column
    matrix = jnp.zeros((owners * SLOTS, LANES), F32)
    limit = jnp.zeros((owners * SLOTS, LANES), F32)
    for j in range(strips):
        entries = jnp.zeros((1, LANES), F32)
        for t in range(strips):
            entries = jnp.where(lane == t, top_value(j, t, strips), entries)
        low, high = limit_rows_ref[j : j + 1, :], limit_rows_ref[strips + j : strips + j + 1, :]
        here = spot == float(j)
        matrix = jnp.where(here, entries, matrix)
        limit = jnp.where(here, jnp.where(odd == 0, low, high), limit)
    fronts = (grads[:, 0:1] * col(S_VALID)) * matrix
    parts = split(jnp.concatenate([grads, fronts], axis=1))
    strip_rows = rows(S_STRIP)
    spot_rows = rows(S_SPOT)
    valid_rows = rows(S_VALID)
    full = []
    top_grad = []
    for w in range(WIN):
        line = jnp.floor(part(strip, w) / SEC_STRIPS)
        same_line = line == jnp.floor(strip_rows[w] / SEC_STRIPS)
        same_strip = same_line & (part(spot, w) == spot_rows[w])
        match = jnp.concatenate(
            [jnp.where(same_strip, valid_rows[w], 0.0), jnp.where(same_line, 1.0, 0.0)], axis=0
        ).astype(BF16)
        both = dot(match, part(parts[0], w)) + dot(match, part(parts[1], w))
        full.append(both[:count, :LANES])
        top_grad.append(both[count:, LANES:])
    full = jnp.concatenate(full, axis=0)
    top = shrink(-STEP * jnp.concatenate(top_grad, axis=0), top_limit)
    approx = jnp.sum(matrix * top, axis=1, keepdims=True)
    point = shrink(-STEP * full, limit)
    point = jnp.where((lane == 0) & (odd == 0), approx, point)
    dots = jnp.sum(point * column, axis=1, keepdims=True)
    weighed = hot * dots
    for w in range(WIN):
        share_ref[w : w + 1, :] = jnp.sum(part(weighed, w), axis=0, keepdims=True) / SOUNDS


def window_slots(first_ref, sectors):
    my_index = lax.axis_index("tile")
    base = my_index - lax.rem(my_index, sectors)
    rows = []
    for shift in range(sectors):
        pair = base + lax.rem(my_index - base + (sectors - shift), sectors)
        rows.append(first_ref[pair, SINGLES, SLOT_ROW : SLOT_ROW + 1, :])
    return rows


def first_step_kernel(
    strips,
    owners,
    first_ref,
    info_ref,
    column_ref,
    twin_ref,
    grad_ref,
    limit_ref,
    limit_rows_ref,
    strip_match_ref,
    top_matrix_ref,
    decay_ref,
    weight_ref,
    blocks_ref,
    mix_ref,
    obs_slot_ref,
    point_ref,
    top_ref,
    share_ref,
    hot_ref,
    line_tops_ref,
    grad_out_ref,
):
    sectors = strips // SEC_STRIPS
    my_index = lax.axis_index("tile")
    window = my_index // sectors
    top_limit = STEP * weight_ref[0:1, :LANES]
    sums = weekly([first_ref[t, SINGLES, SUMS : SUMS + 1, :] for t in range(owners)], sectors)
    scalars = [r / SOUNDS for r in scan_back([-s for s in sums], decay_ref[...])]

    info = info_ref[...]
    slots = window_slots(first_ref, sectors)
    lane = iota((1, LANES), 1)
    count = sectors * SLOTS
    hot = one_hot_bands(to_col(window_row(slots, S_BAND)[:, :count]))
    hot_ref[...] = hot
    spot_row = window_row(slots, S_SPOT)
    line_row = jnp.where(lane < count, jnp.floor(window_row(slots, S_STRIP) / SEC_STRIPS), -1.0)
    on_line = info[:, LINE : LINE + 1] == line_row
    line_tops = jnp.concatenate(
        [jnp.where(on_line, top_entry(spot_row, t, strips), 0.0) for t in range(strips)], axis=0
    )
    line_tops_ref[...] = line_tops
    column = column_ref[...]
    col, along = slot_scalars(hot, pick(scalars, window))
    grads, top_grad = advance(
        strips,
        col,
        along,
        grad_ref[...],
        column,
        twin_ref[...],
        twins(strip_match_ref[...]),
        window_row(slots, S_APPROX),
        window_row(slots, S_TOTAL),
        line_tops,
    )
    updated = shrink(-STEP * grads, limit_ref[...])
    top = shrink(-STEP * top_grad, top_limit)
    point = with_approx(updated, top, top_matrix_ref[...])
    point_ref[...] = point
    top_ref[...] = top
    everyones_step(strips, owners, first_ref, scalars, limit_rows_ref, top_limit, share_ref)
    chosen = forward(point, blocks_ref, mix_ref[...]) - obs_slot_ref[...]
    rows = back_rows(chosen, blocks_ref)
    grad_out_ref[...] = mix_rows(strip_match_ref[...], rows)
    at = iota((SLOTS, LANES), 0)
    fronts = jnp.broadcast_to(rows[0][:, :LANES], (SLOTS, LANES))
    for k in range(1, SLOTS):
        fronts = jnp.where(at == k, rows[k][:, :LANES], fronts)
    share_ref[WIN : WIN + 1, :] = along_lanes(fronts[:, 0:1] * info[:, VALID : VALID + 1])
    share_ref[WIN + 1 :, :] = jnp.zeros((ROWS - 1, LANES), F32)

def second_step_kernel(
    strips,
    owners,
    beta,
    first_ref,
    info_ref,
    column_ref,
    twin_ref,
    grad_ref,
    limit_ref,
    strip_match_ref,
    top_matrix_ref,
    decay_ref,
    weight_ref,
    hot_ref,
    line_tops_ref,
    lead_ref,
    rank_ref,
    send_ref,
    prepared_ref,
    point_ref,
    top_ref,
    blocks_ref,
    mix_ref,
    obs_slot_ref,
    *rest,
):
    sectors = strips // SEC_STRIPS
    shares, rest = rest[:sectors], rest[sectors:]
    message_ref, values_ref = rest
    my_index = lax.axis_index("tile")
    window = my_index // sectors
    odd = lax.rem(my_index, 2)
    totals = shares[0][0:WIN, :] + jnp.where(odd == 1, shares[1][0:WIN, :], shares[-1][0:WIN, :])
    combined, _ = background(first_ref, [totals[w : w + 1, :] for w in range(WIN)], decay_ref[...], sectors)
    hot = hot_ref[...]
    column = column_ref[...]
    col, along = slot_scalars(hot, pick(combined, window))
    grads, top_grad = advance(
        strips,
        col,
        along,
        grad_ref[...],
        column,
        twin_ref[...],
        twins(strip_match_ref[...]),
        side_by_side([share[WIN : WIN + 1, :] for share in shares]),
        window_row(window_slots(first_ref, sectors), S_TOTAL),
        line_tops_ref[...],
    )
    old = point_ref[...]
    old_top = top_ref[...]
    updated = shrink(old - STEP * grads, limit_ref[...])
    top = shrink(old_top - STEP * top_grad, STEP * weight_ref[0:1, :LANES])
    point = updated + beta * (updated - old)
    top = top + beta * (top - old_top)
    point = with_approx(point, top, top_matrix_ref[...])
    values = forward(point, blocks_ref, mix_ref[...])
    values_ref[...] = values
    grad = stack_rows(back_rows(values - obs_slot_ref[...], blocks_ref))

    partial = band_partial(point, column, hot[:SLOTS])
    info = info_ref[...]
    valid = info[:, VALID : VALID + 1]
    top = top * lead_ref[:, 0:1]
    rank = rank_ref[:, 0:1]
    meta = jnp.where(rank == 0.0, pltpu.roll(top, ROWS, 1), pltpu.roll(top, LANES // 2 + ROWS, 1))
    kept = jnp.where(iota((SLOTS, STRIP), 1) == 0, 0.0, point * rank_ref[:, 1:2])
    rows = message_rows(send_ref[...], kept - STEP * (valid * grad), meta, partial) + prepared_ref[...]
    message_ref[...] = rows.reshape(message_ref.shape)


def place_kernel(
    strips,
    owners,
    first_ref,
    band_ref,
    info_ref,
    column_ref,
    place_ref,
    band_hot_ref,
    scaled_ref,
    block_hot_ref,
    send_ref,
    rank_ref,
    lead_ref,
    prepared_ref,
):
    sectors = strips // SEC_STRIPS
    lines = NLAT // owners
    count = owners * ROWS
    my_index = lax.axis_index("tile")
    odd = lax.rem(my_index, 2)
    mine_at = my_index.astype(F32)
    strips_owner = NLAT * SEC_STRIPS // owners
    slots = first_ref[:, SINGLES, SLOT_ROW, :]
    lane = iota((owners, LANES), 1).astype(F32)
    mine = (lane < SLOTS) & (jnp.floor(slots / strips_owner) == mine_at)
    front = jnp.min(jnp.where(mine, lane, float(LANES)), axis=1, keepdims=True)
    back = jnp.max(jnp.where(mine, lane, -1.0), axis=1, keepdims=True)
    back = jnp.where(back > front, back, float(LANES))
    wide = (owners, count)
    pair_of = iota(wide, 1) // ROWS == iota(wide, 0)
    kind = iota((1, count), 1) % ROWS
    tall = (count, owners)
    tall_pair = iota(tall, 0) // ROWS == iota(tall, 1)
    tall_kind = iota((count, 1), 0) % ROWS
    strip_rows = []
    band_col = jnp.zeros((count, 1), F32)
    slot_col = jnp.zeros((count, 1), F32) - 1.0
    for q, at in enumerate((front, back)):
        strip = jnp.sum(jnp.where(lane == at, slots - mine_at * strips_owner + 1.0, 0.0), axis=1, keepdims=True)
        band = jnp.sum(jnp.where((lane == at + S_BAND) & (at < SLOTS), slots + 1.0, 0.0), axis=1, keepdims=True)
        strip_rows.append(jnp.sum(jnp.where(pair_of, strip, 0.0), axis=0, keepdims=True) - 1.0)
        band_tall = jnp.sum(jnp.where(tall_pair, to_row(band), 0.0), axis=1, keepdims=True)
        slot_tall = jnp.sum(jnp.where(tall_pair, to_row(at), 0.0), axis=1, keepdims=True)
        own_kind = (tall_kind == 2 * q) | (tall_kind == 2 * q + 1)
        band_col = jnp.where(own_kind | (tall_kind == 6 + q), band_tall, band_col)
        slot_col = jnp.where(tall_kind == 2 * q + odd, slot_tall, slot_col)
    band_hot_ref[...] = one_hot_bands(band_col - 1.0)
    square = (count, owners * SLOTS)
    of_pair = iota(square, 1) // SLOTS == iota(square, 0) // ROWS
    of_slot = (iota(square, 1) % SLOTS).astype(F32) == slot_col
    chosen = thrice(jnp.where(of_pair & of_slot, 1.0, 0.0))
    scaled_ref[...] = STEP * dot(chosen, split_rows(all_slots(first_ref, COLUMNS)))

    def line_of(strip):
        return jnp.floor(strip / SEC_STRIPS)

    blocks = lines * WIN
    pair = iota((1, count), 1) // ROWS
    window = pair // sectors
    sector = (pair - window * sectors).astype(F32)
    line_col = (iota((blocks, 1), 0) // WIN).astype(F32)
    window_col = iota((blocks, 1), 0) % WIN
    strip_row = jnp.where((kind < 2) | (kind == 6), strip_rows[0], strip_rows[1])
    half_of = jnp.where(kind < 4, kind % 2, 1 - odd)
    slot_line = line_of(strip_row)
    slot_spot = sector * SEC_STRIPS + strip_row - slot_line * SEC_STRIPS
    base = (window == window_col) & (slot_line == line_col) & (strip_row >= 0.0)
    base = jnp.where(base & ((kind < 4) | (kind >= 6)), 1.0, 0.0)
    parts = []
    for half in range(2):
        part = jnp.where(half_of == half, base, 0.0)
        for j in range(strips):
            parts.append(jnp.where(slot_spot == float(j), part, 0.0))
    for q in range(2):
        hit = (window == window_col) & (line_of(strip_rows[q]) == line_col) & (strip_rows[q] >= 0.0) & (kind == 5)
        parts.append(jnp.where(hit, 1.0, 0.0))
    place = jnp.concatenate(parts, axis=0).astype(BF16)
    place_ref[...] = jnp.concatenate([place, place, place], axis=1)

    block_hot_ref[...] = one_hot_bands(to_col(band_ref[...].astype(F32)))

    info = info_ref[...]
    col_of = info[:, COL : COL + 1]
    col_row = to_row(col_of)
    same = jnp.where(col_of == col_row, 1.0, 0.0)
    before = jnp.where(iota((SLOTS, SLOTS), 1) < iota((SLOTS, SLOTS), 0), 1.0, 0.0)
    first = jnp.where(jnp.sum(same * before, axis=1, keepdims=True) > 0.0, 0.0, 1.0)
    owner = jnp.floor(col_of / strips_owner)
    owner_row = jnp.floor(col_row / strips_owner)
    rank = jnp.sum(jnp.where(owner == owner_row, before, 0.0), axis=1, keepdims=True)

    at = iota((SLOTS, LANES), 1)
    rank_ref[...] = jnp.where(at == 0, rank, jnp.where(at == 1, first, 0.0))
    shape = (owners * ROWS, 3 * PARTS * SLOTS)
    target = (iota(shape, 0) // ROWS).astype(F32)
    kind = iota(shape, 0) % ROWS
    place = iota(shape, 1) % (PARTS * SLOTS)
    group = place // SLOTS
    slim_shape = (SLOTS, shape[1])
    slim = iota(slim_shape, 1) % SLOTS == iota(slim_shape, 0)
    owner_wide = jnp.sum(jnp.where(slim, owner, 0.0), axis=0, keepdims=True)
    rank_wide = jnp.sum(jnp.where(slim, rank, 0.0), axis=0, keepdims=True)
    kind_f = kind.astype(F32)
    hit = (group == 0) & (kind_f == 2.0 * rank_wide)
    hit = hit | ((group == 1) & (kind_f == 2.0 * rank_wide + 1.0))
    hit = hit | ((group == 2) & (kind == 5))
    hit = (hit & (owner_wide == target)) | ((place == 3 * SLOTS) & (kind == 4))
    send = jnp.where(hit, 1.0, 0.0).astype(BF16)
    send_ref[...] = send
    lower = (group == 0) & (kind_f == 6.0 + rank_wide) & (iota(shape, 0) // ROWS % 2 == 1)
    upper = (group == 1) & (kind_f == 6.0 + rank_wide) & (iota(shape, 0) // ROWS % 2 == 0)
    hit = (lower | upper) & (owner_wide == target)
    column = column_ref[...]
    zeros = jnp.zeros((2 * SLOTS, LANES), F32)
    stacked = jnp.concatenate([column[:, :LANES], column[:, LANES:], zeros], axis=0)
    prepared_ref[...] = dot(jnp.where(hit, 1.0, 0.0).astype(BF16), split_rows(stacked))

    window = window_slots(first_ref, sectors)
    spot_row = window_row(window, S_SPOT)
    lane = iota((1, LANES), 1)
    line_row = jnp.where(lane < sectors * SLOTS, jnp.floor(window_row(window, S_STRIP) / SEC_STRIPS), -1.0)
    on_line = info[:, LINE : LINE + 1] == line_row
    sector = lax.rem(my_index, sectors).astype(F32)
    sector_row = jnp.floor(spot_row / SEC_STRIPS)
    lane = iota((SLOTS, LANES), 1)
    before = jnp.where(lane < iota((SLOTS, LANES), 0), 1.0, 0.0)
    earlier = jnp.where(lane < SLOTS, before, jnp.where(sector_row < sector, 1.0, 0.0))
    taken = jnp.sum(jnp.where(on_line, earlier, 0.0), axis=1, keepdims=True)
    lead_ref[...] = jnp.broadcast_to(jnp.where(taken > 0.0, 0.0, 1.0), lead_ref.shape)


def finish_kernel(
    strips,
    owners,
    first_ref,
    third_ref,
    values_ref,
    obs_ref,
    place_ref,
    band_hot_ref,
    scaled_ref,
    block_hot_ref,
    decay_ref,
    weight_ref,
    out_ref,
    misfit_ref,
):
    sectors = strips // SEC_STRIPS
    blocks = NLAT // owners * WIN
    count = owners * ROWS
    window = lax.axis_index("tile") // sectors
    differ = values_ref[...].T[MISFIT : MISFIT + SB_DEV, :] - obs_ref[...]
    partials = weekly([third_ref[t, 4:5, :] for t in range(owners)], sectors)
    combined, carried = background(first_ref, partials, decay_ref[...], sectors)
    spread = jnp.concatenate(
        [jnp.broadcast_to(row, (sectors * ROWS, NBANDS)) for row in combined], axis=0
    )
    scalars = jnp.sum(band_hot_ref[...] * spread, axis=1, keepdims=True)
    third = third_ref[...].reshape(count, LANES)
    kind = iota((count, 1), 0) % ROWS
    rows = jnp.where(kind >= 6, -STEP * (scalars * third), third - scalars * scaled_ref[...])
    placed = dot(place_ref[...], split_rows(rows))
    offset = jnp.sum(block_hot_ref[...] * pick(carried, window), axis=1, keepdims=True)
    misfit_ref[...] = differ + offset

    lane = iota((1, LANES), 1)
    for j in range(strips):
        start = (strips + j) * LANES
        values = placed[(strips + j) * blocks : (strips + j + 1) * blocks]
        out_ref[:, start : start + LANES] = shrink(values, STEP * weight_ref[0:1, start : start + LANES])

    low = [placed[j * blocks : (j + 1) * blocks] for j in range(strips)]
    tops = [placed[(2 * strips + q) * blocks : (2 * strips + q + 1) * blocks] for q in range(2)]
    top = pltpu.roll(tops[0], LANES - ROWS, 1) + pltpu.roll(tops[1], LANES // 2 - ROWS, 1)
    made = [jnp.zeros((blocks, LANES), F32) for _ in range(strips)]
    for t in range(strips):
        value = jnp.zeros((blocks, 1), F32)
        for j in range(strips):
            entry = top_value(j, t, strips)
            if entry:
                value = value + entry * low[j][:, 0:1]
        made[0] = jnp.where(lane == t, value + top, made[0])
    m = 1
    while m < LANES:
        for j in range(strips):
            start = strips * m + j * m
            block = start // LANES
            shift = (start % LANES - m) % LANES
            moved = pltpu.roll(low[j], shift, 1) if shift else low[j]
            inside = (lane >= start % LANES) & (lane < start % LANES + m)
            made[block] = jnp.where(inside, moved, made[block])
        m *= 2
    for block in range(strips):
        start = block * LANES
        out_ref[:, start : start + LANES] = shrink(made[block], STEP * weight_ref[0:1, start : start + LANES])


def top_value(spot, index, strips):
    if index == 0:
        return math.sqrt(1.0 / strips)
    m = 1 << (index.bit_length() - 1)
    span = strips // m
    within = spot - (index - m) * span
    if within < 0 or within >= span:
        return 0.0
    return math.sqrt(m / strips) * (1.0 if within < span // 2 else -1.0)


def call(kernel, outs, *operands, **kwargs):
    return pl.pallas_call(
        kernel,
        out_shape=[jax.ShapeDtypeStruct(shape, dtype) for shape, dtype in outs],
        compiler_params=pltpu.CompilerParams(vmem_limit_bytes=40 * 1024 * 1024),
        **kwargs,
    )(*operands)


def body(
    observations,
    jacobian,
    block_row,
    block_col,
    block_count,
    block_band,
    carry_decay,
    sparsity_weight,
):
    owners = lax.axis_size("tile")
    sectors = owners // WIN
    strips = sectors * SEC_STRIPS
    lines = NLAT // owners
    betas = momentum_weights(ITERS)
    arguments = [
        block_band.reshape(1, SB_DEV),
        observations,
        block_row.reshape(1, SLOTS),
        block_col.reshape(1, SLOTS),
        sparsity_weight.reshape(1, -1),
        carry_decay.reshape(1, NBANDS),
        jacobian.reshape(SLOTS * SOUNDS, STRIP),
    ]
    message = ((owners, ROWS, LANES), F32)
    narrow = ((SLOTS, LANES), F32)
    strip_rows = ((SLOTS, STRIP), F32)

    def trade(values):
        return lax.all_to_all(values, "tile", 0, 0, tiled=True)

    def with_sectors(values):
        found = [values]
        for shift in range(1, sectors):
            pairs = [
                (d, d // sectors * sectors + (d + shift) % sectors) for d in range(owners)
            ]
            found.append(lax.ppermute(values, "tile", pairs))
        return found

    arguments = [pltpu.with_memory_space_constraint(a, pltpu.HBM) for a in arguments]
    outs = [
        ((1, SB_DEV), jnp.int32),
        ((SB_DEV, SOUNDS), F32),
        ((1, strips * STRIP), F32),
        ((1, NBANDS), F32),
        ((SLOTS * SOUNDS, STRIP), F32),
        strip_rows,
        strip_rows,
        strip_rows,
        ((SOUNDS, LANES), F32),
        narrow,
        narrow,
        strip_rows,
        ((2 * strips, LANES), F32),
        ((SLOTS, SLOTS), F32),
        narrow,
        ((owners, FIRST_BLOCKS, BLOCK, LANES), F32),
    ]
    (
        bands,
        observed,
        weight,
        decay,
        blocks,
        column,
        twin,
        start_grad,
        obs_slot,
        mix,
        info,
        limit,
        limit_rows,
        strip_match,
        top_matrix,
        first,
    ) = call(
        functools.partial(open_kernel, strips, owners),
        outs,
        *arguments,
        block_count,
        in_specs=[pl.BlockSpec(memory_space=pltpu.HBM)] * len(arguments)
        + [pl.BlockSpec(memory_space=pltpu.SMEM)],
        scratch_shapes=[
            pltpu.VMEM((1, SLOTS), jnp.int32),
            pltpu.VMEM((1, SLOTS), jnp.int32),
            pltpu.VMEM((SLOTS * SOUNDS, STRIP), F32),
            pltpu.SemaphoreType.DMA((len(arguments) - 1 + PIECES,)),
        ],
    )
    first = trade(first)
    point, top, share, hot, line_tops, grad = call(
        functools.partial(first_step_kernel, strips, owners),
        [
            strip_rows,
            narrow,
            ((2 * ROWS, LANES), F32),
            ((sectors * SLOTS, NBANDS), F32),
            ((strips * SLOTS, LANES), F32),
            strip_rows,
        ],
        first,
        info,
        column,
        twin,
        start_grad,
        limit,
        limit_rows,
        strip_match,
        top_matrix,
        decay,
        weight,
        blocks,
        mix,
        obs_slot,
    )
    placed_rows = (2 * strips + 2) * lines * WIN
    *tables, send, rank, lead, prepared = call(
        functools.partial(place_kernel, strips, owners),
        [
            ((placed_rows, 3 * owners * ROWS), BF16),
            ((owners * ROWS, NBANDS), F32),
            ((owners * ROWS, LANES), F32),
            ((SB_DEV, NBANDS), F32),
            ((owners * ROWS, 3 * PARTS * SLOTS), BF16),
            narrow,
            narrow,
            ((owners * ROWS, LANES), F32),
        ],
        first,
        bands,
        info,
        column,
    )
    third, values = call(
        functools.partial(second_step_kernel, strips, owners, betas[1]),
        [message, ((SOUNDS, LANES), F32)],
        first,
        info,
        column,
        twin,
        grad,
        limit,
        strip_match,
        top_matrix,
        decay,
        weight,
        hot,
        line_tops,
        lead,
        rank,
        send,
        prepared,
        point,
        top,
        blocks,
        mix,
        obs_slot,
        *with_sectors(share),
    )
    third = trade(third)
    coeffs, misfit = call(
        functools.partial(finish_kernel, strips, owners),
        [((lines * WIN, strips * STRIP), F32), ((SB_DEV, SOUNDS), F32)],
        first,
        third,
        values,
        observed,
        *tables,
        decay,
        weight,
    )
    return (coeffs.reshape(lines, WIN, strips * STRIP), misfit)


def solution(mesh):
    return jax.shard_map(
        body,
        mesh=mesh,
        in_specs=(
            P(("ens", "tile"), None),
            P("tile", None, None),
            P("tile"),
            P("tile"),
            P("tile"),
            P("tile"),
            P(),
            P(),
        ),
        out_specs=(P(("ens", "tile"), None, None), P(("ens", "tile"), None)),
        check_vma=False,
    )
```
